512 devices in a mesh: segment: 8 (over x, core), kv: 64 (over y, z).
Axes of the slice: x: 4, y: 8, z: 8, core: 2. Of those that a mesh axis runs over, the one named last changes fastest.
Arguments:
- queries: bfloat16 [8, 64, 8192], P('segment', 'kv'), may hold values from -24 to 24
- new_key: bfloat16 [8, 64, 1024], P('segment', 'kv'), may hold values from -6 to 6
- new_value: bfloat16 [8, 64, 1024], P('segment', 'kv'), may hold values from -6 to 6
- key_pool: bfloat16 [8, 2048, 16, 1024], P('segment', 'kv'), may hold values from -16 to 16
- value_pool: bfloat16 [8, 2048, 16, 1024], P('segment', 'kv'), may hold values from -6 to 6
- lengths: int32 [8, 64], P('segment'), may hold values from 1 to 512, as said below
- block_device: int32 [8, 64, 32], P('segment'), may hold values from 0 to 63, as said below
- block_slot: int32 [8, 64, 32], P('segment'), may hold values from 0 to 31, as said below
- residual: bfloat16 [8, 64, 8192], P('segment', None, 'kv'), may hold values from -6 to 6
- out_weight: bfloat16 [8, 8192, 8192], P('segment', None, 'kv'), may hold values from -0.0625 to 0.0625
Outputs:
- passed: bfloat16 [8, 64, 8192], P('segment', None, 'kv')
The draws below stay inside these ranges and needn't reach their ends.
Inputs may be any that keep to these rules, and one draw needn't show every extreme that they name: `lengths`: request 0 of every section has exactly 512 cached tokens. `block_device`: within a section, the live blocks of all requests (b * 16 < length) name distinct (instance, slot) pairs; entries past a request's length are arbitrary. `block_slot`: see block_device.
All inputs are finite; a program needn't handle non-finite values.
Results may differ from the reference program's by a relative error of at most 0.0035.
Values may be sent and summed in bfloat16 or wider, within the bound.
A program may use at most 64 MiB of HBM per device.

```python
import jax
import jax.numpy as jnp
from jax import lax

KV_HEADS = 8
HEAD_DIM = 128
D = 8192
GROUP = 8
BLK = 16
SLOTS = 32
MAXB = 32
R = 64
N_SEGMENT = 8
N_KV = 64


def block_layout(key):
    key = jax.random.fold_in(key, 101)
    segment_keys = jax.random.split(key, N_SEGMENT)
    slot_total = N_KV * SLOTS

    def one_segment(segment_key):
        first_key, second_key, third_key = jax.random.split(segment_key, 3)
        block_counts = jax.random.randint(first_key, (R,), 1, MAXB + 1, dtype=jnp.int32)
        block_counts = block_counts.at[0].set(MAXB)
        tail_tokens = jax.random.randint(second_key, (R,), 1, BLK + 1, dtype=jnp.int32)
        tail_tokens = tail_tokens.at[0].set(BLK)
        context = (block_counts - 1) * BLK + tail_tokens
        offsets = jnp.cumsum(block_counts) - block_counts
        shuffled = jax.random.permutation(third_key, slot_total).astype(jnp.int32)
        entry = (offsets[:, None] + jnp.arange(MAXB, dtype=jnp.int32)[None, :]) % slot_total
        global_slot = shuffled[entry]
        return (context, global_slot // SLOTS, global_slot % SLOTS)
    return jax.vmap(one_segment)(segment_keys)


def draw_lengths(key, part):
    return block_layout(key)[0].astype(jnp.int32)


def draw_block_device(key, part):
    return block_layout(key)[1].astype(jnp.int32)


def draw_block_slot(key, part):
    return block_layout(key)[2].astype(jnp.int32)


def draw_queries(key, part):
    key = jax.random.fold_in(key, 1)
    first_key = jax.random.fold_in(key, 0)
    values = jax.random.normal(first_key, (N_SEGMENT, R, KV_HEADS, GROUP, HEAD_DIM), jnp.float32)
    return jnp.clip(values, -24.0, 24.0).reshape(N_SEGMENT, R, D).astype(jnp.bfloat16)


def draw_key_pool(key, part):
    key = jax.random.fold_in(key, 2)
    first_key = jax.random.fold_in(key, 0)
    values = jax.random.normal(first_key, (N_SEGMENT, N_KV * SLOTS, BLK, KV_HEADS, HEAD_DIM), jnp.float32)
    return jnp.clip(values, -16.0, 16.0).reshape(N_SEGMENT, N_KV * SLOTS, BLK, KV_HEADS * HEAD_DIM).astype(jnp.bfloat16)


def block_scale(rng, dims, cuts, least, high):
    def one(dim, blocks):
        draws = jax.random.uniform(jax.random.fold_in(jax.random.fold_in(rng, 6), dim), (blocks,), jnp.float32, least / len(cuts), high / len(cuts))
        return jnp.repeat(jnp.exp(draws), dims[dim] // blocks).reshape((-1,) + (1,) * (len(dims) - dim - 1))

    level = one(*cuts[0])
    for cut in cuts[1:]:
        level = level * one(*cut)
    return level


def gaussian(stream_key, shape, width, limit, cuts=(), kind=jnp.bfloat16):
    values = width * jax.random.normal(stream_key, shape, jnp.float32)
    if cuts:
        values = values * block_scale(stream_key, shape, cuts, -0.22, 0.18)
    return jnp.clip(values, -limit, limit).astype(kind)


def setup_inputs(seed: int = 0) -> dict:
    streams_of = jax.random.split(jax.random.key(seed), 11)
    return {
        "queries": draw_queries(jax.random.fold_in(streams_of[10], 71), 0),
        "new_key": gaussian(streams_of[1], (N_SEGMENT, R, KV_HEADS * HEAD_DIM), 1.0, 6.0, ((0, 8), (1, 64))),
        "new_value": gaussian(streams_of[2], (N_SEGMENT, R, KV_HEADS * HEAD_DIM), 1.0, 6.0, ((0, 8), (1, 64))),
        "key_pool": draw_key_pool(jax.random.fold_in(streams_of[10], 71), 0),
        "value_pool": gaussian(streams_of[4], (N_SEGMENT, N_KV * SLOTS, BLK, KV_HEADS * HEAD_DIM), 1.0, 6.0, ((0, 8), (1, 64))),
        "lengths": draw_lengths(jax.random.fold_in(streams_of[10], 71), 0),
        "block_device": draw_block_device(jax.random.fold_in(streams_of[10], 71), 0),
        "block_slot": draw_block_slot(jax.random.fold_in(streams_of[10], 71), 0),
        "residual": gaussian(streams_of[8], (N_SEGMENT, R, D), 1.0, 6.0, ((0, 8), (2, 64))),
        "out_weight": gaussian(streams_of[9], (N_SEGMENT, D, D), D ** -0.5, 0.0625, ((0, 8), (2, 64))),
    }


def attend_request(request_query, own_key, own_value, key_segment, value_segment, length, devices, slot_ids):
    positions_all = MAXB * BLK
    global_ids = devices * SLOTS + slot_ids
    key_rows = key_segment[global_ids].reshape(positions_all, KV_HEADS, HEAD_DIM).astype(jnp.float32)
    value_rows = value_segment[global_ids].reshape(positions_all, KV_HEADS, HEAD_DIM).astype(jnp.float32)
    query_heads = request_query.astype(jnp.float32).reshape(KV_HEADS, GROUP, HEAD_DIM)
    score_scale = HEAD_DIM ** -0.5
    scores = jnp.einsum("kgd,tkd->kgt", query_heads, key_rows, precision=lax.Precision.HIGHEST) * score_scale
    positions = jnp.arange(positions_all, dtype=jnp.int32)
    usable = positions < length
    token_device = jnp.repeat(devices, BLK)
    member = (token_device[:, None] == jnp.arange(N_KV, dtype=jnp.int32)[None, :]) & usable[:, None]
    scores = jnp.where(usable[None, None, :], scores, -1e30)
    device_max = jnp.max(jnp.where(member[None, None], scores[..., None], -1e30), axis=2)
    token_max = jnp.take(device_max, token_device, axis=2)
    weights = jnp.where(usable[None, None, :], jnp.exp(scores - token_max), 0.0).astype(jnp.bfloat16)
    weights = lax.optimization_barrier(weights).astype(jnp.float32)
    member_float = member.astype(jnp.float32)
    device_acc = jnp.einsum("kgt,tn,tkd->kgnd", weights, member_float, value_rows, precision=lax.Precision.HIGHEST)
    device_sum = jnp.einsum("kgt,tn->kgn", weights, member_float, precision=lax.Precision.HIGHEST)
    own_score = jnp.sum(query_heads * own_key.astype(jnp.float32).reshape(KV_HEADS, 1, HEAD_DIM), axis=-1) * score_scale
    overall = jnp.maximum(jnp.max(device_max, axis=2), own_score)
    device_weight = jnp.exp(device_max - overall[..., None])
    own_weight = jnp.exp(own_score - overall)
    numerator = jnp.sum(device_weight[..., None] * device_acc, axis=2)
    numerator = numerator + own_weight[..., None] * own_value.astype(jnp.float32).reshape(KV_HEADS, 1, HEAD_DIM)
    denominator = jnp.sum(device_weight * device_sum, axis=2) + own_weight
    return (numerator / denominator[..., None]).reshape(D).astype(jnp.bfloat16)


def section_layer(query_rows, key_rows, value_rows, key_segment, value_segment, length_rows, device_rows, slot_rows, residual_rows, weight):
    def one_request(items):
        return attend_request(items[0], items[1], items[2], key_segment, value_segment, items[3], items[4], items[5])

    attention = lax.map(one_request, (query_rows, key_rows, value_rows, length_rows, device_rows, slot_rows))
    mixed = jnp.dot(attention, weight, preferred_element_type=jnp.float32)
    return (residual_rows.astype(jnp.float32) + mixed).astype(jnp.bfloat16)


def reference(queries, new_key, new_value, key_pool, value_pool, lengths, block_device, block_slot, residual, out_weight):
    sections = []
    for segment_index in range(N_SEGMENT):
        sections.append(section_layer(queries[segment_index], new_key[segment_index], new_value[segment_index], key_pool[segment_index], value_pool[segment_index], lengths[segment_index], block_device[segment_index], block_slot[segment_index], residual[segment_index], out_weight[segment_index]))
    layer_out = jnp.stack(sections, axis=0)
    return jnp.roll(layer_out, 1, axis=0)
```

```python
import functools

import jax
import jax.numpy as jnp
from jax import lax
from jax.experimental import pallas as pl
from jax.experimental.pallas import tpu as pltpu
from jax.sharding import PartitionSpec as P

KV_HEADS = 8
HEAD_DIM = 128
HEADS = 64
HALF = HEADS // 2
PAIR = 16
BLK = 16
MESH = pl.DeviceIdType.MESH
EMPTY = -1e30
FLOOR = -1e29
SCALE = HEAD_DIM ** (-0.5)

ASK_FIRST, ASK_SECOND, PART, PART_STAT, MERGED, MERGED_STAT, TELL_FIRST, TELL_SECOND = range(8)


def offsets(n):
    near = []
    for step in range(1, n // 2 + 1):
        near.append(step)
        if step != n - step:
            near.append(n - step)
    return near


def kernel(
    n_seg,
    n,
    q_ref,
    nk_ref,
    nv_ref,
    len_ref,
    dev_ref,
    slot_ref,
    res_ref,
    k_hbm,
    v_hbm,
    w_hbm,
    out_ref,
    k_buf,
    v_buf,
    w_buf,
    kt_buf,
    bias_buf,
    q_all,
    part,
    part_stat,
    got,
    got_stat,
    merged,
    merged_stat,
    last,
    last_stat,
    attn,
    told,
    rows32,
    told_all,
    turn,
    line,
    landed,
    send_sem,
    recv_sem,
    load_sem,
    pass_sem,
):
    f32, bf16 = jnp.float32, jnp.bfloat16
    seg = lax.axis_index("segment")
    me = lax.axis_index("kv")
    y, z = lax.div(me, n), lax.rem(me, n)
    first, second = (z, y), (y, z)
    slots = k_buf.shape[0]
    tokens = slots * BLK
    rows = n * PAIR

    def at_first(half, i):
        return y * n + i if half == 0 else i * n + z

    def at_second(half, i):
        return i * n + z if half == 0 else y * n + i

    def peer(base, off):
        return lax.rem(base + off, n)

    def copy(stage, half, src, dst, there, here, device):
        return pltpu.make_async_remote_copy(
            src_ref=src,
            dst_ref=dst,
            send_sem=send_sem.at[stage, half, there],
            recv_sem=recv_sem.at[stage, half, here],
            device_id={"kv": device},
            device_id_type=MESH,
        )

    following, before = lax.rem(seg + 1, n_seg), lax.rem(seg + n_seg - 1, n_seg)

    barrier = pltpu.get_barrier_semaphore()
    for off in offsets(n):
        for half in range(2):
            pl.semaphore_signal(
                barrier,
                inc=1,
                device_id={"kv": at_first(half, peer(first[half], off))},
                device_id_type=MESH,
            )
    for other in (following, before):
        pl.semaphore_signal(barrier, inc=1, device_id={"segment": other}, device_id_type=MESH)

    load_k = pltpu.make_async_copy(k_hbm, k_buf, load_sem.at[0])
    load_v = pltpu.make_async_copy(v_hbm, v_buf, load_sem.at[1])
    load_w = pltpu.make_async_copy(w_hbm, w_buf, load_sem.at[2])
    load_k.start()
    load_v.start()
    load_w.start()

    for half in range(2):
        q_all[half, second[half], first[half]] = q_ref[half]

    pl.semaphore_wait(barrier, 2 * (n - 1) + 2)

    def ask_first(half, i, here):
        return copy(
            ASK_FIRST, half, q_ref.at[half], q_all.at[half, second[half], here], i, here, at_first(half, i)
        )

    def ask_second(half, i, here):
        return copy(
            ASK_SECOND, half, q_all.at[half, second[half]], q_all.at[half, here], i, here, at_second(half, i)
        )

    for off in offsets(n):
        for half in range(2):
            ask_first(half, peer(first[half], off), first[half]).start()

    requests = n * n
    eye = lax.broadcasted_iota(jnp.int32, (requests, requests), 0) == lax.broadcasted_iota(
        jnp.int32, (requests, requests), 1
    )
    context = jnp.sum(
        jnp.where(eye, jnp.broadcast_to(len_ref[...].astype(f32), (requests, requests)), 0.0),
        axis=1,
        keepdims=True,
    )
    blocks = dev_ref.shape[1]
    holder = jnp.where(dev_ref[...] == me, slot_ref[...], -1)
    numbers = lax.broadcasted_iota(jnp.int32, (requests, blocks), 1).astype(f32)
    live = jnp.clip(context - numbers * BLK, 0.0, float(BLK))
    slot_of = lax.broadcasted_iota(jnp.int32, (requests, slots), 1)
    count = jnp.zeros((requests, slots), f32)
    for b in range(blocks):
        count = count + jnp.where(slot_of == holder[:, b : b + 1], live[:, b : b + 1], 0.0)
    spread = (
        lax.div(lax.broadcasted_iota(jnp.int32, (slots, tokens), 1), BLK)
        == lax.broadcasted_iota(jnp.int32, (slots, tokens), 0)
    ).astype(bf16)
    limit = jnp.dot(count.astype(bf16), spread, preferred_element_type=f32)
    place = lax.rem(lax.broadcasted_iota(jnp.int32, (requests, tokens), 1), BLK).astype(f32)
    mask = jnp.where(place < limit, 0.0, EMPTY)
    wide = bias_buf.shape[2]
    for c in range(tokens // wide):
        bias_buf[c] = mask[:, c * wide : (c + 1) * wide]

    load_k.wait()
    for pair in range(4):
        kt_buf[pair] = k_buf[:, :, pair * 256 : (pair + 1) * 256].reshape(tokens, 256).T

    for half in range(2):
        for off in offsets(n):
            i = peer(first[half], off)
            ask_first(half, i, i).wait_recv()
        for off in offsets(n):
            ask_second(half, peer(second[half], off), second[half]).start()
    load_v.wait()

    row_of = lax.broadcasted_iota(jnp.int32, (rows, 128), 0)
    upper = lax.rem(row_of, PAIR) < PAIR // 2
    keep_upper = upper.astype(f32).astype(bf16)
    keep_lower = (1.0 - upper.astype(f32)).astype(bf16)
    lane = lax.broadcasted_iota(jnp.int32, (PAIR, 128), 1)

    def both_sides(x):
        return jnp.concatenate([x * keep_upper, x * keep_lower], axis=1)

    def attend(half, b):
        which = pl.ds(b * n, n) if half == 0 else pl.ds(b, n, stride=n)
        bias = jnp.concatenate([bias_buf[c, which, :] for c in range(tokens // wide)], axis=1)
        bias = jnp.broadcast_to(bias[:, None, :], (n, PAIR, tokens)).reshape(rows, tokens)
        stat = jnp.full((PAIR, 128), EMPTY, f32)
        for p in range(2):
            pair = half * 2 + p
            x = q_all[half, b, :, p * PAIR : (p + 1) * PAIR, :].reshape(rows, 128)
            score = jnp.dot(both_sides(x), kt_buf[pair], preferred_element_type=f32) + bias
            top = jnp.maximum(jnp.max(score, axis=1, keepdims=True), FLOOR)
            prob = jnp.exp((score - top) * SCALE).astype(bf16)
            total = jnp.sum(prob.astype(f32), axis=1, keepdims=True)
            value = v_buf[:, :, pair * 256 : (pair + 1) * 256].reshape(tokens, 256)
            acc = jnp.dot(prob, value, preferred_element_type=f32)
            acc = jnp.where(upper, acc[:, :128], acc[:, 128:])
            acc = acc / jnp.maximum(total, 0.5)
            part[half, b, :, p * PAIR : (p + 1) * PAIR, :] = acc.astype(bf16).reshape(n, PAIR, 128)
            lse = jnp.where(total > 0.0, top * SCALE + jnp.log(jnp.maximum(total, 0.5)), EMPTY)
            lse = lse.reshape(n, PAIR, 1)
            for r in range(n):
                stat = jnp.where(lane == p * n + r, lse[r], stat)
        part_stat[half, b] = stat

    def send_part(half, i, here):
        return copy(PART, half, part.at[half, i], got.at[half, here], i, here, at_second(half, i))

    def send_part_stat(half, i, here):
        return copy(
            PART_STAT, half, part_stat.at[half, i], got_stat.at[half, here], i, here, at_second(half, i)
        )

    for half in range(2):
        attend(half, second[half])
        got[half, second[half]] = part[half, second[half]]
        got_stat[half, second[half]] = part_stat[half, second[half]]

    def one_block(j, carry):
        step = lax.div(j + 1, 2)
        off = lax.rem(n + step * (2 * lax.rem(j, 2) - 1), n)
        for half in range(2):
            i = peer(second[half], off)
            ask_second(half, i, i).wait_recv()
        for half in range(2):
            i = peer(second[half], off)
            attend(half, i)
        for half in range(2):
            i = peer(second[half], off)
            send_part(half, i, second[half]).start()
            send_part_stat(half, i, second[half]).start()
        return carry

    lax.fori_loop(1, n, one_block, 0)

    def send_merged(half, i, here):
        return copy(MERGED, half, merged.at[half, i], last.at[half, here], i, here, at_first(half, i))

    def send_merged_stat(half, i, here):
        return copy(
            MERGED_STAT, half, merged_stat.at[half], last_stat.at[half, here], i, here, at_first(half, i)
        )

    for half in range(2):
        for off in offsets(n):
            i = peer(second[half], off)
            send_part(half, i, i).wait_recv()
            send_part_stat(half, i, i).wait_recv()
        stat = got_stat[half]
        top = jnp.max(stat, axis=0)
        weight = jnp.exp(stat - top[None])
        total = jnp.sum(weight, axis=0)
        weight = weight / total[None]
        merged_stat[half] = top + jnp.log(total)
        for r in range(n):
            for p in range(2):
                c = p * n + r
                piece = got[half, :, r, p * PAIR : (p + 1) * PAIR, :].astype(f32)
                merged[half, r, p * PAIR : (p + 1) * PAIR, :] = jnp.sum(
                    piece * weight[:, :, c : c + 1], axis=0
                ).astype(bf16)
        for off in offsets(n):
            i = peer(first[half], off)
            send_merged_stat(half, i, first[half]).start()
            send_merged(half, i, first[half]).start()
        last[half, first[half]] = merged[half, first[half]]
        last_stat[half, first[half]] = merged_stat[half]

    def tell_first(half, i, here):
        return copy(TELL_FIRST, half, attn.at[half], told.at[half, here], i, here, at_first(half, i))

    def tell_second(half, i, here):
        return copy(
            TELL_SECOND,
            half,
            told_all.at[half, second[half]],
            told_all.at[half, here],
            i,
            here,
            at_second(half, i),
        )

    new_keys = nk_ref[...].astype(f32)
    new_values = nv_ref[...].astype(f32)
    for half in range(2):
        kv_half = slice(half * 4, half * 4 + 4)
        query = q_ref[half].astype(f32).reshape(4, 8, 128)
        own = jnp.sum(query * new_keys[kv_half][:, None, :], axis=2, keepdims=True) * SCALE
        own = own.reshape(HALF, 1)
        own_value = jnp.broadcast_to(new_values[kv_half][:, None, :], (4, 8, 128)).reshape(HALF, 128)
        for off in offsets(n):
            i = peer(first[half], off)
            send_merged_stat(half, i, i).wait_recv()
            send_merged(half, i, i).wait_recv()
        lses = []
        for i in range(n):
            stat = last_stat[half, i]
            lses.append(
                jnp.concatenate(
                    [
                        jnp.sum(
                            jnp.where(lane == p * n + first[half], stat, 0.0), axis=1, keepdims=True
                        )
                        for p in range(2)
                    ],
                    axis=0,
                )
            )
        top = own
        for lse in lses:
            top = jnp.maximum(top, lse)
        weight = jnp.exp(own - top)
        total = weight
        acc = weight * own_value
        for i in range(n):
            weight = jnp.exp(lses[i] - top)
            total = total + weight
            acc = acc + weight * last[half, i].astype(f32)
        attn[half] = (acc / total).astype(bf16)
        for off in offsets(n):
            tell_first(half, peer(first[half], off), first[half]).start()
        told[half, first[half]] = attn[half]

    for half in range(2):
        for off in offsets(n):
            i = peer(first[half], off)
            tell_first(half, i, i).wait_recv()
        rows32[half] = told[half].astype(f32).reshape(n * HALF, 128)
        for h in range(HALF // 2):
            tile = [rows32[half, pl.ds(2 * h + s, n, stride=HALF), :] for s in range(2)]
            told_all[half, second[half], h] = jnp.concatenate(tile, axis=0).astype(bf16)
        for off in offsets(n):
            tell_second(half, peer(second[half], off), second[half]).start()

    load_w.wait()
    out_rows = 2 * n
    first_rows = lax.rem(lax.broadcasted_iota(jnp.int32, (n * out_rows, 128), 0), out_rows) < n
    keep_first = first_rows.astype(f32).astype(bf16)
    keep_rest = (1.0 - first_rows.astype(f32)).astype(bf16)
    depth = HALF * HEAD_DIM
    mixed = []
    for half in range(2):
        for off in offsets(n):
            i = peer(second[half], off)
            tell_second(half, i, i).wait_recv()
        pieces = []
        for h in range(HALF // 2):
            x = told_all[half, :, h].reshape(n * out_rows, 128)
            pieces.append(x * keep_first)
            pieces.append(x * keep_rest)
        acc = jnp.dot(
            jnp.concatenate(pieces, axis=1),
            w_buf[half * depth : (half + 1) * depth, :],
            preferred_element_type=f32,
        )
        mixed.append(jnp.sum(acc.reshape(n, 2, n, 128), axis=1))
    turn[...] = mixed[1].reshape(requests, 128)
    other = jnp.concatenate([turn[pl.ds(i, n, stride=n), :] for i in range(n)], axis=0)
    layer = res_ref[...].astype(f32) + (mixed[0].reshape(requests, 128) + other)
    line[...] = layer.astype(bf16)

    hand = pltpu.make_async_remote_copy(
        src_ref=line,
        dst_ref=landed,
        send_sem=pass_sem.at[0],
        recv_sem=pass_sem.at[1],
        device_id={"segment": following},
        device_id_type=MESH,
    )
    hand.start()

    for half in range(2):
        for off in offsets(n):
            i = peer(first[half], off)
            ask_first(half, i, i).wait_send()
            send_merged(half, i, i).wait_send()
            send_merged_stat(half, i, i).wait_send()
            tell_first(half, i, i).wait_send()
            i = peer(second[half], off)
            ask_second(half, i, i).wait_send()
            send_part(half, i, i).wait_send()
            send_part_stat(half, i, i).wait_send()
            tell_second(half, i, i).wait_send()
    hand.wait()
    out_ref[...] = landed[...]


def local(
    n_seg,
    n,
    queries,
    new_key,
    new_value,
    key_pool,
    value_pool,
    lengths,
    block_device,
    block_slot,
    residual,
    out_weight,
):
    f32, bf16 = jnp.float32, jnp.bfloat16
    slots = key_pool.shape[1]
    tokens = slots * BLK
    requests = n * n
    whole = pl.BlockSpec(memory_space=pltpu.VMEM)
    outside = pl.BlockSpec(memory_space=pl.ANY)
    out = pl.pallas_call(
        functools.partial(kernel, n_seg, n),
        out_shape=jax.ShapeDtypeStruct((requests, 128), bf16),
        in_specs=[whole] * 7 + [outside] * 3,
        out_specs=whole,
        scratch_shapes=[
            pltpu.VMEM((slots, BLK, KV_HEADS * HEAD_DIM), bf16),
            pltpu.VMEM((slots, BLK, KV_HEADS * HEAD_DIM), bf16),
            pltpu.VMEM((HEADS * HEAD_DIM, 128), bf16),
            pltpu.VMEM((4, 256, tokens), bf16),
            pltpu.VMEM((max(tokens // 128, 1), requests, min(tokens, 128)), f32),
            pltpu.VMEM((2, n, n, HALF, 128), bf16),
            pltpu.VMEM((2, n, n, HALF, 128), bf16),
            pltpu.VMEM((2, n, PAIR, 128), f32),
            pltpu.VMEM((2, n, n, HALF, 128), bf16),
            pltpu.VMEM((2, n, PAIR, 128), f32),
            pltpu.VMEM((2, n, HALF, 128), bf16),
            pltpu.VMEM((2, PAIR, 128), f32),
            pltpu.VMEM((2, n, HALF, 128), bf16),
            pltpu.VMEM((2, n, PAIR, 128), f32),
            pltpu.VMEM((2, HALF, 128), bf16),
            pltpu.VMEM((2, n, HALF, 128), bf16),
            pltpu.VMEM((2, n * HALF, 128), f32),
            pltpu.VMEM((2, n, HALF // 2, 2 * n, 128), bf16),
            pltpu.VMEM((requests, 128), f32),
            pltpu.VMEM((requests, 128), bf16),
            pltpu.VMEM((requests, 128), bf16),
            pltpu.SemaphoreType.DMA((8, 2, n)),
            pltpu.SemaphoreType.DMA((8, 2, n)),
            pltpu.SemaphoreType.DMA((3,)),
            pltpu.SemaphoreType.DMA((2,)),
        ],
        compiler_params=pltpu.CompilerParams(
            collective_id=0, has_side_effects=True, vmem_limit_bytes=40 * 1024 * 1024
        ),
        name="decode_layer",
    )(
        queries[0].reshape(2, HALF, 128),
        new_key[0].reshape(KV_HEADS, HEAD_DIM),
        new_value[0].reshape(KV_HEADS, HEAD_DIM),
        lengths,
        block_device[0],
        block_slot[0],
        residual[0],
        key_pool[0],
        value_pool[0],
        out_weight[0],
    )
    return out[None]


def solution(mesh):
    placed = (
        P("segment", "kv", None),
        P("segment", "kv", None),
        P("segment", "kv", None),
        P("segment", "kv", None, None),
        P("segment", "kv", None, None),
        P("segment", None),
        P("segment", None, None),
        P("segment", None, None),
        P("segment", None, "kv"),
        P("segment", None, "kv"),
    )
    n_seg = mesh.shape["segment"]
    n = next(i for i in range(1, 64) if i * i == mesh.shape["kv"])
    return jax.shard_map(
        functools.partial(local, n_seg, n),
        mesh=mesh,
        in_specs=placed,
        out_specs=P("segment", None, "kv"),
        check_vma=False,
    )
```

```python
import functools

import jax
import jax.numpy as jnp
from jax import lax
from jax.experimental import pallas as pl
from jax.experimental.pallas import tpu as pltpu
from jax.sharding import PartitionSpec as P

KV_HEADS = 8
HEAD_DIM = 128
HEADS = 64
HALF = HEADS // 2
PAIR = 16
BLK = 16
MESH = pl.DeviceIdType.MESH
EMPTY = -1e30
FLOOR = -1e29
SCALE = HEAD_DIM ** (-0.5)

ASK_FIRST, PART, PART_STAT, MERGED, MERGED_STAT, TELL_FIRST = range(6)
ASK_SECOND, TELL_SECOND = range(2)


def offsets(n):
    near = []
    for step in range(1, n // 2 + 1):
        near.append(step)
        if step != n - step:
            near.append(n - step)
    return near


def heads_in_row(raw, rows):
    flat = raw[0].astype(jnp.float32)
    for h in range(rows.shape[0]):
        rows[h : h + 1, :] = flat[:, h * HEAD_DIM : (h + 1) * HEAD_DIM]


def kernel(
    n_seg,
    n,
    q_hbm,
    nk_hbm,
    nv_hbm,
    len_hbm,
    dev_hbm,
    slot_hbm,
    res_hbm,
    k_hbm,
    v_hbm,
    w_hbm,
    out_ref,
    q_raw,
    nk_raw,
    nv_raw,
    len_buf,
    dev_buf,
    slot_buf,
    res_buf,
    rows64,
    q_ref,
    k_buf,
    v_buf,
    w_buf,
    kt_buf,
    bias_buf,
    q_all,
    part,
    part_stat,
    got,
    got_stat,
    merged,
    merged_stat,
    last,
    last_stat,
    attn,
    told,
    rows32,
    told_all,
    turn,
    line,
    landed,
    send_sem,
    recv_sem,
    ring_send,
    ring_recv,
    load_sem,
    pass_sem,
):
    f32, bf16 = jnp.float32, jnp.bfloat16
    seg = lax.axis_index("segment")
    me = lax.axis_index("kv")
    y, z = lax.div(me, n), lax.rem(me, n)
    first, second = (z, y), (y, z)
    slots = k_buf.shape[0]
    tokens = slots * BLK
    rows = n * PAIR

    def at_first(half, i):
        return y * n + i if half == 0 else i * n + z

    def at_second(half, i):
        return i * n + z if half == 0 else y * n + i

    def peer(base, off):
        return lax.rem(base + off, n)

    def copy(stage, half, src, dst, there, here, device):
        return pltpu.make_async_remote_copy(
            src_ref=src,
            dst_ref=dst,
            send_sem=send_sem.at[stage, half, there],
            recv_sem=recv_sem.at[stage, half, here],
            device_id={"kv": device},
            device_id_type=MESH,
        )

    following, before = lax.rem(seg + 1, n_seg), lax.rem(seg + n_seg - 1, n_seg)

    barrier = pltpu.get_barrier_semaphore()
    for off in offsets(n):
        for half in range(2):
            pl.semaphore_signal(
                barrier,
                inc=1,
                device_id={"kv": at_first(half, peer(first[half], off))},
                device_id_type=MESH,
            )
    for other in (following, before):
        pl.semaphore_signal(barrier, inc=1, device_id={"segment": other}, device_id_type=MESH)

    loads = [
        pltpu.make_async_copy(src, dst, load_sem.at[i])
        for i, (src, dst) in enumerate(
            (
                (q_hbm, q_raw),
                (len_hbm, len_buf),
                (dev_hbm, dev_buf),
                (slot_hbm, slot_buf),
                (k_hbm, k_buf),
                (v_hbm, v_buf),
                (nk_hbm, nk_raw),
                (nv_hbm, nv_raw),
                (res_hbm, res_buf),
                (w_hbm, w_buf),
            )
        )
    ]
    for load in loads:
        load.start()

    loads[0].wait()
    heads_in_row(q_raw, rows64)
    for half in range(2):
        for p in range(2):
            start = half * HALF + p * PAIR
            q_ref[half, p] = rows64[start : start + PAIR, :].astype(bf16)
            q_all[half, second[half], p, first[half]] = q_ref[half, p]

    pl.semaphore_wait(barrier, 2 * (n - 1) + 2)

    steps = n // 2

    def ask_first(half, i, here):
        return copy(
            ASK_FIRST,
            half,
            q_ref.at[half],
            q_all.at[half, second[half], :, here],
            i,
            here,
            at_first(half, i),
        )

    def origin(half, way, t):
        return lax.rem(second[half] + (n - t if way == 0 else t), n)

    def hop(ring, half, way, piece, t):
        index = ((half * 2 + way) * 2 + piece) * steps + t - 1
        block = origin(half, way, t - 1)
        if ring == ASK_SECOND:
            ref = q_all.at[half, block, piece]
        else:
            ref = told_all.at[half, block, pl.ds(piece * (HALF // 4), HALF // 4)]
        return pltpu.make_async_remote_copy(
            src_ref=ref,
            dst_ref=ref,
            send_sem=ring_send.at[ring, index],
            recv_sem=ring_recv.at[ring, index],
            device_id={"kv": at_second(half, peer(second[half], 1 if way == 0 else n - 1))},
            device_id_type=MESH,
        )

    def arrival(ring, half, way, piece, t):
        index = ((half * 2 + way) * 2 + piece) * steps + t - 1
        block = origin(half, way, t)
        if ring == ASK_SECOND:
            ref = q_all.at[half, block, piece]
        else:
            ref = told_all.at[half, block, pl.ds(piece * (HALF // 4), HALF // 4)]
        return pltpu.make_async_remote_copy(
            src_ref=ref,
            dst_ref=ref,
            send_sem=ring_send.at[ring, index],
            recv_sem=ring_recv.at[ring, index],
            device_id={"kv": at_second(half, peer(second[half], 1 if way == 0 else n - 1))},
            device_id_type=MESH,
        )

    def relay(ring, t):
        for piece in range(2):
            for half in range(2):
                for way in range(2):
                    arrival(ring, half, way, piece, t).wait_recv()
                    if piece == way:
                        hop(ring, half, way, piece, t + 1).start()
                    else:

                        @pl.when(t + 1 < steps)
                        def _():
                            hop(ring, half, way, piece, t + 1).start()

    def begin(ring, half):
        for piece in range(2):
            for way in range(2):
                if steps > 1 or piece == way:
                    hop(ring, half, way, piece, 1).start()

    def finish(ring, half):
        for way in range(2):
            arrival(ring, half, way, way, steps).wait_recv()

    for off in offsets(n):
        for half in range(2):
            ask_first(half, peer(first[half], off), first[half]).start()

    requests = n * n
    for load in loads[1:4]:
        load.wait()
    blocks = dev_buf.shape[1]
    holder = jnp.where(dev_buf[0] == me, slot_buf[0], -1)
    numbers = lax.broadcasted_iota(jnp.int32, (blocks, requests), 0)
    live = jnp.clip(len_buf[...] - numbers * BLK, 0, BLK).astype(f32)
    slot_of = lax.broadcasted_iota(jnp.int32, (slots, requests), 0)
    count = jnp.zeros((slots, requests), f32)
    for b in range(blocks):
        count = count + jnp.where(slot_of == holder[b : b + 1, :], live[b : b + 1, :], 0.0)
    spread = (
        lax.div(lax.broadcasted_iota(jnp.int32, (slots, tokens), 1), BLK)
        == lax.broadcasted_iota(jnp.int32, (slots, tokens), 0)
    ).astype(bf16)
    limit = lax.dot_general(
        count.astype(bf16), spread, (((0,), (0,)), ((), ())), preferred_element_type=f32
    )
    place = lax.rem(lax.broadcasted_iota(jnp.int32, (requests, tokens), 1), BLK).astype(f32)
    mask = jnp.where(place < limit, 0.0, EMPTY)
    wide = bias_buf.shape[2]
    for c in range(tokens // wide):
        bias_buf[c] = mask[:, c * wide : (c + 1) * wide]

    loads[4].wait()
    for pair in range(4):
        kt_buf[pair] = k_buf[:, :, pair * 256 : (pair + 1) * 256].reshape(tokens, 256).T

    for half in range(2):
        for off in offsets(n):
            i = peer(first[half], off)
            ask_first(half, i, i).wait_recv()
        begin(ASK_SECOND, half)
    loads[5].wait()

    def tiles(count):
        inside = lax.rem(lax.broadcasted_iota(jnp.int32, (count * PAIR, 128), 0), PAIR)
        return inside < PAIR // 2

    lane = lax.broadcasted_iota(jnp.int32, (PAIR // 2, 128), 1)

    def attend(half, those):
        count = len(those) * n
        upper = tiles(count)
        keep_upper = upper.astype(f32).astype(bf16)
        keep_lower = (1.0 - upper.astype(f32)).astype(bf16)
        bias = []
        for b in those:
            which = pl.ds(b * n, n) if half == 0 else pl.ds(b, n, stride=n)
            bias.append(
                jnp.concatenate([bias_buf[c, which, :] for c in range(tokens // wide)], axis=1)
            )
        bias = jnp.concatenate(bias, axis=0)
        bias = jnp.broadcast_to(bias[:, None, :], (count, PAIR, tokens)).reshape(
            count * PAIR, tokens
        )
        stats = [jnp.full((PAIR // 2, 128), EMPTY, f32) for _ in those]
        for p in range(2):
            pair = half * 2 + p
            x = jnp.concatenate([q_all[half, b, p].reshape(rows, 128) for b in those], axis=0)
            x = jnp.concatenate([x * keep_upper, x * keep_lower], axis=1)
            score = jnp.dot(x, kt_buf[pair], preferred_element_type=f32) + bias
            top = jnp.maximum(jnp.max(score, axis=1, keepdims=True), FLOOR)
            prob = jnp.exp((score - top) * SCALE).astype(bf16)
            total = jnp.sum(prob.astype(f32), axis=1, keepdims=True)
            value = v_buf[:, :, pair * 256 : (pair + 1) * 256].reshape(tokens, 256)
            acc = jnp.dot(prob, value, preferred_element_type=f32)
            acc = jnp.where(upper, acc[:, :128], acc[:, 128:])
            acc = (acc / jnp.maximum(total, 0.5)).astype(bf16).reshape(count, PAIR, 128)
            lse = jnp.where(total > 0.0, top * SCALE + jnp.log(jnp.maximum(total, 0.5)), EMPTY)
            lse = lse.reshape(count, 2, PAIR // 2, 1)
            for k, b in enumerate(those):
                part[half, b, :, p * PAIR : (p + 1) * PAIR, :] = acc[k * n : (k + 1) * n]
                for r in range(n):
                    for side in range(2):
                        stats[k] = jnp.where(
                            lane == (side * 2 + p) * n + r, lse[k * n + r, side], stats[k]
                        )
        for k, b in enumerate(those):
            part_stat[half, b] = stats[k]

    def send_part(half, i, here):
        return copy(PART, half, part.at[half, i], got.at[half, here], i, here, at_second(half, i))

    def send_part_stat(half, i, here):
        return copy(
            PART_STAT, half, part_stat.at[half, i], got_stat.at[half, here], i, here, at_second(half, i)
        )

    def send_parts(half, b):
        send_part(half, b, second[half]).start()
        send_part_stat(half, b, second[half]).start()

    for half in range(2):
        attend(half, [second[half]])
        got[half, second[half]] = part[half, second[half]]
        got_stat[half, second[half]] = part_stat[half, second[half]]

    def one_step(t, carry):
        relay(ASK_SECOND, t)
        for half in range(2):
            those = [origin(half, way, t) for way in range(2)]
            attend(half, those)
            for b in those:
                send_parts(half, b)
        return carry

    lax.fori_loop(1, steps, one_step, 0)
    for half in range(2):
        finish(ASK_SECOND, half)
        those = [origin(half, 0, steps)]
        attend(half, those)
        send_parts(half, those[0])

    def send_merged(half, i, here):
        return copy(MERGED, half, merged.at[half, i], last.at[half, here], i, here, at_first(half, i))

    def send_merged_stat(half, i, here):
        return copy(
            MERGED_STAT, half, merged_stat.at[half], last_stat.at[half, here], i, here, at_first(half, i)
        )

    for half in range(2):
        for off in offsets(n):
            i = peer(second[half], off)
            send_part(half, i, i).wait_recv()
            send_part_stat(half, i, i).wait_recv()
        stat = got_stat[half]
        top = jnp.max(stat, axis=0)
        weight = jnp.exp(stat - top[None])
        total = jnp.sum(weight, axis=0)
        weight = weight / total[None]
        merged_stat[half] = top + jnp.log(total)
        for r in range(n):
            for p in range(2):
                scale = jnp.concatenate(
                    [
                        weight[:, :, (side * 2 + p) * n + r : (side * 2 + p) * n + r + 1]
                        for side in range(2)
                    ],
                    axis=1,
                )
                piece = got[half, :, r, p * PAIR : (p + 1) * PAIR, :].astype(f32)
                merged[half, r, p * PAIR : (p + 1) * PAIR, :] = jnp.sum(
                    piece * scale, axis=0
                ).astype(bf16)
        for off in offsets(n):
            i = peer(first[half], off)
            send_merged_stat(half, i, first[half]).start()
            send_merged(half, i, first[half]).start()
        last[half, first[half]] = merged[half, first[half]]
        last_stat[half, first[half]] = merged_stat[half]

    def tell_first(half, i, here):
        return copy(TELL_FIRST, half, attn.at[half], told.at[half, here], i, here, at_first(half, i))

    for load in loads[6:9]:
        load.wait()
    heads_in_row(nk_raw, rows64.at[pl.ds(0, KV_HEADS)])
    new_keys = rows64[:KV_HEADS, :]
    heads_in_row(nv_raw, rows64.at[pl.ds(KV_HEADS, KV_HEADS)])
    new_values = rows64[KV_HEADS : 2 * KV_HEADS, :]
    for half in range(2):
        kv_half = slice(half * 4, half * 4 + 4)
        query = q_ref[half].astype(f32).reshape(4, 8, 128)
        own = jnp.sum(query * new_keys[kv_half][:, None, :], axis=2, keepdims=True) * SCALE
        own = own.reshape(HALF, 1)
        own_value = jnp.broadcast_to(new_values[kv_half][:, None, :], (4, 8, 128)).reshape(HALF, 128)
        for off in offsets(n):
            i = peer(first[half], off)
            send_merged_stat(half, i, i).wait_recv()
            send_merged(half, i, i).wait_recv()
        lses = []
        for i in range(n):
            stat = last_stat[half, i]
            lses.append(
                jnp.concatenate(
                    [
                        jnp.sum(
                            jnp.where(lane == (side * 2 + p) * n + first[half], stat, 0.0),
                            axis=1,
                            keepdims=True,
                        )
                        for p in range(2)
                        for side in range(2)
                    ],
                    axis=0,
                )
            )
        top = own
        for lse in lses:
            top = jnp.maximum(top, lse)
        weight = jnp.exp(own - top)
        total = weight
        acc = weight * own_value
        for i in range(n):
            weight = jnp.exp(lses[i] - top)
            total = total + weight
            acc = acc + weight * last[half, i].astype(f32)
        attn[half] = (acc / total).astype(bf16)
        for off in offsets(n):
            tell_first(half, peer(first[half], off), first[half]).start()
        told[half, first[half]] = attn[half]

    for half in range(2):
        for off in offsets(n):
            i = peer(first[half], off)
            tell_first(half, i, i).wait_recv()
        rows32[half] = told[half].astype(f32).reshape(n * HALF, 128)
        for h in range(HALF // 2):
            tile = [rows32[half, pl.ds(2 * h + s, n, stride=HALF), :] for s in range(2)]
            told_all[half, second[half], h] = jnp.concatenate(tile, axis=0).astype(bf16)
        begin(TELL_SECOND, half)

    def pass_on(t, carry):
        relay(TELL_SECOND, t)
        return carry

    lax.fori_loop(1, steps, pass_on, 0)
    loads[9].wait()
    out_rows = 2 * n
    first_rows = lax.rem(lax.broadcasted_iota(jnp.int32, (n * out_rows, 128), 0), out_rows) < n
    keep_first = first_rows.astype(f32).astype(bf16)
    keep_rest = (1.0 - first_rows.astype(f32)).astype(bf16)
    depth = HALF * HEAD_DIM
    mixed = []
    for half in range(2):
        finish(TELL_SECOND, half)
        pieces = []
        for h in range(HALF // 2):
            x = told_all[half, :, h].reshape(n * out_rows, 128)
            pieces.append(x * keep_first)
            pieces.append(x * keep_rest)
        acc = jnp.dot(
            jnp.concatenate(pieces, axis=1),
            w_buf[half * depth : (half + 1) * depth, :],
            preferred_element_type=f32,
        )
        mixed.append(jnp.sum(acc.reshape(n, 2, n, 128), axis=1))
    turn[...] = mixed[1].reshape(requests, 128)
    other = jnp.concatenate([turn[pl.ds(i, n, stride=n), :] for i in range(n)], axis=0)
    layer = res_buf[0].astype(f32) + (mixed[0].reshape(requests, 128) + other)
    line[...] = layer.astype(bf16)

    hand = pltpu.make_async_remote_copy(
        src_ref=line,
        dst_ref=landed,
        send_sem=pass_sem.at[0],
        recv_sem=pass_sem.at[1],
        device_id={"segment": following},
        device_id_type=MESH,
    )
    hand.start()

    for half in range(2):
        for off in offsets(n):
            i = peer(first[half], off)
            ask_first(half, i, i).wait_send()
            send_merged(half, i, i).wait_send()
            send_merged_stat(half, i, i).wait_send()
            tell_first(half, i, i).wait_send()
            i = peer(second[half], off)
            send_part(half, i, i).wait_send()
            send_part_stat(half, i, i).wait_send()
        for ring in (ASK_SECOND, TELL_SECOND):
            for way in range(2):
                for piece in range(2):
                    for t in range(1, steps + 1):
                        if t < steps or piece == way:
                            hop(ring, half, way, piece, t).wait_send()
    hand.wait()
    out_ref[...] = landed[...]


def local(
    n_seg,
    n,
    queries,
    new_key,
    new_value,
    key_pool,
    value_pool,
    lengths,
    block_device,
    block_slot,
    residual,
    out_weight,
):
    f32, bf16 = jnp.float32, jnp.bfloat16
    slots = key_pool.shape[1]
    tokens = slots * BLK
    requests = n * n
    whole = pl.BlockSpec(memory_space=pltpu.VMEM)
    outside = pl.BlockSpec(memory_space=pltpu.HBM)
    blocks = block_device.shape[2]
    out = pl.pallas_call(
        functools.partial(kernel, n_seg, n),
        out_shape=jax.ShapeDtypeStruct((requests, 128), bf16),
        in_specs=[outside] * 10,
        out_specs=whole,
        scratch_shapes=[
            pltpu.VMEM((1, 1, HEADS * HEAD_DIM), bf16),
            pltpu.VMEM((1, 1, KV_HEADS * HEAD_DIM), bf16),
            pltpu.VMEM((1, 1, KV_HEADS * HEAD_DIM), bf16),
            pltpu.VMEM((1, requests), jnp.int32),
            pltpu.VMEM((1, blocks, requests), jnp.int32),
            pltpu.VMEM((1, blocks, requests), jnp.int32),
            pltpu.VMEM((1, requests, 128), bf16),
            pltpu.VMEM((HEADS, 128), f32),
            pltpu.VMEM((2, 2, PAIR, 128), bf16),
            pltpu.VMEM((slots, BLK, KV_HEADS * HEAD_DIM), bf16),
            pltpu.VMEM((slots, BLK, KV_HEADS * HEAD_DIM), bf16),
            pltpu.VMEM((HEADS * HEAD_DIM, 128), bf16),
            pltpu.VMEM((4, 256, tokens), bf16),
            pltpu.VMEM((max(tokens // 128, 1), requests, min(tokens, 128)), f32),
            pltpu.VMEM((2, n, 2, n, PAIR, 128), bf16),
            pltpu.VMEM((2, n, n, HALF, 128), bf16),
            pltpu.VMEM((2, n, PAIR // 2, 128), f32),
            pltpu.VMEM((2, n, n, HALF, 128), bf16),
            pltpu.VMEM((2, n, PAIR // 2, 128), f32),
            pltpu.VMEM((2, n, HALF, 128), bf16),
            pltpu.VMEM((2, PAIR // 2, 128), f32),
            pltpu.VMEM((2, n, HALF, 128), bf16),
            pltpu.VMEM((2, n, PAIR // 2, 128), f32),
            pltpu.VMEM((2, HALF, 128), bf16),
            pltpu.VMEM((2, n, HALF, 128), bf16),
            pltpu.VMEM((2, n * HALF, 128), f32),
            pltpu.VMEM((2, n, HALF // 2, 2 * n, 128), bf16),
            pltpu.VMEM((requests, 128), f32),
            pltpu.VMEM((requests, 128), bf16),
            pltpu.VMEM((requests, 128), bf16),
            pltpu.SemaphoreType.DMA((6, 2, n)),
            pltpu.SemaphoreType.DMA((6, 2, n)),
            pltpu.SemaphoreType.DMA((2, 8 * (n // 2))),
            pltpu.SemaphoreType.DMA((2, 8 * (n // 2))),
            pltpu.SemaphoreType.DMA((10,)),
            pltpu.SemaphoreType.DMA((2,)),
        ],
        compiler_params=pltpu.CompilerParams(
            collective_id=0, has_side_effects=True, vmem_limit_bytes=40 * 1024 * 1024
        ),
        name="decode_layer",
    )(
        queries,
        new_key,
        new_value,
        lengths,
        jnp.swapaxes(block_device, 1, 2),
        jnp.swapaxes(block_slot, 1, 2),
        residual,
        key_pool[0],
        value_pool[0],
        out_weight[0],
    )
    return out[None]


def solution(mesh):
    placed = (
        P("segment", "kv", None),
        P("segment", "kv", None),
        P("segment", "kv", None),
        P("segment", "kv", None, None),
        P("segment", "kv", None, None),
        P("segment", None),
        P("segment", None, None),
        P("segment", None, None),
        P("segment", None, "kv"),
        P("segment", None, "kv"),
    )
    n_seg = mesh.shape["segment"]
    n = next(i for i in range(1, 64) if i * i == mesh.shape["kv"])
    return jax.shard_map(
        functools.partial(local, n_seg, n),
        mesh=mesh,
        in_specs=placed,
        out_specs=P("segment", None, "kv"),
        check_vma=False,
    )
```

```python
import functools

import jax
import jax.numpy as jnp
from jax import lax
from jax.experimental import pallas as pl
from jax.experimental.pallas import tpu as pltpu
from jax.sharding import PartitionSpec as P

KV_HEADS = 8
HEAD_DIM = 128
HEADS = 64
HALF = HEADS // 2
PAIR = 16
BLK = 16
MESH = pl.DeviceIdType.MESH
EMPTY = -1e30
FLOOR = -1e29
SCALE = HEAD_DIM ** (-0.5)
LOG2_E = 1.4426950408889634

ASK_FIRST, PART, PART_STAT, MERGED, MERGED_STAT, TELL_FIRST = range(6)
ASK_SECOND, TELL_SECOND = range(2)


def offsets(n):
    near = []
    for step in range(1, n // 2 + 1):
        near.append(step)
        if step != n - step:
            near.append(n - step)
    return near


def heads_in_row(raw, rows):
    flat = raw[0].astype(jnp.float32)
    for h in range(rows.shape[0]):
        rows[h : h + 1, :] = flat[:, h * HEAD_DIM : (h + 1) * HEAD_DIM]


def kernel(
    n_seg,
    n,
    q_hbm,
    nk_hbm,
    nv_hbm,
    len_hbm,
    dev_hbm,
    slot_hbm,
    res_hbm,
    k_hbm,
    v_hbm,
    w_hbm,
    out_ref,
    q_raw,
    nk_raw,
    nv_raw,
    len_buf,
    dev_buf,
    slot_buf,
    res_buf,
    rows64,
    q_ref,
    k_buf,
    v_buf,
    w_buf,
    kt_buf,
    bias_buf,
    q_all,
    part,
    part_stat,
    got,
    got_stat,
    merged,
    merged_stat,
    last,
    last_stat,
    attn,
    told,
    rows32,
    told_all,
    turn,
    line,
    landed,
    send_sem,
    recv_sem,
    ring_send,
    ring_recv,
    load_sem,
    pass_sem,
):
    f32, bf16 = jnp.float32, jnp.bfloat16
    seg = lax.axis_index("segment")
    me = lax.axis_index("kv")
    y, z = lax.div(me, n), lax.rem(me, n)
    first, second = (z, y), (y, z)
    slots = k_buf.shape[0]
    tokens = slots * BLK
    rows = n * PAIR

    def at_first(half, i):
        return y * n + i if half == 0 else i * n + z

    def at_second(half, i):
        return i * n + z if half == 0 else y * n + i

    def peer(base, off):
        return lax.rem(base + off, n)

    def copy(stage, half, src, dst, there, here, device):
        return pltpu.make_async_remote_copy(
            src_ref=src,
            dst_ref=dst,
            send_sem=send_sem.at[stage, half, there],
            recv_sem=recv_sem.at[stage, half, here],
            device_id={"kv": device},
            device_id_type=MESH,
        )

    following, before = lax.rem(seg + 1, n_seg), lax.rem(seg + n_seg - 1, n_seg)

    barrier = pltpu.get_barrier_semaphore()
    for off in offsets(n):
        for half in range(2):
            pl.semaphore_signal(
                barrier,
                inc=1,
                device_id={"kv": at_first(half, peer(first[half], off))},
                device_id_type=MESH,
            )
    for other in (following, before):
        pl.semaphore_signal(barrier, inc=1, device_id={"segment": other}, device_id_type=MESH)

    loads = [
        pltpu.make_async_copy(src, dst, load_sem.at[i])
        for i, (src, dst) in enumerate(
            (
                (q_hbm, q_raw),
                (len_hbm, len_buf),
                (dev_hbm, dev_buf),
                (slot_hbm, slot_buf),
                (k_hbm, k_buf),
                (v_hbm, v_buf),
                (nk_hbm, nk_raw),
                (nv_hbm, nv_raw),
                (res_hbm, res_buf),
                (w_hbm, w_buf),
            )
        )
    ]
    for load in loads:
        load.start()

    loads[0].wait()
    heads_in_row(q_raw, rows64)
    for half in range(2):
        for p in range(2):
            start = half * HALF + p * PAIR
            q_ref[half, p] = rows64[start : start + PAIR, :].astype(bf16)
            q_all[half, second[half], p, first[half]] = q_ref[half, p]

    pl.semaphore_wait(barrier, 2 * (n - 1) + 2)

    steps = n // 2

    def ask_first(half, i, here):
        return copy(
            ASK_FIRST,
            half,
            q_ref.at[half],
            q_all.at[half, second[half], :, here],
            i,
            here,
            at_first(half, i),
        )

    def origin(half, way, t):
        return lax.rem(second[half] + (n - t if way == 0 else t), n)

    def hop(ring, half, way, piece, t):
        index = ((half * 2 + way) * 2 + piece) * steps + t - 1
        block = origin(half, way, t - 1)
        if ring == ASK_SECOND:
            ref = q_all.at[half, block, piece]
        else:
            ref = told_all.at[half, block, pl.ds(piece * (HALF // 4), HALF // 4)]
        return pltpu.make_async_remote_copy(
            src_ref=ref,
            dst_ref=ref,
            send_sem=ring_send.at[ring, index],
            recv_sem=ring_recv.at[ring, index],
            device_id={"kv": at_second(half, peer(second[half], 1 if way == 0 else n - 1))},
            device_id_type=MESH,
        )

    def arrival(ring, half, way, piece, t):
        index = ((half * 2 + way) * 2 + piece) * steps + t - 1
        block = origin(half, way, t)
        if ring == ASK_SECOND:
            ref = q_all.at[half, block, piece]
        else:
            ref = told_all.at[half, block, pl.ds(piece * (HALF // 4), HALF // 4)]
        return pltpu.make_async_remote_copy(
            src_ref=ref,
            dst_ref=ref,
            send_sem=ring_send.at[ring, index],
            recv_sem=ring_recv.at[ring, index],
            device_id={"kv": at_second(half, peer(second[half], 1 if way == 0 else n - 1))},
            device_id_type=MESH,
        )

    def relay(ring, t):
        for piece in range(2):
            for half in range(2):
                for way in range(2):
                    arrival(ring, half, way, piece, t).wait_recv()
                    if piece == way:
                        hop(ring, half, way, piece, t + 1).start()
                    else:

                        @pl.when(t + 1 < steps)
                        def _():
                            hop(ring, half, way, piece, t + 1).start()

    def begin(ring, half):
        for piece in range(2):
            for way in range(2):
                if steps > 1 or piece == way:
                    hop(ring, half, way, piece, 1).start()

    def finish(ring, half):
        for way in range(2):
            arrival(ring, half, way, way, steps).wait_recv()

    for off in offsets(n):
        for half in range(2):
            ask_first(half, peer(first[half], off), first[half]).start()

    requests = n * n
    for load in loads[1:4]:
        load.wait()
    blocks = dev_buf.shape[1]
    holder = jnp.where(dev_buf[0] == me, slot_buf[0], -1)
    numbers = lax.broadcasted_iota(jnp.int32, (blocks, requests), 0)
    live = jnp.clip(len_buf[...] - numbers * BLK, 0, BLK).astype(f32)
    slot_of = lax.broadcasted_iota(jnp.int32, (slots, requests), 0)
    count = jnp.zeros((slots, requests), f32)
    for b in range(blocks):
        count = count + jnp.where(slot_of == holder[b : b + 1, :], live[b : b + 1, :], 0.0)
    spread = (
        lax.div(lax.broadcasted_iota(jnp.int32, (slots, tokens), 1), BLK)
        == lax.broadcasted_iota(jnp.int32, (slots, tokens), 0)
    ).astype(bf16)
    limit = lax.dot_general(
        count.astype(bf16), spread, (((0,), (0,)), ((), ())), preferred_element_type=f32
    )
    place = lax.rem(lax.broadcasted_iota(jnp.int32, (requests, tokens), 1), BLK).astype(f32)
    mask = jnp.where(place < limit, 0.0, EMPTY)
    wide = bias_buf.shape[2]
    for c in range(tokens // wide):
        bias_buf[c] = mask[:, c * wide : (c + 1) * wide]

    loads[4].wait()
    for pair in range(4):
        kt_buf[pair] = k_buf[:, :, pair * 256 : (pair + 1) * 256].reshape(tokens, 256).T

    for half in range(2):
        for off in offsets(n):
            i = peer(first[half], off)
            ask_first(half, i, i).wait_recv()
        begin(ASK_SECOND, half)
    loads[5].wait()

    def tiles(count):
        inside = lax.rem(lax.broadcasted_iota(jnp.int32, (count * PAIR, 128), 0), PAIR)
        return inside < PAIR // 2

    lane = lax.broadcasted_iota(jnp.int32, (PAIR // 2, 128), 1)

    def attend(half, those):
        count = len(those) * n
        upper = tiles(count)
        keep_upper = upper.astype(f32).astype(bf16)
        keep_lower = (1.0 - upper.astype(f32)).astype(bf16)
        bias = []
        for b in those:
            which = pl.ds(b * n, n) if half == 0 else pl.ds(b, n, stride=n)
            bias.append(
                jnp.concatenate([bias_buf[c, which, :] for c in range(tokens // wide)], axis=1)
            )
        bias = jnp.concatenate(bias, axis=0)
        bias = jnp.broadcast_to(bias[:, None, :], (count, PAIR, tokens)).reshape(
            count * PAIR, tokens
        )
        stats = [jnp.full((PAIR // 2, 128), EMPTY, f32) for _ in those]
        for p in range(2):
            pair = half * 2 + p
            x = jnp.concatenate([q_all[half, b, p].reshape(rows, 128) for b in those], axis=0)
            x = jnp.concatenate([x * keep_upper, x * keep_lower], axis=1)
            score = jnp.dot(x, kt_buf[pair], preferred_element_type=f32) + bias
            top = jnp.maximum(jnp.max(score, axis=1, keepdims=True), FLOOR)
            prob = jnp.exp2((score - top) * (SCALE * LOG2_E))
            total = jnp.sum(prob, axis=1, keepdims=True)
            value = v_buf[:, :, pair * 256 : (pair + 1) * 256].reshape(tokens, 256)
            acc = jnp.dot(prob.astype(bf16), value, preferred_element_type=f32)
            acc = jnp.where(upper, acc[:, :128], acc[:, 128:])
            acc = (acc / jnp.maximum(total, 0.5)).astype(bf16).reshape(count, PAIR, 128)
            lse = jnp.where(total > 0.0, top * SCALE + jnp.log(jnp.maximum(total, 0.5)), EMPTY)
            lse = lse.reshape(count, 2, PAIR // 2, 1)
            for k, b in enumerate(those):
                part[half, b, :, p * PAIR : (p + 1) * PAIR, :] = acc[k * n : (k + 1) * n]
                for r in range(n):
                    for side in range(2):
                        stats[k] = jnp.where(
                            lane == (side * 2 + p) * n + r, lse[k * n + r, side], stats[k]
                        )
        for k, b in enumerate(those):
            part_stat[half, b] = stats[k]

    def send_part(half, i, here):
        return copy(PART, half, part.at[half, i], got.at[half, here], i, here, at_second(half, i))

    def send_part_stat(half, i, here):
        return copy(
            PART_STAT, half, part_stat.at[half, i], got_stat.at[half, here], i, here, at_second(half, i)
        )

    def send_parts(half, b):
        send_part(half, b, second[half]).start()
        send_part_stat(half, b, second[half]).start()

    for half in range(2):
        attend(half, [second[half]])
        got[half, second[half]] = part[half, second[half]]
        got_stat[half, second[half]] = part_stat[half, second[half]]

    def one_step(t, carry):
        relay(ASK_SECOND, t)
        for half in range(2):
            those = [origin(half, way, t) for way in range(2)]
            attend(half, those)
            for b in those:
                send_parts(half, b)
        return carry

    lax.fori_loop(1, steps, one_step, 0)
    for half in range(2):
        finish(ASK_SECOND, half)
        those = [origin(half, 0, steps)]
        attend(half, those)
        send_parts(half, those[0])

    def send_merged(half, i, here):
        return copy(MERGED, half, merged.at[half, i], last.at[half, here], i, here, at_first(half, i))

    def send_merged_stat(half, i, here):
        return copy(
            MERGED_STAT, half, merged_stat.at[half], last_stat.at[half, here], i, here, at_first(half, i)
        )

    for half in range(2):
        for off in offsets(n):
            i = peer(second[half], off)
            send_part(half, i, i).wait_recv()
            send_part_stat(half, i, i).wait_recv()
        stat = got_stat[half]
        top = jnp.max(stat, axis=0)
        weight = jnp.exp(stat - top[None])
        total = jnp.sum(weight, axis=0)
        weight = weight / total[None]
        merged_stat[half] = top + jnp.log(total)
        for r in range(n):
            for p in range(2):
                scale = jnp.concatenate(
                    [
                        weight[:, :, (side * 2 + p) * n + r : (side * 2 + p) * n + r + 1]
                        for side in range(2)
                    ],
                    axis=1,
                )
                piece = got[half, :, r, p * PAIR : (p + 1) * PAIR, :].astype(f32)
                merged[half, r, p * PAIR : (p + 1) * PAIR, :] = jnp.sum(
                    piece * scale, axis=0
                ).astype(bf16)
        for off in offsets(n):
            i = peer(first[half], off)
            send_merged_stat(half, i, first[half]).start()
            send_merged(half, i, first[half]).start()
        last[half, first[half]] = merged[half, first[half]]
        last_stat[half, first[half]] = merged_stat[half]

    def tell_first(half, i, here):
        return copy(TELL_FIRST, half, attn.at[half], told.at[half, here], i, here, at_first(half, i))

    for load in loads[6:9]:
        load.wait()
    heads_in_row(nk_raw, rows64.at[pl.ds(0, KV_HEADS)])
    new_keys = rows64[:KV_HEADS, :]
    heads_in_row(nv_raw, rows64.at[pl.ds(KV_HEADS, KV_HEADS)])
    new_values = rows64[KV_HEADS : 2 * KV_HEADS, :]
    for half in range(2):
        kv_half = slice(half * 4, half * 4 + 4)
        query = q_ref[half].astype(f32).reshape(4, 8, 128)
        own = jnp.sum(query * new_keys[kv_half][:, None, :], axis=2, keepdims=True) * SCALE
        own = own.reshape(HALF, 1)
        own_value = jnp.broadcast_to(new_values[kv_half][:, None, :], (4, 8, 128)).reshape(HALF, 128)
        for off in offsets(n):
            i = peer(first[half], off)
            send_merged_stat(half, i, i).wait_recv()
            send_merged(half, i, i).wait_recv()
        lses = []
        for i in range(n):
            stat = last_stat[half, i]
            lses.append(
                jnp.concatenate(
                    [
                        jnp.sum(
                            jnp.where(lane == (side * 2 + p) * n + first[half], stat, 0.0),
                            axis=1,
                            keepdims=True,
                        )
                        for p in range(2)
                        for side in range(2)
                    ],
                    axis=0,
                )
            )
        top = own
        for lse in lses:
            top = jnp.maximum(top, lse)
        weight = jnp.exp(own - top)
        total = weight
        acc = weight * own_value
        for i in range(n):
            weight = jnp.exp(lses[i] - top)
            total = total + weight
            acc = acc + weight * last[half, i].astype(f32)
        attn[half] = (acc / total).astype(bf16)
        for off in offsets(n):
            tell_first(half, peer(first[half], off), first[half]).start()
        told[half, first[half]] = attn[half]

    for half in range(2):
        for off in offsets(n):
            i = peer(first[half], off)
            tell_first(half, i, i).wait_recv()
        rows32[half] = told[half].astype(f32).reshape(n * HALF, 128)
        for h in range(HALF // 2):
            tile = [rows32[half, pl.ds(2 * h + s, n, stride=HALF), :] for s in range(2)]
            told_all[half, second[half], h] = jnp.concatenate(tile, axis=0).astype(bf16)
        begin(TELL_SECOND, half)

    def pass_on(t, carry):
        relay(TELL_SECOND, t)
        return carry

    lax.fori_loop(1, steps, pass_on, 0)
    loads[9].wait()
    out_rows = 2 * n
    first_rows = lax.rem(lax.broadcasted_iota(jnp.int32, (n * out_rows, 128), 0), out_rows) < n
    keep_first = first_rows.astype(f32).astype(bf16)
    keep_rest = (1.0 - first_rows.astype(f32)).astype(bf16)
    depth = HALF * HEAD_DIM
    mixed = []
    for half in range(2):
        finish(TELL_SECOND, half)
        pieces = []
        for h in range(HALF // 2):
            x = told_all[half, :, h].reshape(n * out_rows, 128)
            pieces.append(x * keep_first)
            pieces.append(x * keep_rest)
        acc = jnp.dot(
            jnp.concatenate(pieces, axis=1),
            w_buf[half * depth : (half + 1) * depth, :],
            preferred_element_type=f32,
        )
        mixed.append(jnp.sum(acc.reshape(n, 2, n, 128), axis=1))
    turn[...] = mixed[1].reshape(requests, 128)
    other = jnp.concatenate([turn[pl.ds(i, n, stride=n), :] for i in range(n)], axis=0)
    layer = res_buf[0].astype(f32) + (mixed[0].reshape(requests, 128) + other)
    line[...] = layer.astype(bf16)

    hand = pltpu.make_async_remote_copy(
        src_ref=line,
        dst_ref=landed,
        send_sem=pass_sem.at[0],
        recv_sem=pass_sem.at[1],
        device_id={"segment": following},
        device_id_type=MESH,
    )
    hand.start()

    for half in range(2):
        for off in offsets(n):
            i = peer(first[half], off)
            ask_first(half, i, i).wait_send()
            send_merged(half, i, i).wait_send()
            send_merged_stat(half, i, i).wait_send()
            tell_first(half, i, i).wait_send()
            i = peer(second[half], off)
            send_part(half, i, i).wait_send()
            send_part_stat(half, i, i).wait_send()
        for ring in (ASK_SECOND, TELL_SECOND):
            for way in range(2):
                for piece in range(2):
                    for t in range(1, steps + 1):
                        if t < steps or piece == way:
                            hop(ring, half, way, piece, t).wait_send()
    hand.wait()
    out_ref[...] = landed[...]


def local(
    n_seg,
    n,
    queries,
    new_key,
    new_value,
    key_pool,
    value_pool,
    lengths,
    block_device,
    block_slot,
    residual,
    out_weight,
):
    f32, bf16 = jnp.float32, jnp.bfloat16
    slots = key_pool.shape[1]
    tokens = slots * BLK
    requests = n * n
    whole = pl.BlockSpec(memory_space=pltpu.VMEM)
    outside = pl.BlockSpec(memory_space=pltpu.HBM)
    blocks = block_device.shape[2]
    out = pl.pallas_call(
        functools.partial(kernel, n_seg, n),
        out_shape=jax.ShapeDtypeStruct((requests, 128), bf16),
        in_specs=[outside] * 10,
        out_specs=whole,
        scratch_shapes=[
            pltpu.VMEM((1, 1, HEADS * HEAD_DIM), bf16),
            pltpu.VMEM((1, 1, KV_HEADS * HEAD_DIM), bf16),
            pltpu.VMEM((1, 1, KV_HEADS * HEAD_DIM), bf16),
            pltpu.VMEM((1, requests), jnp.int32),
            pltpu.VMEM((1, blocks, requests), jnp.int32),
            pltpu.VMEM((1, blocks, requests), jnp.int32),
            pltpu.VMEM((1, requests, 128), bf16),
            pltpu.VMEM((HEADS, 128), f32),
            pltpu.VMEM((2, 2, PAIR, 128), bf16),
            pltpu.VMEM((slots, BLK, KV_HEADS * HEAD_DIM), bf16),
            pltpu.VMEM((slots, BLK, KV_HEADS * HEAD_DIM), bf16),
            pltpu.VMEM((HEADS * HEAD_DIM, 128), bf16),
            pltpu.VMEM((4, 256, tokens), bf16),
            pltpu.VMEM((max(tokens // 128, 1), requests, min(tokens, 128)), f32),
            pltpu.VMEM((2, n, 2, n, PAIR, 128), bf16),
            pltpu.VMEM((2, n, n, HALF, 128), bf16),
            pltpu.VMEM((2, n, PAIR // 2, 128), f32),
            pltpu.VMEM((2, n, n, HALF, 128), bf16),
            pltpu.VMEM((2, n, PAIR // 2, 128), f32),
            pltpu.VMEM((2, n, HALF, 128), bf16),
            pltpu.VMEM((2, PAIR // 2, 128), f32),
            pltpu.VMEM((2, n, HALF, 128), bf16),
            pltpu.VMEM((2, n, PAIR // 2, 128), f32),
            pltpu.VMEM((2, HALF, 128), bf16),
            pltpu.VMEM((2, n, HALF, 128), bf16),
            pltpu.VMEM((2, n * HALF, 128), f32),
            pltpu.VMEM((2, n, HALF // 2, 2 * n, 128), bf16),
            pltpu.VMEM((requests, 128), f32),
            pltpu.VMEM((requests, 128), bf16),
            pltpu.VMEM((requests, 128), bf16),
            pltpu.SemaphoreType.DMA((6, 2, n)),
            pltpu.SemaphoreType.DMA((6, 2, n)),
            pltpu.SemaphoreType.DMA((2, 8 * (n // 2))),
            pltpu.SemaphoreType.DMA((2, 8 * (n // 2))),
            pltpu.SemaphoreType.DMA((10,)),
            pltpu.SemaphoreType.DMA((2,)),
        ],
        compiler_params=pltpu.CompilerParams(
            collective_id=0, has_side_effects=True, vmem_limit_bytes=60 * 1024 * 1024
        ),
        name="decode_layer",
    )(
        queries,
        new_key,
        new_value,
        lengths,
        jnp.swapaxes(block_device, 1, 2),
        jnp.swapaxes(block_slot, 1, 2),
        residual,
        key_pool[0],
        value_pool[0],
        out_weight[0],
    )
    return out[None]


def solution(mesh):
    placed = (
        P("segment", "kv", None),
        P("segment", "kv", None),
        P("segment", "kv", None),
        P("segment", "kv", None, None),
        P("segment", "kv", None, None),
        P("segment", None),
        P("segment", None, None),
        P("segment", None, None),
        P("segment", None, "kv"),
        P("segment", None, "kv"),
    )
    n_seg = mesh.shape["segment"]
    n = next(i for i in range(1, 64) if i * i == mesh.shape["kv"])
    return jax.shard_map(
        functools.partial(local, n_seg, n),
        mesh=mesh,
        in_specs=placed,
        out_specs=P("segment", None, "kv"),
        check_vma=False,
    )
```

```python
import functools

import jax
import jax.numpy as jnp
from jax import lax
from jax.experimental import pallas as pl
from jax.experimental.pallas import tpu as pltpu
from jax.sharding import PartitionSpec as P

KV_HEADS = 8
HEAD_DIM = 128
HEADS = 64
HALF = HEADS // 2
PAIR = 16
BLK = 16
MESH = pl.DeviceIdType.MESH
EMPTY = -1e30
FLOOR = -1e29
SCALE = HEAD_DIM ** (-0.5)
LOG2_E = 1.4426950408889634

ASK_FIRST, PART, MERGED, TELL_FIRST = range(4)
ASK_SECOND, TELL_SECOND = range(2)


def offsets(n):
    near = []
    for step in range(1, n // 2 + 1):
        near.append(step)
        if step != n - step:
            near.append(n - step)
    return near


def heads_in_row(raw, rows):
    flat = raw[0].astype(jnp.float32)
    for h in range(rows.shape[0]):
        rows[h : h + 1, :] = flat[:, h * HEAD_DIM : (h + 1) * HEAD_DIM]


def kernel(
    n_seg,
    n,
    q_hbm,
    nk_hbm,
    nv_hbm,
    len_hbm,
    dev_hbm,
    slot_hbm,
    res_hbm,
    k_hbm,
    v_hbm,
    w_hbm,
    out_ref,
    q_raw,
    nk_raw,
    nv_raw,
    len_buf,
    dev_buf,
    slot_buf,
    res_buf,
    rows64,
    q_ref,
    k_buf,
    v_buf,
    w_buf,
    kt_buf,
    bias_buf,
    q_all,
    part,
    got,
    merged,
    last,
    attn,
    told,
    rows32,
    told_all,
    turn,
    line,
    landed,
    send_sem,
    recv_sem,
    ring_send,
    ring_recv,
    load_sem,
    pass_sem,
):
    f32, bf16 = jnp.float32, jnp.bfloat16
    seg = lax.axis_index("segment")
    me = lax.axis_index("kv")
    y, z = lax.div(me, n), lax.rem(me, n)
    first, second = (z, y), (y, z)
    slots = k_buf.shape[0]
    tokens = slots * BLK
    rows = n * PAIR

    def at_first(half, i):
        return y * n + i if half == 0 else i * n + z

    def at_second(half, i):
        return i * n + z if half == 0 else y * n + i

    def peer(base, off):
        return lax.rem(base + off, n)

    def copy(stage, half, src, dst, device):
        return pltpu.make_async_remote_copy(
            src_ref=src,
            dst_ref=dst,
            send_sem=send_sem.at[stage, half],
            recv_sem=recv_sem.at[stage, half],
            device_id={"kv": device},
            device_id_type=MESH,
        )

    def neighbours(half):
        return at_first(half, peer(first[half], 1)), at_second(half, peer(second[half], 1))

    following, before = lax.rem(seg + 1, n_seg), lax.rem(seg + n_seg - 1, n_seg)

    barrier = pltpu.get_barrier_semaphore()
    for off in offsets(n):
        for half in range(2):
            pl.semaphore_signal(
                barrier,
                inc=1,
                device_id={"kv": at_first(half, peer(first[half], off))},
                device_id_type=MESH,
            )
    for other in (following, before):
        pl.semaphore_signal(barrier, inc=1, device_id={"segment": other}, device_id_type=MESH)

    loads = [
        pltpu.make_async_copy(src, dst, load_sem.at[i])
        for i, (src, dst) in enumerate(
            (
                (q_hbm, q_raw),
                (len_hbm, len_buf),
                (dev_hbm, dev_buf),
                (slot_hbm, slot_buf),
                (k_hbm, k_buf),
                (v_hbm, v_buf),
                (nk_hbm, nk_raw),
                (nv_hbm, nv_raw),
                (res_hbm, res_buf),
                (w_hbm.at[:, 0], w_buf.at[0]),
                (w_hbm.at[:, 1], w_buf.at[1]),
            )
        )
    ]
    for load in loads:
        load.start()

    loads[0].wait()
    heads_in_row(q_raw, rows64)
    for half in range(2):
        for p in range(2):
            start = half * HALF + p * PAIR
            q_ref[half, p] = rows64[start : start + PAIR, :].astype(bf16)
            q_all[half, second[half], p, first[half]] = q_ref[half, p]

    pl.semaphore_wait(barrier, 2 * (n - 1) + 2)

    steps = n // 2

    def ask_first(half, i):
        mine = first[half]
        return copy(
            ASK_FIRST, half, q_ref.at[half], q_all.at[half, second[half], :, mine], at_first(half, i)
        )

    def asked(half):
        every = q_all.at[half, second[half], :, pl.ds(0, n - 1)]
        return copy(ASK_FIRST, half, every, every, neighbours(half)[0])

    def origin(half, way, t):
        return lax.rem(second[half] + (n - t if way == 0 else t), n)

    def piece_of(ring, half, block, piece):
        if ring == ASK_SECOND:
            return q_all.at[half, block] if piece is None else q_all.at[half, block, piece]
        rows_of = HALF // 4
        return told_all.at[half, block, pl.ds(piece * rows_of, rows_of)]

    def ring_copy(ring, half, way, piece, t, block):
        index = ((half * 2 + way) * 2 + (piece or 0)) * steps + t - 1
        ref = piece_of(ring, half, block, piece)
        return pltpu.make_async_remote_copy(
            src_ref=ref,
            dst_ref=ref,
            send_sem=ring_send.at[ring, index],
            recv_sem=ring_recv.at[ring, index],
            device_id={"kv": at_second(half, peer(second[half], 1 if way == 0 else n - 1))},
            device_id_type=MESH,
        )

    def hop(ring, half, way, piece, t):
        return ring_copy(ring, half, way, piece, t, origin(half, way, t - 1))

    def arrival(ring, half, way, piece, t):
        return ring_copy(ring, half, way, piece, t, origin(half, way, t))

    def ask_hop(half, way, t):
        if isinstance(t, int):
            hop(ASK_SECOND, half, way, None if t < steps else way, t).start()
        else:

            @pl.when(t < steps)
            def _():
                hop(ASK_SECOND, half, way, None, t).start()

            @pl.when(t == steps)
            def _():
                hop(ASK_SECOND, half, way, way, t).start()

    def ask_relay(t):
        for half in range(2):
            for way in range(2):
                arrival(ASK_SECOND, half, way, None, t).wait_recv()
                ask_hop(half, way, t + 1)

    def relay(ring, t):
        for piece in range(2):
            for half in range(2):
                for way in range(2):
                    arrival(ring, half, way, piece, t).wait_recv()
                    if piece == way:
                        hop(ring, half, way, piece, t + 1).start()
                    else:

                        @pl.when(t + 1 < steps)
                        def _():
                            hop(ring, half, way, piece, t + 1).start()

    def begin(ring, half):
        for piece in range(2):
            for way in range(2):
                if steps > 1 or piece == way:
                    hop(ring, half, way, piece, 1).start()

    def finish(ring, half):
        for way in range(2):
            arrival(ring, half, way, way, steps).wait_recv()

    for off in offsets(n):
        for half in range(2):
            ask_first(half, peer(first[half], off)).start()

    requests = n * n
    for load in loads[1:4]:
        load.wait()
    blocks = dev_buf.shape[1]
    holder = jnp.where(dev_buf[0] == me, slot_buf[0], -1)
    numbers = lax.broadcasted_iota(jnp.int32, (blocks, requests), 0)
    live = jnp.clip(len_buf[...] - numbers * BLK, 0, BLK).astype(f32)
    slot_of = lax.broadcasted_iota(jnp.int32, (slots, requests), 0)
    count = jnp.zeros((slots, requests), f32)
    for b in range(blocks):
        count = count + jnp.where(slot_of == holder[b : b + 1, :], live[b : b + 1, :], 0.0)
    spread = (
        lax.div(lax.broadcasted_iota(jnp.int32, (slots, tokens), 1), BLK)
        == lax.broadcasted_iota(jnp.int32, (slots, tokens), 0)
    ).astype(bf16)
    limit = lax.dot_general(
        count.astype(bf16), spread, (((0,), (0,)), ((), ())), preferred_element_type=f32
    )
    place = lax.rem(lax.broadcasted_iota(jnp.int32, (requests, tokens), 1), BLK).astype(f32)
    mask = jnp.where(place < limit, 0.0, EMPTY)
    wide = bias_buf.shape[2]
    for c in range(tokens // wide):
        bias_buf[c] = mask[:, c * wide : (c + 1) * wide]

    for half in range(2):
        asked(half).wait_recv()
        for way in range(2):
            ask_hop(half, way, 1)
    loads[4].wait()
    for pair in range(4):
        kt_buf[pair] = k_buf[:, :, pair * 256 : (pair + 1) * 256].reshape(tokens, 256).T
    loads[5].wait()

    def tiles(count):
        inside = lax.rem(lax.broadcasted_iota(jnp.int32, (count * PAIR, 128), 0), PAIR)
        return inside < PAIR // 2

    lane = lax.broadcasted_iota(jnp.int32, (PAIR // 2, 128), 1)
    used = 4 * n

    def pack(stat):
        high = stat.astype(bf16).astype(f32)
        rest = stat - high
        middle = rest.astype(bf16).astype(f32)
        low = rest - middle
        both = jnp.where(
            lane < used,
            high,
            jnp.where(lane < 2 * used, pltpu.roll(middle, used, 1), pltpu.roll(low, 2 * used, 1)),
        )
        return jnp.concatenate([both, jnp.zeros_like(both)], axis=0).astype(bf16)

    def unpack(tile):
        sides = tile.astype(f32)[: PAIR // 2]
        return (sides + pltpu.roll(sides, 128 - used, 1)) + pltpu.roll(sides, 128 - 2 * used, 1)

    def attend(half, those):
        count = len(those) * n
        upper = tiles(count)
        keep_upper = upper.astype(f32).astype(bf16)
        keep_lower = (1.0 - upper.astype(f32)).astype(bf16)
        bias = []
        for b in those:
            which = pl.ds(b * n, n) if half == 0 else pl.ds(b, n, stride=n)
            bias.append(
                jnp.concatenate([bias_buf[c, which, :] for c in range(tokens // wide)], axis=1)
            )
        bias = jnp.concatenate(bias, axis=0)
        bias = jnp.broadcast_to(bias[:, None, :], (count, PAIR, tokens)).reshape(
            count * PAIR, tokens
        )
        stats = [jnp.full((PAIR // 2, 128), EMPTY, f32) for _ in those]
        for p in range(2):
            pair = half * 2 + p
            x = jnp.concatenate([q_all[half, b, p].reshape(rows, 128) for b in those], axis=0)
            x = jnp.concatenate([x * keep_upper, x * keep_lower], axis=1)
            score = jnp.dot(x, kt_buf[pair], preferred_element_type=f32) + bias
            top = jnp.maximum(jnp.max(score, axis=1, keepdims=True), FLOOR)
            prob = jnp.exp2((score - top) * (SCALE * LOG2_E))
            total = jnp.sum(prob, axis=1, keepdims=True)
            value = v_buf[:, :, pair * 256 : (pair + 1) * 256].reshape(tokens, 256)
            acc = jnp.dot(prob.astype(bf16), value, preferred_element_type=f32)
            acc = jnp.where(upper, acc[:, :128], acc[:, 128:])
            acc = (acc / jnp.maximum(total, 0.5)).astype(bf16).reshape(count, PAIR, 128)
            lse = jnp.where(total > 0.0, top * SCALE + jnp.log(jnp.maximum(total, 0.5)), EMPTY)
            lse = lse.reshape(count, 2, PAIR // 2, 1)
            for k, b in enumerate(those):
                for r in range(n):
                    part[half, b, r * HALF + p * PAIR : r * HALF + (p + 1) * PAIR, :] = acc[k * n + r]
                    for side in range(2):
                        stats[k] = jnp.where(
                            lane == (side * 2 + p) * n + r, lse[k * n + r, side], stats[k]
                        )
        for k, b in enumerate(those):
            part[half, b, n * HALF :, :] = pack(stats[k])

    def send_part(half, i):
        return copy(PART, half, part.at[half, i], got.at[half, second[half]], at_second(half, i))

    def parted(half):
        every = got.at[half, pl.ds(0, n - 1)]
        return copy(PART, half, every, every, neighbours(half)[1])

    for half in range(2):
        attend(half, [second[half]])
        got[half, second[half]] = part[half, second[half]]

    def one_step(t, carry):
        ask_relay(t)
        for half in range(2):
            those = [origin(half, way, t) for way in range(2)]
            attend(half, those)
            for b in those:
                send_part(half, b).start()
        return carry

    lax.fori_loop(1, steps, one_step, 0)
    for half in range(2):
        finish(ASK_SECOND, half)
        those = [origin(half, 0, steps)]
        attend(half, those)
        send_part(half, those[0]).start()

    def send_merged(half, i):
        return copy(MERGED, half, merged.at[half, i], last.at[half, first[half]], at_first(half, i))

    def all_merged(half):
        every = last.at[half, pl.ds(0, n - 1)]
        return copy(MERGED, half, every, every, neighbours(half)[0])

    for half in range(2):
        parted(half).wait_recv()
        stat = jnp.stack([unpack(got[half, i, n * HALF :, :]) for i in range(n)], axis=0)
        top = jnp.max(stat, axis=0)
        weight = jnp.exp(stat - top[None])
        total = jnp.sum(weight, axis=0)
        weight = weight / total[None]
        tail = pack(top + jnp.log(total))
        for r in range(n):
            for p in range(2):
                scale = jnp.concatenate(
                    [
                        weight[:, :, (side * 2 + p) * n + r : (side * 2 + p) * n + r + 1]
                        for side in range(2)
                    ],
                    axis=1,
                )
                start = r * HALF + p * PAIR
                piece = got[half, :, start : start + PAIR, :].astype(f32)
                merged[half, r, p * PAIR : (p + 1) * PAIR, :] = jnp.sum(
                    piece * scale, axis=0
                ).astype(bf16)
            merged[half, r, HALF:, :] = tail
        for off in offsets(n):
            send_merged(half, peer(first[half], off)).start()
        last[half, first[half]] = merged[half, first[half]]

    def tell_first(half, i):
        return copy(TELL_FIRST, half, attn.at[half], told.at[half, first[half]], at_first(half, i))

    def all_told(half):
        every = told.at[half, pl.ds(0, n - 1)]
        return copy(TELL_FIRST, half, every, every, neighbours(half)[0])

    for load in loads[6:9]:
        load.wait()
    heads_in_row(nk_raw, rows64.at[pl.ds(0, KV_HEADS)])
    new_keys = rows64[:KV_HEADS, :]
    heads_in_row(nv_raw, rows64.at[pl.ds(KV_HEADS, KV_HEADS)])
    new_values = rows64[KV_HEADS : 2 * KV_HEADS, :]
    for half in range(2):
        kv_half = slice(half * 4, half * 4 + 4)
        query = q_ref[half].astype(f32).reshape(4, 8, 128)
        own = jnp.sum(query * new_keys[kv_half][:, None, :], axis=2, keepdims=True) * SCALE
        own = own.reshape(HALF, 1)
        own_value = jnp.broadcast_to(new_values[kv_half][:, None, :], (4, 8, 128)).reshape(HALF, 128)
        all_merged(half).wait_recv()
        lses = []
        for i in range(n):
            stat = unpack(last[half, i, HALF:, :])
            lses.append(
                jnp.concatenate(
                    [
                        jnp.sum(
                            jnp.where(lane == (side * 2 + p) * n + first[half], stat, 0.0),
                            axis=1,
                            keepdims=True,
                        )
                        for p in range(2)
                        for side in range(2)
                    ],
                    axis=0,
                )
            )
        top = own
        for lse in lses:
            top = jnp.maximum(top, lse)
        weight = jnp.exp(own - top)
        total = weight
        acc = weight * own_value
        for i in range(n):
            weight = jnp.exp(lses[i] - top)
            total = total + weight
            acc = acc + weight * last[half, i, :HALF, :].astype(f32)
        attn[half] = (acc / total).astype(bf16)
        for off in offsets(n):
            tell_first(half, peer(first[half], off)).start()
        told[half, first[half]] = attn[half]

    for half in range(2):
        all_told(half).wait_recv()
        rows32[half] = told[half].astype(f32).reshape(n * HALF, 128)
        for h in range(HALF // 2):
            tile = [rows32[half, pl.ds(2 * h + s, n, stride=HALF), :] for s in range(2)]
            told_all[half, second[half], h] = jnp.concatenate(tile, axis=0).astype(bf16)
        begin(TELL_SECOND, half)

    def pass_on(t, carry):
        relay(TELL_SECOND, t)
        return carry

    lax.fori_loop(1, steps, pass_on, 0)
    loads[9].wait()
    loads[10].wait()
    depth = HALF // 2 * HEAD_DIM
    mixed = []
    for half in range(2):
        finish(TELL_SECOND, half)
        x = jnp.concatenate(
            [told_all[half, :, h].reshape(n * 2 * n, 128) for h in range(HALF // 2)], axis=1
        )
        w = jnp.concatenate(
            [
                w_buf[side, half * (HALF // 2) : (half + 1) * (HALF // 2)].reshape(depth, 128)
                for side in range(2)
            ],
            axis=1,
        )
        acc = jnp.dot(x, w, preferred_element_type=f32).reshape(n, 2, n, 256)
        mixed.append(acc[:, 0, :, :128] + acc[:, 1, :, 128:])
    turn[...] = mixed[1].reshape(requests, 128)
    other = jnp.concatenate([turn[pl.ds(i, n, stride=n), :] for i in range(n)], axis=0)
    layer = res_buf[0].astype(f32) + (mixed[0].reshape(requests, 128) + other)
    line[...] = layer.astype(bf16)

    hand = pltpu.make_async_remote_copy(
        src_ref=line,
        dst_ref=landed,
        send_sem=pass_sem.at[0],
        recv_sem=pass_sem.at[1],
        device_id={"segment": following},
        device_id_type=MESH,
    )
    hand.start()

    for half in range(2):
        for stage in (asked, parted, all_merged, all_told):
            stage(half).wait_send()
        for way in range(2):
            for t in range(1, steps + 1):
                hop(ASK_SECOND, half, way, None if t < steps else way, t).wait_send()
            for piece in range(2):
                for t in range(1, steps + 1):
                    if t < steps or piece == way:
                        hop(TELL_SECOND, half, way, piece, t).wait_send()
    hand.wait()
    out_ref[...] = landed[...]


def local(
    n_seg,
    n,
    queries,
    new_key,
    new_value,
    key_pool,
    value_pool,
    lengths,
    block_device,
    block_slot,
    residual,
    out_weight,
):
    f32, bf16 = jnp.float32, jnp.bfloat16
    slots = key_pool.shape[1]
    tokens = slots * BLK
    requests = n * n
    whole = pl.BlockSpec(memory_space=pltpu.VMEM)
    outside = pl.BlockSpec(memory_space=pltpu.HBM)
    blocks = block_device.shape[2]
    out = pl.pallas_call(
        functools.partial(kernel, n_seg, n),
        out_shape=jax.ShapeDtypeStruct((requests, 128), bf16),
        in_specs=[outside] * 10,
        out_specs=whole,
        scratch_shapes=[
            pltpu.VMEM((1, 1, HEADS * HEAD_DIM), bf16),
            pltpu.VMEM((1, 1, KV_HEADS * HEAD_DIM), bf16),
            pltpu.VMEM((1, 1, KV_HEADS * HEAD_DIM), bf16),
            pltpu.VMEM((1, requests), jnp.int32),
            pltpu.VMEM((1, blocks, requests), jnp.int32),
            pltpu.VMEM((1, blocks, requests), jnp.int32),
            pltpu.VMEM((1, requests, 128), bf16),
            pltpu.VMEM((HEADS, 128), f32),
            pltpu.VMEM((2, 2, PAIR, 128), bf16),
            pltpu.VMEM((slots, BLK, KV_HEADS * HEAD_DIM), bf16),
            pltpu.VMEM((slots, BLK, KV_HEADS * HEAD_DIM), bf16),
            pltpu.VMEM((2, HEADS // 2, HEAD_DIM, 128), bf16),
            pltpu.VMEM((4, 256, tokens), bf16),
            pltpu.VMEM((max(tokens // 128, 1), requests, min(tokens, 128)), f32),
            pltpu.VMEM((2, n, 2, n, PAIR, 128), bf16),
            pltpu.VMEM((2, n, n * HALF + PAIR, 128), bf16),
            pltpu.VMEM((2, n, n * HALF + PAIR, 128), bf16),
            pltpu.VMEM((2, n, HALF + PAIR, 128), bf16),
            pltpu.VMEM((2, n, HALF + PAIR, 128), bf16),
            pltpu.VMEM((2, HALF, 128), bf16),
            pltpu.VMEM((2, n, HALF, 128), bf16),
            pltpu.VMEM((2, n * HALF, 128), f32),
            pltpu.VMEM((2, n, HALF // 2, 2 * n, 128), bf16),
            pltpu.VMEM((requests, 128), f32),
            pltpu.VMEM((requests, 128), bf16),
            pltpu.VMEM((requests, 128), bf16),
            pltpu.SemaphoreType.DMA((4, 2)),
            pltpu.SemaphoreType.DMA((4, 2)),
            pltpu.SemaphoreType.DMA((2, 8 * (n // 2))),
            pltpu.SemaphoreType.DMA((2, 8 * (n // 2))),
            pltpu.SemaphoreType.DMA((11,)),
            pltpu.SemaphoreType.DMA((2,)),
        ],
        compiler_params=pltpu.CompilerParams(
            collective_id=0, has_side_effects=True, vmem_limit_bytes=60 * 1024 * 1024
        ),
        name="decode_layer",
    )(
        queries,
        new_key,
        new_value,
        lengths,
        jnp.swapaxes(block_device, 1, 2),
        jnp.swapaxes(block_slot, 1, 2),
        residual,
        key_pool[0],
        value_pool[0],
        out_weight[0].reshape(HEADS // 2, 2, HEAD_DIM, 128),
    )
    return out[None]


def solution(mesh):
    placed = (
        P("segment", "kv", None),
        P("segment", "kv", None),
        P("segment", "kv", None),
        P("segment", "kv", None, None),
        P("segment", "kv", None, None),
        P("segment", None),
        P("segment", None, None),
        P("segment", None, None),
        P("segment", None, "kv"),
        P("segment", None, "kv"),
    )
    n_seg = mesh.shape["segment"]
    n = next(i for i in range(1, 64) if i * i == mesh.shape["kv"])
    return jax.shard_map(
        functools.partial(local, n_seg, n),
        mesh=mesh,
        in_specs=placed,
        out_specs=P("segment", None, "kv"),
        check_vma=False,
    )
```

```python
import functools

import jax
import jax.numpy as jnp
from jax import lax
from jax.experimental import pallas as pl
from jax.experimental.pallas import tpu as pltpu
from jax.sharding import PartitionSpec as P

KV_HEADS = 8
HEAD_DIM = 128
HEADS = 64
HALF = HEADS // 2
PAIR = 16
BLK = 16
MESH = pl.DeviceIdType.MESH
EMPTY = -1e30
FLOOR = -1e29
SCALE = HEAD_DIM ** (-0.5)
LOG2_E = 1.4426950408889634

ASK_FIRST, PART, MERGED, TELL_FIRST = range(4)
ASK_SECOND, TELL_SECOND = range(2)


def offsets(n):
    near = []
    for step in range(1, n // 2 + 1):
        near.append(step)
        if step != n - step:
            near.append(n - step)
    return near


def heads_in_row(raw, rows):
    flat = raw[0].astype(jnp.float32)
    for h in range(rows.shape[0]):
        rows[h : h + 1, :] = flat[:, h * HEAD_DIM : (h + 1) * HEAD_DIM]


def kernel(
    n_seg,
    n,
    q_hbm,
    nk_hbm,
    nv_hbm,
    len_hbm,
    dev_hbm,
    slot_hbm,
    res_hbm,
    k_hbm,
    v_hbm,
    w_hbm,
    out_ref,
    q_raw,
    nk_raw,
    nv_raw,
    len_buf,
    dev_buf,
    slot_buf,
    res_buf,
    rows64,
    q_ref,
    k_buf,
    v_buf,
    w_buf,
    kt_buf,
    bias_buf,
    q_all,
    part,
    got,
    merged,
    last,
    attn,
    told,
    rows32,
    told_all,
    turn,
    line,
    landed,
    send_sem,
    recv_sem,
    ring_send,
    ring_recv,
    load_sem,
    pass_sem,
):
    f32, bf16 = jnp.float32, jnp.bfloat16
    seg = lax.axis_index("segment")
    me = lax.axis_index("kv")
    y, z = lax.div(me, n), lax.rem(me, n)
    first, second = (z, y), (y, z)
    slots = k_buf.shape[0]
    tokens = slots * BLK
    rows = n * PAIR

    def at_first(half, i):
        return y * n + i if half == 0 else i * n + z

    def at_second(half, i):
        return i * n + z if half == 0 else y * n + i

    def peer(base, off):
        return lax.rem(base + off, n)

    def copy(stage, half, src, dst, device):
        return pltpu.make_async_remote_copy(
            src_ref=src,
            dst_ref=dst,
            send_sem=send_sem.at[stage, half],
            recv_sem=recv_sem.at[stage, half],
            device_id={"kv": device},
            device_id_type=MESH,
        )

    def neighbours(half):
        return at_first(half, peer(first[half], 1)), at_second(half, peer(second[half], 1))

    following, before = lax.rem(seg + 1, n_seg), lax.rem(seg + n_seg - 1, n_seg)

    barrier = pltpu.get_barrier_semaphore()
    for off in offsets(n):
        for half in range(2):
            pl.semaphore_signal(
                barrier,
                inc=1,
                device_id={"kv": at_first(half, peer(first[half], off))},
                device_id_type=MESH,
            )
    for other in (following, before):
        pl.semaphore_signal(barrier, inc=1, device_id={"segment": other}, device_id_type=MESH)

    loads = [
        pltpu.make_async_copy(src, dst, load_sem.at[i])
        for i, (src, dst) in enumerate(
            (
                (q_hbm, q_raw),
                (len_hbm, len_buf),
                (dev_hbm, dev_buf),
                (slot_hbm, slot_buf),
                (k_hbm, k_buf),
                (v_hbm, v_buf),
                (nk_hbm, nk_raw),
                (nv_hbm, nv_raw),
                (res_hbm, res_buf),
                (w_hbm.at[:, 0], w_buf.at[0]),
                (w_hbm.at[:, 1], w_buf.at[1]),
            )
        )
    ]
    for load in loads:
        load.start()

    loads[0].wait()
    heads_in_row(q_raw, rows64)
    for half in range(2):
        for p in range(2):
            start = half * HALF + p * PAIR
            q_ref[half, p] = rows64[start : start + PAIR, :].astype(bf16)
            q_all[half, second[half], p, first[half]] = q_ref[half, p]

    pl.semaphore_wait(barrier, 2 * (n - 1) + 2)

    steps = n // 2

    def ask_first(half, i):
        mine = first[half]
        return copy(
            ASK_FIRST, half, q_ref.at[half], q_all.at[half, second[half], :, mine], at_first(half, i)
        )

    def asked(half):
        every = q_all.at[half, second[half], :, pl.ds(0, n - 1)]
        return copy(ASK_FIRST, half, every, every, neighbours(half)[0])

    def origin(half, way, t):
        return lax.rem(second[half] + (n - t if way == 0 else t), n)

    def piece_of(ring, half, block, piece):
        if ring == ASK_SECOND:
            return q_all.at[half, block] if piece is None else q_all.at[half, block, piece]
        rows_of = HALF // 4
        return told_all.at[half, block, pl.ds(piece * rows_of, rows_of)]

    def ring_copy(ring, half, way, piece, t, block):
        index = ((half * 2 + way) * 2 + (piece or 0)) * steps + t - 1
        ref = piece_of(ring, half, block, piece)
        return pltpu.make_async_remote_copy(
            src_ref=ref,
            dst_ref=ref,
            send_sem=ring_send.at[ring, index],
            recv_sem=ring_recv.at[ring, index],
            device_id={"kv": at_second(half, peer(second[half], 1 if way == 0 else n - 1))},
            device_id_type=MESH,
        )

    def hop(ring, half, way, piece, t):
        return ring_copy(ring, half, way, piece, t, origin(half, way, t - 1))

    def arrival(ring, half, way, piece, t):
        return ring_copy(ring, half, way, piece, t, origin(half, way, t))

    def ask_hop(half, way, t):
        if isinstance(t, int):
            hop(ASK_SECOND, half, way, None if t < steps else way, t).start()
        else:

            @pl.when(t < steps)
            def _():
                hop(ASK_SECOND, half, way, None, t).start()

            @pl.when(t == steps)
            def _():
                hop(ASK_SECOND, half, way, way, t).start()

    def ask_relay(t):
        for half in range(2):
            for way in range(2):
                arrival(ASK_SECOND, half, way, None, t).wait_recv()
                ask_hop(half, way, t + 1)

    def relay(ring, t):
        for piece in range(2):
            for half in range(2):
                for way in range(2):
                    arrival(ring, half, way, piece, t).wait_recv()
                    if piece == way:
                        hop(ring, half, way, piece, t + 1).start()
                    else:

                        @pl.when(t + 1 < steps)
                        def _():
                            hop(ring, half, way, piece, t + 1).start()

    def begin(ring, half):
        for piece in range(2):
            for way in range(2):
                if steps > 1 or piece == way:
                    hop(ring, half, way, piece, 1).start()

    def finish(ring, half):
        for way in range(2):
            arrival(ring, half, way, way, steps).wait_recv()

    for off in offsets(n):
        for half in range(2):
            ask_first(half, peer(first[half], off)).start()

    requests = n * n
    for load in loads[1:4]:
        load.wait()
    blocks = dev_buf.shape[1]
    holder = jnp.where(dev_buf[0] == me, slot_buf[0], -1)
    numbers = lax.broadcasted_iota(jnp.int32, (blocks, requests), 0)
    live = jnp.clip(len_buf[...] - numbers * BLK, 0, BLK).astype(f32)
    slot_of = lax.broadcasted_iota(jnp.int32, (slots, requests), 0)
    count = jnp.zeros((slots, requests), f32)
    for b in range(blocks):
        count = count + jnp.where(slot_of == holder[b : b + 1, :], live[b : b + 1, :], 0.0)
    spread = (
        lax.div(lax.broadcasted_iota(jnp.int32, (slots, tokens), 1), BLK)
        == lax.broadcasted_iota(jnp.int32, (slots, tokens), 0)
    ).astype(bf16)
    limit = lax.dot_general(
        count.astype(bf16), spread, (((0,), (0,)), ((), ())), preferred_element_type=f32
    )
    place = lax.rem(lax.broadcasted_iota(jnp.int32, (requests, tokens), 1), BLK).astype(f32)
    mask = jnp.where(place < limit, 0.0, EMPTY)
    for r in range(requests):
        bias_buf[r] = jnp.broadcast_to(mask[r : r + 1, :], (PAIR // 2, tokens))

    for half in range(2):
        asked(half).wait_recv()
        for way in range(2):
            ask_hop(half, way, 1)
    loads[4].wait()
    for pair in range(4):
        kt_buf[pair] = k_buf[:, :, pair * 256 : (pair + 1) * 256].reshape(tokens, 256).T
    loads[5].wait()

    def tiles(count):
        inside = lax.rem(lax.broadcasted_iota(jnp.int32, (count * PAIR, 128), 0), PAIR)
        return inside < PAIR // 2

    lane = lax.broadcasted_iota(jnp.int32, (PAIR // 2, 128), 1)
    used = 4 * n

    def three(stat):
        high = stat.astype(bf16).astype(f32)
        rest = stat - high
        middle = rest.astype(bf16).astype(f32)
        low = rest - middle
        return jnp.where(
            lane < used,
            high,
            jnp.where(lane < 2 * used, pltpu.roll(middle, used, 1), pltpu.roll(low, 2 * used, 1)),
        )

    def pack(above, below):
        return jnp.concatenate([three(above), three(below)], axis=0).astype(bf16)

    def unpack(tile):
        sides = tile.astype(f32)
        sides = (sides + pltpu.roll(sides, 128 - used, 1)) + pltpu.roll(sides, 128 - 2 * used, 1)
        return sides[: PAIR // 2], sides[PAIR // 2 :]

    def attend(half, those):
        count = len(those) * n
        upper = tiles(count)
        keep_upper = upper.astype(f32).astype(bf16)
        keep_lower = (1.0 - upper.astype(f32)).astype(bf16)
        bias = jnp.concatenate(
            [
                bias_buf[pl.ds(b * n, n)]
                if half == 0
                else jnp.stack([bias_buf[f * n + b] for f in range(n)], axis=0)
                for b in those
            ],
            axis=0,
        )
        tops = [jnp.full((PAIR // 2, 128), FLOOR, f32) for _ in those]
        totals = [jnp.zeros((PAIR // 2, 128), f32) for _ in those]
        for p in range(2):
            pair = half * 2 + p
            x = jnp.concatenate([q_all[half, b, p].reshape(rows, 128) for b in those], axis=0)
            x = jnp.concatenate([x * keep_upper, x * keep_lower], axis=1)
            score = jnp.dot(x, kt_buf[pair], preferred_element_type=f32)
            score = score.reshape(count, 2, PAIR // 2, tokens) + bias[:, None]
            score = score.reshape(count * PAIR, tokens)
            top = jnp.maximum(jnp.max(score, axis=1, keepdims=True), FLOOR)
            prob = jnp.exp2((score - top) * (SCALE * LOG2_E))
            total = jnp.sum(prob, axis=1, keepdims=True)
            value = v_buf[:, :, pair * 256 : (pair + 1) * 256].reshape(tokens, 256)
            acc = jnp.dot(prob.astype(bf16), value, preferred_element_type=f32)
            acc = jnp.where(upper, acc[:, :128], acc[:, 128:])
            acc = acc.astype(bf16).reshape(count, PAIR, 128)
            top = top.reshape(count, 2, PAIR // 2, 1)
            total = total.reshape(count, 2, PAIR // 2, 1)
            for k, b in enumerate(those):
                for r in range(n):
                    part[half, b, r * HALF + p * PAIR : r * HALF + (p + 1) * PAIR, :] = acc[k * n + r]
                    for side in range(2):
                        here = lane == (side * 2 + p) * n + r
                        tops[k] = jnp.where(here, top[k * n + r, side], tops[k])
                        totals[k] = jnp.where(here, total[k * n + r, side], totals[k])
        for k, b in enumerate(those):
            part[half, b, n * HALF :, :] = pack(tops[k], totals[k])

    def send_part(half, i):
        return copy(PART, half, part.at[half, i], got.at[half, second[half]], at_second(half, i))

    def parted(half):
        every = got.at[half, pl.ds(0, n - 1)]
        return copy(PART, half, every, every, neighbours(half)[1])

    for half in range(2):
        attend(half, [second[half]])
        got[half, second[half]] = part[half, second[half]]

    def one_step(t, carry):
        ask_relay(t)
        those = [[origin(half, way, t) for way in range(2)] for half in range(2)]
        for half in range(2):
            attend(half, those[half])
        for half in range(2):
            for b in those[half]:
                send_part(half, b).start()
        return carry

    lax.fori_loop(1, steps, one_step, 0)
    for half in range(2):
        finish(ASK_SECOND, half)
        those = [origin(half, 0, steps)]
        attend(half, those)
        send_part(half, those[0]).start()

    def send_merged(half, i):
        return copy(MERGED, half, merged.at[half, i], last.at[half, first[half]], at_first(half, i))

    def all_merged(half):
        every = last.at[half, pl.ds(0, n - 1)]
        return copy(MERGED, half, every, every, neighbours(half)[0])

    for half in range(2):
        parted(half).wait_recv()
        sides = [unpack(got[half, i, n * HALF :, :]) for i in range(n)]
        tops = jnp.stack([above for above, _ in sides], axis=0)
        totals = jnp.stack([below for _, below in sides], axis=0)
        top = jnp.max(tops, axis=0)
        weight = jnp.exp((tops - top[None]) * SCALE)
        total = jnp.sum(weight * totals, axis=0)
        some = jnp.maximum(total, 0.5)
        weight = weight / some[None]
        lse = jnp.where(total > 0.0, top * SCALE + jnp.log(some), EMPTY)
        tail = pack(lse, jnp.zeros_like(lse))
        for r in range(n):
            for p in range(2):
                scale = jnp.concatenate(
                    [
                        weight[:, :, (side * 2 + p) * n + r : (side * 2 + p) * n + r + 1]
                        for side in range(2)
                    ],
                    axis=1,
                )
                start = r * HALF + p * PAIR
                piece = got[half, :, start : start + PAIR, :].astype(f32)
                merged[half, r, p * PAIR : (p + 1) * PAIR, :] = jnp.sum(
                    piece * scale, axis=0
                ).astype(bf16)
            merged[half, r, HALF:, :] = tail
        for off in offsets(n):
            send_merged(half, peer(first[half], off)).start()
        last[half, first[half]] = merged[half, first[half]]

    def tell_first(half, i):
        return copy(TELL_FIRST, half, attn.at[half], told.at[half, first[half]], at_first(half, i))

    def all_told(half):
        every = told.at[half, pl.ds(0, n - 1)]
        return copy(TELL_FIRST, half, every, every, neighbours(half)[0])

    for load in loads[6:9]:
        load.wait()
    heads_in_row(nk_raw, rows64.at[pl.ds(0, KV_HEADS)])
    new_keys = rows64[:KV_HEADS, :]
    heads_in_row(nv_raw, rows64.at[pl.ds(KV_HEADS, KV_HEADS)])
    new_values = rows64[KV_HEADS : 2 * KV_HEADS, :]
    for half in range(2):
        kv_half = slice(half * 4, half * 4 + 4)
        query = q_ref[half].astype(f32).reshape(4, 8, 128)
        own = jnp.sum(query * new_keys[kv_half][:, None, :], axis=2, keepdims=True) * SCALE
        own = own.reshape(HALF, 1)
        own_value = jnp.broadcast_to(new_values[kv_half][:, None, :], (4, 8, 128)).reshape(HALF, 128)
        all_merged(half).wait_recv()
        lses = []
        for i in range(n):
            stat = unpack(last[half, i, HALF:, :])[0]
            lses.append(
                jnp.concatenate(
                    [
                        jnp.sum(
                            jnp.where(lane == (side * 2 + p) * n + first[half], stat, 0.0),
                            axis=1,
                            keepdims=True,
                        )
                        for p in range(2)
                        for side in range(2)
                    ],
                    axis=0,
                )
            )
        top = own
        for lse in lses:
            top = jnp.maximum(top, lse)
        weight = jnp.exp(own - top)
        total = weight
        acc = weight * own_value
        for i in range(n):
            weight = jnp.exp(lses[i] - top)
            total = total + weight
            acc = acc + weight * last[half, i, :HALF, :].astype(f32)
        attn[half] = (acc / total).astype(bf16)
        for off in offsets(n):
            tell_first(half, peer(first[half], off)).start()
        told[half, first[half]] = attn[half]

    for half in range(2):
        all_told(half).wait_recv()
        rows32[half] = told[half].astype(f32).reshape(n * HALF, 128)
        for h in range(HALF // 2):
            tile = [rows32[half, pl.ds(2 * h + s, n, stride=HALF), :] for s in range(2)]
            told_all[half, second[half], h] = jnp.concatenate(tile, axis=0).astype(bf16)
        begin(TELL_SECOND, half)

    def pass_on(t, carry):
        relay(TELL_SECOND, t)
        return carry

    lax.fori_loop(1, steps, pass_on, 0)
    loads[9].wait()
    loads[10].wait()
    depth = HALF // 2 * HEAD_DIM
    mixed = []
    for half in range(2):
        finish(TELL_SECOND, half)
        x = jnp.concatenate(
            [told_all[half, :, h].reshape(n * 2 * n, 128) for h in range(HALF // 2)], axis=1
        )
        w = jnp.concatenate(
            [
                w_buf[side, half * (HALF // 2) : (half + 1) * (HALF // 2)].reshape(depth, 128)
                for side in range(2)
            ],
            axis=1,
        )
        acc = jnp.dot(x, w, preferred_element_type=f32).reshape(n, 2, n, 256)
        mixed.append(acc[:, 0, :, :128] + acc[:, 1, :, 128:])
    turn[...] = mixed[1].reshape(requests, 128)
    other = jnp.concatenate([turn[pl.ds(i, n, stride=n), :] for i in range(n)], axis=0)
    layer = res_buf[0].astype(f32) + (mixed[0].reshape(requests, 128) + other)
    line[...] = layer.astype(bf16)

    hand = pltpu.make_async_remote_copy(
        src_ref=line,
        dst_ref=landed,
        send_sem=pass_sem.at[0],
        recv_sem=pass_sem.at[1],
        device_id={"segment": following},
        device_id_type=MESH,
    )
    hand.start()

    for half in range(2):
        for stage in (asked, parted, all_merged, all_told):
            stage(half).wait_send()
        for way in range(2):
            for t in range(1, steps + 1):
                hop(ASK_SECOND, half, way, None if t < steps else way, t).wait_send()
            for piece in range(2):
                for t in range(1, steps + 1):
                    if t < steps or piece == way:
                        hop(TELL_SECOND, half, way, piece, t).wait_send()
    hand.wait()
    out_ref[...] = landed[...]


def local(
    n_seg,
    n,
    queries,
    new_key,
    new_value,
    key_pool,
    value_pool,
    lengths,
    block_device,
    block_slot,
    residual,
    out_weight,
):
    f32, bf16 = jnp.float32, jnp.bfloat16
    slots = key_pool.shape[1]
    tokens = slots * BLK
    requests = n * n
    whole = pl.BlockSpec(memory_space=pltpu.VMEM)
    outside = pl.BlockSpec(memory_space=pltpu.HBM)
    blocks = block_device.shape[2]
    out = pl.pallas_call(
        functools.partial(kernel, n_seg, n),
        out_shape=jax.ShapeDtypeStruct((requests, 128), bf16),
        in_specs=[outside] * 10,
        out_specs=whole,
        scratch_shapes=[
            pltpu.VMEM((1, 1, HEADS * HEAD_DIM), bf16),
            pltpu.VMEM((1, 1, KV_HEADS * HEAD_DIM), bf16),
            pltpu.VMEM((1, 1, KV_HEADS * HEAD_DIM), bf16),
            pltpu.VMEM((1, requests), jnp.int32),
            pltpu.VMEM((1, blocks, requests), jnp.int32),
            pltpu.VMEM((1, blocks, requests), jnp.int32),
            pltpu.VMEM((1, requests, 128), bf16),
            pltpu.VMEM((HEADS, 128), f32),
            pltpu.VMEM((2, 2, PAIR, 128), bf16),
            pltpu.VMEM((slots, BLK, KV_HEADS * HEAD_DIM), bf16),
            pltpu.VMEM((slots, BLK, KV_HEADS * HEAD_DIM), bf16),
            pltpu.VMEM((2, HEADS // 2, HEAD_DIM, 128), bf16),
            pltpu.VMEM((4, 256, tokens), bf16),
            pltpu.VMEM((requests, PAIR // 2, tokens), f32),
            pltpu.VMEM((2, n, 2, n, PAIR, 128), bf16),
            pltpu.VMEM((2, n, n * HALF + PAIR, 128), bf16),
            pltpu.VMEM((2, n, n * HALF + PAIR, 128), bf16),
            pltpu.VMEM((2, n, HALF + PAIR, 128), bf16),
            pltpu.VMEM((2, n, HALF + PAIR, 128), bf16),
            pltpu.VMEM((2, HALF, 128), bf16),
            pltpu.VMEM((2, n, HALF, 128), bf16),
            pltpu.VMEM((2, n * HALF, 128), f32),
            pltpu.VMEM((2, n, HALF // 2, 2 * n, 128), bf16),
            pltpu.VMEM((requests, 128), f32),
            pltpu.VMEM((requests, 128), bf16),
            pltpu.VMEM((requests, 128), bf16),
            pltpu.SemaphoreType.DMA((4, 2)),
            pltpu.SemaphoreType.DMA((4, 2)),
            pltpu.SemaphoreType.DMA((2, 8 * (n // 2))),
            pltpu.SemaphoreType.DMA((2, 8 * (n // 2))),
            pltpu.SemaphoreType.DMA((11,)),
            pltpu.SemaphoreType.DMA((2,)),
        ],
        compiler_params=pltpu.CompilerParams(
            collective_id=0, has_side_effects=True, vmem_limit_bytes=60 * 1024 * 1024
        ),
        name="decode_layer",
    )(
        queries,
        new_key,
        new_value,
        lengths,
        jnp.swapaxes(block_device, 1, 2),
        jnp.swapaxes(block_slot, 1, 2),
        residual,
        key_pool[0],
        value_pool[0],
        out_weight[0].reshape(HEADS // 2, 2, HEAD_DIM, 128),
    )
    return out[None]


def solution(mesh):
    placed = (
        P("segment", "kv", None),
        P("segment", "kv", None),
        P("segment", "kv", None),
        P("segment", "kv", None, None),
        P("segment", "kv", None, None),
        P("segment", None),
        P("segment", None, None),
        P("segment", None, None),
        P("segment", None, "kv"),
        P("segment", None, "kv"),
    )
    n_seg = mesh.shape["segment"]
    n = next(i for i in range(1, 64) if i * i == mesh.shape["kv"])
    return jax.shard_map(
        functools.partial(local, n_seg, n),
        mesh=mesh,
        in_specs=placed,
        out_specs=P("segment", None, "kv"),
        check_vma=False,
    )
```

```python
import functools

import jax
import jax.numpy as jnp
from jax import lax
from jax.experimental import pallas as pl
from jax.experimental.pallas import tpu as pltpu
from jax.sharding import PartitionSpec as P

KV_HEADS = 8
HEAD_DIM = 128
HEADS = 64
HALF = HEADS // 2
PAIR = 16
BLK = 16
MESH = pl.DeviceIdType.MESH
EMPTY = -1e30
FLOOR = -1e29
SCALE = HEAD_DIM ** (-0.5)
LOG2_E = 1.4426950408889634

ASK_FIRST, PART, MERGED, TELL_FIRST = range(4)
ASK_SECOND, TELL_SECOND = range(2)

LEGS = (
    (0, None, 3, -3),
    (0, None, -3, 3),
    (0, None, 1, -1),
    (0, None, -1, 1),
    (-3, None, -1, -2),
    (3, None, 1, 2),
    (-3, 0, 1, -4),
    (3, 1, -1, 4),
)


def offsets(n):
    near = []
    for step in range(1, n // 2 + 1):
        near.append(step)
        if step != n - step:
            near.append(n - step)
    return near


def heads_in_row(raw, rows):
    flat = raw[0].astype(jnp.float32)
    for h in range(rows.shape[0]):
        rows[h : h + 1, :] = flat[:, h * HEAD_DIM : (h + 1) * HEAD_DIM]


def kernel(
    n_seg,
    n,
    q_hbm,
    nk_hbm,
    nv_hbm,
    len_hbm,
    dev_hbm,
    slot_hbm,
    res_hbm,
    k_hbm,
    v_hbm,
    w_hbm,
    out_ref,
    q_raw,
    nk_raw,
    nv_raw,
    len_buf,
    dev_buf,
    slot_buf,
    res_buf,
    rows64,
    q_ref,
    k_buf,
    v_buf,
    w_buf,
    kt_buf,
    bias_buf,
    q_all,
    part,
    got,
    merged,
    last,
    attn,
    told,
    rows32,
    told_all,
    turn,
    line,
    landed,
    send_sem,
    recv_sem,
    leg_send,
    leg_recv,
    load_sem,
    pass_sem,
):
    f32, bf16 = jnp.float32, jnp.bfloat16
    seg = lax.axis_index("segment")
    me = lax.axis_index("kv")
    y, z = lax.div(me, n), lax.rem(me, n)
    first, second = (z, y), (y, z)
    slots = k_buf.shape[0]
    tokens = slots * BLK
    rows = n * PAIR

    def at_first(half, i):
        return y * n + i if half == 0 else i * n + z

    def at_second(half, i):
        return i * n + z if half == 0 else y * n + i

    def peer(base, off):
        return lax.rem(base + off, n)

    def copy(stage, half, src, dst, device):
        return pltpu.make_async_remote_copy(
            src_ref=src,
            dst_ref=dst,
            send_sem=send_sem.at[stage, half],
            recv_sem=recv_sem.at[stage, half],
            device_id={"kv": device},
            device_id_type=MESH,
        )

    def neighbours(half):
        return at_first(half, peer(first[half], 1)), at_second(half, peer(second[half], 1))

    following, before = lax.rem(seg + 1, n_seg), lax.rem(seg + n_seg - 1, n_seg)

    barrier = pltpu.get_barrier_semaphore()
    for off in offsets(n):
        for half in range(2):
            pl.semaphore_signal(
                barrier,
                inc=1,
                device_id={"kv": at_first(half, peer(first[half], off))},
                device_id_type=MESH,
            )
    for other in (following, before):
        pl.semaphore_signal(barrier, inc=1, device_id={"segment": other}, device_id_type=MESH)

    loads = [
        pltpu.make_async_copy(src, dst, load_sem.at[i])
        for i, (src, dst) in enumerate(
            (
                (q_hbm, q_raw),
                (len_hbm, len_buf),
                (dev_hbm, dev_buf),
                (slot_hbm, slot_buf),
                (k_hbm, k_buf),
                (v_hbm, v_buf),
                (nk_hbm, nk_raw),
                (nv_hbm, nv_raw),
                (res_hbm, res_buf),
                (w_hbm.at[:, 0], w_buf.at[0]),
                (w_hbm.at[:, 1], w_buf.at[1]),
            )
        )
    ]
    for load in loads:
        load.start()

    loads[0].wait()
    heads_in_row(q_raw, rows64)
    for half in range(2):
        for p in range(2):
            start = half * HALF + p * PAIR
            q_ref[half, p] = rows64[start : start + PAIR, :].astype(bf16)
            q_all[half, second[half], p, first[half]] = q_ref[half, p]

    pl.semaphore_wait(barrier, 2 * (n - 1) + 2)

    def ask_first(half, i):
        mine = first[half]
        return copy(
            ASK_FIRST, half, q_ref.at[half], q_all.at[half, second[half], :, mine], at_first(half, i)
        )

    def asked(half):
        every = q_all.at[half, second[half], :, pl.ds(0, n - 1)]
        return copy(ASK_FIRST, half, every, every, neighbours(half)[0])

    def piece_of(ring, half, block, piece):
        if piece is None:
            return (q_all if ring == ASK_SECOND else told_all).at[half, block]
        if ring == ASK_SECOND:
            return q_all.at[half, block, piece]
        rows_of = HALF // 4
        return told_all.at[half, block, pl.ds(piece * rows_of, rows_of)]

    def leg_copy(ring, half, leg, block):
        ref = piece_of(ring, half, peer(second[half], n + block), LEGS[leg][1])
        return pltpu.make_async_remote_copy(
            src_ref=ref,
            dst_ref=ref,
            send_sem=leg_send.at[ring, half * len(LEGS) + leg],
            recv_sem=leg_recv.at[ring, half * len(LEGS) + leg],
            device_id={"kv": at_second(half, peer(second[half], n + LEGS[leg][2]))},
            device_id_type=MESH,
        )

    def leave(ring, half, leg):
        return leg_copy(ring, half, leg, LEGS[leg][0])

    def arrive(ring, half, leg):
        return leg_copy(ring, half, leg, LEGS[leg][3])

    def begin(ring, half):
        for leg in range(4):
            leave(ring, half, leg).start()

    def forward(ring, half):
        for way in range(2):
            arrive(ring, half, way).wait_recv()
            leave(ring, half, 4 + way).start()
        for way in range(2):
            leave(ring, half, 6 + way).start()

    for off in offsets(n):
        for half in range(2):
            ask_first(half, peer(first[half], off)).start()

    requests = n * n
    for load in loads[1:4]:
        load.wait()
    blocks = dev_buf.shape[1]
    holder = jnp.where(dev_buf[0] == me, slot_buf[0], -1)
    numbers = lax.broadcasted_iota(jnp.int32, (blocks, requests), 0)
    live = jnp.clip(len_buf[...] - numbers * BLK, 0, BLK).astype(f32)
    slot_of = lax.broadcasted_iota(jnp.int32, (slots, requests), 0)
    count = jnp.zeros((slots, requests), f32)
    for b in range(blocks):
        count = count + jnp.where(slot_of == holder[b : b + 1, :], live[b : b + 1, :], 0.0)
    spread = (
        lax.div(lax.broadcasted_iota(jnp.int32, (slots, tokens), 1), BLK)
        == lax.broadcasted_iota(jnp.int32, (slots, tokens), 0)
    ).astype(bf16)
    limit = lax.dot_general(
        count.astype(bf16), spread, (((0,), (0,)), ((), ())), preferred_element_type=f32
    )
    place = lax.rem(lax.broadcasted_iota(jnp.int32, (requests, tokens), 1), BLK).astype(f32)
    mask = jnp.where(place < limit, 0.0, EMPTY)
    for r in range(requests):
        bias_buf[r] = jnp.broadcast_to(mask[r : r + 1, :], (PAIR // 2, tokens))

    for half in range(2):
        asked(half).wait_recv()
        begin(ASK_SECOND, half)
    loads[4].wait()
    for pair in range(4):
        kt_buf[pair] = k_buf[:, :, pair * 256 : (pair + 1) * 256].reshape(tokens, 256).T
    loads[5].wait()

    def tiles(count):
        inside = lax.rem(lax.broadcasted_iota(jnp.int32, (count * PAIR, 128), 0), PAIR)
        return inside < PAIR // 2

    lane = lax.broadcasted_iota(jnp.int32, (PAIR // 2, 128), 1)
    used = 4 * n

    def three(stat):
        high = stat.astype(bf16).astype(f32)
        rest = stat - high
        middle = rest.astype(bf16).astype(f32)
        low = rest - middle
        return jnp.where(
            lane < used,
            high,
            jnp.where(lane < 2 * used, pltpu.roll(middle, used, 1), pltpu.roll(low, 2 * used, 1)),
        )

    def pack(above, below):
        return jnp.concatenate([three(above), three(below)], axis=0).astype(bf16)

    def unpack(tile):
        sides = tile.astype(f32)
        sides = (sides + pltpu.roll(sides, 128 - used, 1)) + pltpu.roll(sides, 128 - 2 * used, 1)
        return sides[: PAIR // 2], sides[PAIR // 2 :]

    def attend(half, those):
        count = len(those) * n
        upper = tiles(count)
        keep_upper = upper.astype(f32).astype(bf16)
        keep_lower = (1.0 - upper.astype(f32)).astype(bf16)
        bias = jnp.concatenate(
            [
                bias_buf[pl.ds(b * n, n)]
                if half == 0
                else jnp.stack([bias_buf[f * n + b] for f in range(n)], axis=0)
                for b in those
            ],
            axis=0,
        )
        tops = [jnp.full((PAIR // 2, 128), FLOOR, f32) for _ in those]
        totals = [jnp.zeros((PAIR // 2, 128), f32) for _ in those]
        for p in range(2):
            pair = half * 2 + p
            x = jnp.concatenate([q_all[half, b, p].reshape(rows, 128) for b in those], axis=0)
            x = jnp.concatenate([x * keep_upper, x * keep_lower], axis=1)
            score = jnp.dot(x, kt_buf[pair], preferred_element_type=f32)
            score = score.reshape(count, 2, PAIR // 2, tokens) + bias[:, None]
            score = score.reshape(count * PAIR, tokens)
            top = jnp.maximum(jnp.max(score, axis=1, keepdims=True), FLOOR)
            prob = jnp.exp2((score - top) * (SCALE * LOG2_E))
            total = jnp.sum(prob, axis=1, keepdims=True)
            value = v_buf[:, :, pair * 256 : (pair + 1) * 256].reshape(tokens, 256)
            acc = jnp.dot(prob.astype(bf16), value, preferred_element_type=f32)
            acc = jnp.where(upper, acc[:, :128], acc[:, 128:])
            acc = acc.astype(bf16).reshape(count, PAIR, 128)
            top = top.reshape(count, 2, PAIR // 2, 1)
            total = total.reshape(count, 2, PAIR // 2, 1)
            for k, b in enumerate(those):
                for r in range(n):
                    part[half, b, r * HALF + p * PAIR : r * HALF + (p + 1) * PAIR, :] = acc[k * n + r]
                    for side in range(2):
                        here = lane == (side * 2 + p) * n + r
                        tops[k] = jnp.where(here, top[k * n + r, side], tops[k])
                        totals[k] = jnp.where(here, total[k * n + r, side], totals[k])
        for k, b in enumerate(those):
            part[half, b, n * HALF :, :] = pack(tops[k], totals[k])

    def send_part(half, i):
        return copy(PART, half, part.at[half, i], got.at[half, second[half]], at_second(half, i))

    def parted(half):
        every = got.at[half, pl.ds(0, n - 1)]
        return copy(PART, half, every, every, neighbours(half)[1])

    for half in range(2):
        attend(half, [second[half]])
        got[half, second[half]] = part[half, second[half]]

    for half in range(2):
        forward(ASK_SECOND, half)

    def one_step(t, carry):
        @pl.when(t == 1)
        def _():
            for half in range(2):
                for leg in (2, 3):
                    arrive(ASK_SECOND, half, leg).wait_recv()

        @pl.when(t == 2)
        def _():
            for half in range(2):
                for leg in (4, 5):
                    arrive(ASK_SECOND, half, leg).wait_recv()

        away = lax.rem(t + 2, 3) + 1
        those = [
            [peer(second[half], n - away), peer(second[half], away)] for half in range(2)
        ]
        for half in range(2):
            attend(half, those[half])
        for half in range(2):
            for b in those[half]:
                send_part(half, b).start()
        return carry

    lax.fori_loop(0, 3, one_step, 0)
    for half in range(2):
        for leg in (6, 7):
            arrive(ASK_SECOND, half, leg).wait_recv()
        across = peer(second[half], n // 2)
        attend(half, [across])
        send_part(half, across).start()

    def send_merged(half, i):
        return copy(MERGED, half, merged.at[half, i], last.at[half, first[half]], at_first(half, i))

    def all_merged(half):
        every = last.at[half, pl.ds(0, n - 1)]
        return copy(MERGED, half, every, every, neighbours(half)[0])

    for half in range(2):
        parted(half).wait_recv()
        sides = [unpack(got[half, i, n * HALF :, :]) for i in range(n)]
        tops = jnp.stack([above for above, _ in sides], axis=0)
        totals = jnp.stack([below for _, below in sides], axis=0)
        top = jnp.max(tops, axis=0)
        weight = jnp.exp((tops - top[None]) * SCALE)
        total = jnp.sum(weight * totals, axis=0)
        some = jnp.maximum(total, 0.5)
        weight = weight / some[None]
        lse = jnp.where(total > 0.0, top * SCALE + jnp.log(some), EMPTY)
        tail = pack(lse, jnp.zeros_like(lse))
        for r in range(n):
            for p in range(2):
                scale = jnp.concatenate(
                    [
                        weight[:, :, (side * 2 + p) * n + r : (side * 2 + p) * n + r + 1]
                        for side in range(2)
                    ],
                    axis=1,
                )
                start = r * HALF + p * PAIR
                piece = got[half, :, start : start + PAIR, :].astype(f32)
                merged[half, r, p * PAIR : (p + 1) * PAIR, :] = jnp.sum(
                    piece * scale, axis=0
                ).astype(bf16)
            merged[half, r, HALF:, :] = tail
        for off in offsets(n):
            send_merged(half, peer(first[half], off)).start()
        last[half, first[half]] = merged[half, first[half]]

    def tell_first(half, i):
        return copy(TELL_FIRST, half, attn.at[half], told.at[half, first[half]], at_first(half, i))

    def all_told(half):
        every = told.at[half, pl.ds(0, n - 1)]
        return copy(TELL_FIRST, half, every, every, neighbours(half)[0])

    for load in loads[6:9]:
        load.wait()
    heads_in_row(nk_raw, rows64.at[pl.ds(0, KV_HEADS)])
    new_keys = rows64[:KV_HEADS, :]
    heads_in_row(nv_raw, rows64.at[pl.ds(KV_HEADS, KV_HEADS)])
    new_values = rows64[KV_HEADS : 2 * KV_HEADS, :]
    for half in range(2):
        kv_half = slice(half * 4, half * 4 + 4)
        query = q_ref[half].astype(f32).reshape(4, 8, 128)
        own = jnp.sum(query * new_keys[kv_half][:, None, :], axis=2, keepdims=True) * SCALE
        own = own.reshape(HALF, 1)
        own_value = jnp.broadcast_to(new_values[kv_half][:, None, :], (4, 8, 128)).reshape(HALF, 128)
        all_merged(half).wait_recv()
        lses = []
        for i in range(n):
            stat = unpack(last[half, i, HALF:, :])[0]
            lses.append(
                jnp.concatenate(
                    [
                        jnp.sum(
                            jnp.where(lane == (side * 2 + p) * n + first[half], stat, 0.0),
                            axis=1,
                            keepdims=True,
                        )
                        for p in range(2)
                        for side in range(2)
                    ],
                    axis=0,
                )
            )
        top = own
        for lse in lses:
            top = jnp.maximum(top, lse)
        weight = jnp.exp(own - top)
        total = weight
        acc = weight * own_value
        for i in range(n):
            weight = jnp.exp(lses[i] - top)
            total = total + weight
            acc = acc + weight * last[half, i, :HALF, :].astype(f32)
        attn[half] = (acc / total).astype(bf16)
        for off in offsets(n):
            tell_first(half, peer(first[half], off)).start()
        told[half, first[half]] = attn[half]

    for half in range(2):
        all_told(half).wait_recv()
        rows32[half] = told[half].astype(f32).reshape(n * HALF, 128)
        for h in range(HALF // 2):
            tile = [rows32[half, pl.ds(2 * h + s, n, stride=HALF), :] for s in range(2)]
            told_all[half, second[half], h] = jnp.concatenate(tile, axis=0).astype(bf16)
        begin(TELL_SECOND, half)

    for half in range(2):
        forward(TELL_SECOND, half)
    loads[9].wait()
    loads[10].wait()
    depth = HALF // 2 * HEAD_DIM
    mixed = []
    for half in range(2):
        for leg in range(2, len(LEGS)):
            arrive(TELL_SECOND, half, leg).wait_recv()
        x = jnp.concatenate(
            [told_all[half, :, h].reshape(n * 2 * n, 128) for h in range(HALF // 2)], axis=1
        )
        w = jnp.concatenate(
            [
                w_buf[side, half * (HALF // 2) : (half + 1) * (HALF // 2)].reshape(depth, 128)
                for side in range(2)
            ],
            axis=1,
        )
        acc = jnp.dot(x, w, preferred_element_type=f32).reshape(n, 2, n, 256)
        mixed.append(acc[:, 0, :, :128] + acc[:, 1, :, 128:])
    turn[...] = mixed[1].reshape(requests, 128)
    other = jnp.concatenate([turn[pl.ds(i, n, stride=n), :] for i in range(n)], axis=0)
    layer = res_buf[0].astype(f32) + (mixed[0].reshape(requests, 128) + other)
    line[...] = layer.astype(bf16)

    hand = pltpu.make_async_remote_copy(
        src_ref=line,
        dst_ref=landed,
        send_sem=pass_sem.at[0],
        recv_sem=pass_sem.at[1],
        device_id={"segment": following},
        device_id_type=MESH,
    )
    hand.start()

    for half in range(2):
        for stage in (asked, parted, all_merged, all_told):
            stage(half).wait_send()
        for ring in (ASK_SECOND, TELL_SECOND):
            for leg in range(len(LEGS)):
                leave(ring, half, leg).wait_send()
    hand.wait()
    out_ref[...] = landed[...]


def local(
    n_seg,
    n,
    queries,
    new_key,
    new_value,
    key_pool,
    value_pool,
    lengths,
    block_device,
    block_slot,
    residual,
    out_weight,
):
    f32, bf16 = jnp.float32, jnp.bfloat16
    slots = key_pool.shape[1]
    tokens = slots * BLK
    requests = n * n
    whole = pl.BlockSpec(memory_space=pltpu.VMEM)
    outside = pl.BlockSpec(memory_space=pltpu.HBM)
    blocks = block_device.shape[2]
    out = pl.pallas_call(
        functools.partial(kernel, n_seg, n),
        out_shape=jax.ShapeDtypeStruct((requests, 128), bf16),
        in_specs=[outside] * 10,
        out_specs=whole,
        scratch_shapes=[
            pltpu.VMEM((1, 1, HEADS * HEAD_DIM), bf16),
            pltpu.VMEM((1, 1, KV_HEADS * HEAD_DIM), bf16),
            pltpu.VMEM((1, 1, KV_HEADS * HEAD_DIM), bf16),
            pltpu.VMEM((1, requests), jnp.int32),
            pltpu.VMEM((1, blocks, requests), jnp.int32),
            pltpu.VMEM((1, blocks, requests), jnp.int32),
            pltpu.VMEM((1, requests, 128), bf16),
            pltpu.VMEM((HEADS, 128), f32),
            pltpu.VMEM((2, 2, PAIR, 128), bf16),
            pltpu.VMEM((slots, BLK, KV_HEADS * HEAD_DIM), bf16),
            pltpu.VMEM((slots, BLK, KV_HEADS * HEAD_DIM), bf16),
            pltpu.VMEM((2, HEADS // 2, HEAD_DIM, 128), bf16),
            pltpu.VMEM((4, 256, tokens), bf16),
            pltpu.VMEM((requests, PAIR // 2, tokens), f32),
            pltpu.VMEM((2, n, 2, n, PAIR, 128), bf16),
            pltpu.VMEM((2, n, n * HALF + PAIR, 128), bf16),
            pltpu.VMEM((2, n, n * HALF + PAIR, 128), bf16),
            pltpu.VMEM((2, n, HALF + PAIR, 128), bf16),
            pltpu.VMEM((2, n, HALF + PAIR, 128), bf16),
            pltpu.VMEM((2, HALF, 128), bf16),
            pltpu.VMEM((2, n, HALF, 128), bf16),
            pltpu.VMEM((2, n * HALF, 128), f32),
            pltpu.VMEM((2, n, HALF // 2, 2 * n, 128), bf16),
            pltpu.VMEM((requests, 128), f32),
            pltpu.VMEM((requests, 128), bf16),
            pltpu.VMEM((requests, 128), bf16),
            pltpu.SemaphoreType.DMA((4, 2)),
            pltpu.SemaphoreType.DMA((4, 2)),
            pltpu.SemaphoreType.DMA((2, 2 * len(LEGS))),
            pltpu.SemaphoreType.DMA((2, 2 * len(LEGS))),
            pltpu.SemaphoreType.DMA((11,)),
            pltpu.SemaphoreType.DMA((2,)),
        ],
        compiler_params=pltpu.CompilerParams(
            collective_id=0, has_side_effects=True, vmem_limit_bytes=60 * 1024 * 1024
        ),
        name="decode_layer",
    )(
        queries,
        new_key,
        new_value,
        lengths,
        jnp.swapaxes(block_device, 1, 2),
        jnp.swapaxes(block_slot, 1, 2),
        residual,
        key_pool[0],
        value_pool[0],
        out_weight[0].reshape(HEADS // 2, 2, HEAD_DIM, 128),
    )
    return out[None]


def solution(mesh):
    placed = (
        P("segment", "kv", None),
        P("segment", "kv", None),
        P("segment", "kv", None),
        P("segment", "kv", None, None),
        P("segment", "kv", None, None),
        P("segment", None),
        P("segment", None, None),
        P("segment", None, None),
        P("segment", None, "kv"),
        P("segment", None, "kv"),
    )
    n_seg = mesh.shape["segment"]
    n = next(i for i in range(1, 64) if i * i == mesh.shape["kv"])
    return jax.shard_map(
        functools.partial(local, n_seg, n),
        mesh=mesh,
        in_specs=placed,
        out_specs=P("segment", None, "kv"),
        check_vma=False,
    )
```

```python
import functools

import jax
import jax.numpy as jnp
from jax import lax
from jax.experimental import pallas as pl
from jax.experimental.pallas import tpu as pltpu
from jax.sharding import PartitionSpec as P

KV_HEADS = 8
HEAD_DIM = 128
HEADS = 64
HALF = HEADS // 2
PAIR = 16
BLK = 16
MESH = pl.DeviceIdType.MESH
EMPTY = -1e30
FLOOR = -1e29
SCALE = HEAD_DIM ** (-0.5)
LOG2_E = 1.4426950408889634

ASK_FIRST, PART, MERGED, TELL_FIRST = range(4)
ASK_SECOND, TELL_SECOND = range(2)

LEGS = (
    (0, None, 3, -3),
    (0, None, -3, 3),
    (0, None, 1, -1),
    (0, None, -1, 1),
    (-3, None, -1, -2),
    (3, None, 1, 2),
    (-3, 0, 1, -4),
    (3, 1, -1, 4),
)


def offsets(n):
    near = []
    for step in range(1, n // 2 + 1):
        near.append(step)
        if step != n - step:
            near.append(n - step)
    return near


def heads_in_row(raw, rows):
    flat = raw[0].astype(jnp.float32)
    for h in range(rows.shape[0]):
        rows[h : h + 1, :] = flat[:, h * HEAD_DIM : (h + 1) * HEAD_DIM]


def kernel(
    n_seg,
    n,
    q_hbm,
    nk_hbm,
    nv_hbm,
    len_hbm,
    dev_hbm,
    slot_hbm,
    res_hbm,
    k_hbm,
    v_hbm,
    w_hbm,
    out_ref,
    q_raw,
    nk_raw,
    nv_raw,
    len_buf,
    dev_buf,
    slot_buf,
    res_buf,
    rows64,
    q_ref,
    k_buf,
    v_buf,
    w_buf,
    kt_buf,
    bias_buf,
    q_all,
    part,
    got,
    merged,
    last,
    attn,
    told,
    rows32,
    told_all,
    turn,
    line,
    landed,
    send_sem,
    recv_sem,
    leg_send,
    leg_recv,
    relay,
    relay_send,
    relay_recv,
    load_sem,
    pass_sem,
):
    f32, bf16 = jnp.float32, jnp.bfloat16
    seg = lax.axis_index("segment")
    me = lax.axis_index("kv")
    y, z = lax.div(me, n), lax.rem(me, n)
    first, second = (z, y), (y, z)
    slots = k_buf.shape[0]
    tokens = slots * BLK
    rows = n * PAIR

    def at_first(half, i):
        return y * n + i if half == 0 else i * n + z

    def at_second(half, i):
        return i * n + z if half == 0 else y * n + i

    def peer(base, off):
        return lax.rem(base + off, n)

    def copy(stage, half, src, dst, device):
        return pltpu.make_async_remote_copy(
            src_ref=src,
            dst_ref=dst,
            send_sem=send_sem.at[stage, half],
            recv_sem=recv_sem.at[stage, half],
            device_id={"kv": device},
            device_id_type=MESH,
        )

    def neighbours(half):
        return at_first(half, peer(first[half], 1)), at_second(half, peer(second[half], 1))

    following, before = lax.rem(seg + 1, n_seg), lax.rem(seg + n_seg - 1, n_seg)

    barrier = pltpu.get_barrier_semaphore()
    for off in offsets(n):
        for half in range(2):
            pl.semaphore_signal(
                barrier,
                inc=1,
                device_id={"kv": at_first(half, peer(first[half], off))},
                device_id_type=MESH,
            )
    for other in (following, before):
        pl.semaphore_signal(barrier, inc=1, device_id={"segment": other}, device_id_type=MESH)

    loads = [
        pltpu.make_async_copy(src, dst, load_sem.at[i])
        for i, (src, dst) in enumerate(
            (
                (q_hbm, q_raw),
                (len_hbm, len_buf),
                (dev_hbm, dev_buf),
                (slot_hbm, slot_buf),
                (k_hbm, k_buf),
                (v_hbm, v_buf),
                (nk_hbm, nk_raw),
                (nv_hbm, nv_raw),
                (res_hbm, res_buf),
                (w_hbm.at[:, 0], w_buf.at[0]),
                (w_hbm.at[:, 1], w_buf.at[1]),
            )
        )
    ]
    for load in loads:
        load.start()

    loads[0].wait()
    heads_in_row(q_raw, rows64)
    for half in range(2):
        for p in range(2):
            start = half * HALF + p * PAIR
            q_ref[half, p] = rows64[start : start + PAIR, :].astype(bf16)
            q_all[half, second[half], p, first[half]] = q_ref[half, p]

    pl.semaphore_wait(barrier, 2 * (n - 1) + 2)

    def ask_first(half, i):
        mine = first[half]
        return copy(
            ASK_FIRST, half, q_ref.at[half], q_all.at[half, second[half], :, mine], at_first(half, i)
        )

    def asked(half):
        every = q_all.at[half, second[half], :, pl.ds(0, n - 1)]
        return copy(ASK_FIRST, half, every, every, neighbours(half)[0])

    def piece_of(ring, half, block, piece):
        if piece is None:
            return (q_all if ring == ASK_SECOND else told_all).at[half, block]
        if ring == ASK_SECOND:
            return q_all.at[half, block, piece]
        rows_of = HALF // 4
        return told_all.at[half, block, pl.ds(piece * rows_of, rows_of)]

    def leg_copy(ring, half, leg, block):
        ref = piece_of(ring, half, peer(second[half], n + block), LEGS[leg][1])
        return pltpu.make_async_remote_copy(
            src_ref=ref,
            dst_ref=ref,
            send_sem=leg_send.at[ring, half * len(LEGS) + leg],
            recv_sem=leg_recv.at[ring, half * len(LEGS) + leg],
            device_id={"kv": at_second(half, peer(second[half], n + LEGS[leg][2]))},
            device_id_type=MESH,
        )

    def leave(ring, half, leg):
        return leg_copy(ring, half, leg, LEGS[leg][0])

    def arrive(ring, half, leg):
        return leg_copy(ring, half, leg, LEGS[leg][3])

    def begin(ring, half):
        for leg in range(4):
            leave(ring, half, leg).start()

    def forward(ring, half):
        for way in range(2):
            arrive(ring, half, way).wait_recv()
            leave(ring, half, 4 + way).start()
        for way in range(2):
            leave(ring, half, 6 + way).start()

    for off in offsets(n):
        for half in range(2):
            ask_first(half, peer(first[half], off)).start()

    requests = n * n
    for load in loads[1:4]:
        load.wait()
    blocks = dev_buf.shape[1]
    holder = jnp.where(dev_buf[0] == me, slot_buf[0], -1)
    numbers = lax.broadcasted_iota(jnp.int32, (blocks, requests), 0)
    live = jnp.clip(len_buf[...] - numbers * BLK, 0, BLK).astype(f32)
    slot_of = lax.broadcasted_iota(jnp.int32, (slots, requests), 0)
    count = jnp.zeros((slots, requests), f32)
    for b in range(blocks):
        count = count + jnp.where(slot_of == holder[b : b + 1, :], live[b : b + 1, :], 0.0)
    spread = (
        lax.div(lax.broadcasted_iota(jnp.int32, (slots, tokens), 1), BLK)
        == lax.broadcasted_iota(jnp.int32, (slots, tokens), 0)
    ).astype(bf16)
    limit = lax.dot_general(
        count.astype(bf16), spread, (((0,), (0,)), ((), ())), preferred_element_type=f32
    )
    place = lax.rem(lax.broadcasted_iota(jnp.int32, (requests, tokens), 1), BLK).astype(f32)
    mask = jnp.where(place < limit, 0.0, EMPTY)
    for r in range(requests):
        bias_buf[r] = jnp.broadcast_to(mask[r : r + 1, :], (PAIR // 2, tokens))

    for half in range(2):
        asked(half).wait_recv()
        begin(ASK_SECOND, half)
    loads[4].wait()
    for pair in range(4):
        kt_buf[pair] = k_buf[:, :, pair * 256 : (pair + 1) * 256].reshape(tokens, 256).T
    loads[5].wait()

    def tiles(count):
        inside = lax.rem(lax.broadcasted_iota(jnp.int32, (count * PAIR, 128), 0), PAIR)
        return inside < PAIR // 2

    lane = lax.broadcasted_iota(jnp.int32, (PAIR // 2, 128), 1)
    used = 4 * n

    def three(stat):
        high = stat.astype(bf16).astype(f32)
        rest = stat - high
        middle = rest.astype(bf16).astype(f32)
        low = rest - middle
        return jnp.where(
            lane < used,
            high,
            jnp.where(lane < 2 * used, pltpu.roll(middle, used, 1), pltpu.roll(low, 2 * used, 1)),
        )

    def pack(above, below):
        return jnp.concatenate([three(above), three(below)], axis=0).astype(bf16)

    def unpack(tile):
        sides = tile.astype(f32)
        sides = (sides + pltpu.roll(sides, 128 - used, 1)) + pltpu.roll(sides, 128 - 2 * used, 1)
        return sides[: PAIR // 2], sides[PAIR // 2 :]

    def attend(half, those):
        count = len(those) * n
        upper = tiles(count)
        keep_upper = upper.astype(f32).astype(bf16)
        keep_lower = (1.0 - upper.astype(f32)).astype(bf16)
        bias = jnp.concatenate(
            [
                bias_buf[pl.ds(b * n, n)]
                if half == 0
                else jnp.stack([bias_buf[f * n + b] for f in range(n)], axis=0)
                for b in those
            ],
            axis=0,
        )
        tops = [jnp.full((PAIR // 2, 128), FLOOR, f32) for _ in those]
        totals = [jnp.zeros((PAIR // 2, 128), f32) for _ in those]
        for p in range(2):
            pair = half * 2 + p
            x = jnp.concatenate([q_all[half, b, p].reshape(rows, 128) for b in those], axis=0)
            x = jnp.concatenate([x * keep_upper, x * keep_lower], axis=1)
            score = jnp.dot(x, kt_buf[pair], preferred_element_type=f32)
            score = score.reshape(count, 2, PAIR // 2, tokens) + bias[:, None]
            score = score.reshape(count * PAIR, tokens)
            top = jnp.maximum(jnp.max(score, axis=1, keepdims=True), FLOOR)
            prob = jnp.exp2((score - top) * (SCALE * LOG2_E))
            total = jnp.sum(prob, axis=1, keepdims=True)
            value = v_buf[:, :, pair * 256 : (pair + 1) * 256].reshape(tokens, 256)
            acc = jnp.dot(prob.astype(bf16), value, preferred_element_type=f32)
            acc = jnp.where(upper, acc[:, :128], acc[:, 128:])
            acc = acc.astype(bf16).reshape(count, PAIR, 128)
            top = top.reshape(count, 2, PAIR // 2, 1)
            total = total.reshape(count, 2, PAIR // 2, 1)
            for k, b in enumerate(those):
                for r in range(n):
                    part[half, b, r * HALF + p * PAIR : r * HALF + (p + 1) * PAIR, :] = acc[k * n + r]
                    for side in range(2):
                        here = lane == (side * 2 + p) * n + r
                        tops[k] = jnp.where(here, top[k * n + r, side], tops[k])
                        totals[k] = jnp.where(here, total[k * n + r, side], totals[k])
        for k, b in enumerate(those):
            part[half, b, n * HALF :, :] = pack(tops[k], totals[k])

    def send_part(half, i):
        return copy(PART, half, part.at[half, i], got.at[half, second[half]], at_second(half, i))

    cut = n * HALF // 2
    spans = (pl.ds(0, cut), pl.ds(cut, n * HALF + PAIR - cut))

    def relay_in(half, way):
        return pltpu.make_async_remote_copy(
            src_ref=part.at[half, peer(second[half], n // 2), spans[way]],
            dst_ref=relay.at[half, spans[way]],
            send_sem=relay_send.at[half, way],
            recv_sem=relay_recv.at[half, way],
            device_id={"kv": at_second(half, peer(second[half], 1 if way == 0 else n - 1))},
            device_id_type=MESH,
        )

    def relay_out(half, way):
        source = peer(second[half], n - 1 if way == 0 else 1)
        return pltpu.make_async_remote_copy(
            src_ref=relay.at[half, spans[way]],
            dst_ref=got.at[half, source, spans[way]],
            send_sem=relay_send.at[half, 2 + way],
            recv_sem=relay_recv.at[half, 2 + way],
            device_id={"kv": at_second(half, peer(second[half], 3 if way == 0 else n - 3))},
            device_id_type=MESH,
        )

    def parted(half):
        every = got.at[half, pl.ds(0, n - 2)]
        return copy(PART, half, every, every, neighbours(half)[1])

    for half in range(2):
        attend(half, [second[half]])
        got[half, second[half]] = part[half, second[half]]

    for half in range(2):
        forward(ASK_SECOND, half)

    def one_step(t, carry):
        @pl.when(t == 1)
        def _():
            for half in range(2):
                for leg in (2, 3):
                    arrive(ASK_SECOND, half, leg).wait_recv()

        @pl.when(t == 2)
        def _():
            for half in range(2):
                for leg in (6, 7):
                    arrive(ASK_SECOND, half, leg).wait_recv()
                across = peer(second[half], n // 2)
                attend(half, [across])
                for way in range(2):
                    relay_in(half, way).start()
            for half in range(2):
                for leg in (4, 5):
                    arrive(ASK_SECOND, half, leg).wait_recv()

        away = lax.rem(t + 2, 3) + 1
        those = [
            [peer(second[half], n - away), peer(second[half], away)] for half in range(2)
        ]
        for half in range(2):
            attend(half, those[half])
        for half in range(2):
            for b in those[half]:
                send_part(half, b).start()
        return carry

    lax.fori_loop(0, 3, one_step, 0)
    for half in range(2):
        for way in range(2):
            relay_in(half, way).wait_recv()
            relay_out(half, way).start()

    def send_merged(half, i):
        return copy(MERGED, half, merged.at[half, i], last.at[half, first[half]], at_first(half, i))

    def all_merged(half):
        every = last.at[half, pl.ds(0, n - 1)]
        return copy(MERGED, half, every, every, neighbours(half)[0])

    for half in range(2):
        parted(half).wait_recv()
        for way in range(2):
            relay_out(half, way).wait_recv()
        sides = [unpack(got[half, i, n * HALF :, :]) for i in range(n)]
        tops = jnp.stack([above for above, _ in sides], axis=0)
        totals = jnp.stack([below for _, below in sides], axis=0)
        top = jnp.max(tops, axis=0)
        weight = jnp.exp((tops - top[None]) * SCALE)
        total = jnp.sum(weight * totals, axis=0)
        some = jnp.maximum(total, 0.5)
        weight = weight / some[None]
        lse = jnp.where(total > 0.0, top * SCALE + jnp.log(some), EMPTY)
        tail = pack(lse, jnp.zeros_like(lse))
        for r in range(n):
            for p in range(2):
                scale = jnp.concatenate(
                    [
                        weight[:, :, (side * 2 + p) * n + r : (side * 2 + p) * n + r + 1]
                        for side in range(2)
                    ],
                    axis=1,
                )
                start = r * HALF + p * PAIR
                piece = got[half, :, start : start + PAIR, :].astype(f32)
                merged[half, r, p * PAIR : (p + 1) * PAIR, :] = jnp.sum(
                    piece * scale, axis=0
                ).astype(bf16)
            merged[half, r, HALF:, :] = tail
        for off in offsets(n):
            send_merged(half, peer(first[half], off)).start()
        last[half, first[half]] = merged[half, first[half]]

    def tell_first(half, i):
        return copy(TELL_FIRST, half, attn.at[half], told.at[half, first[half]], at_first(half, i))

    def all_told(half):
        every = told.at[half, pl.ds(0, n - 1)]
        return copy(TELL_FIRST, half, every, every, neighbours(half)[0])

    for load in loads[6:9]:
        load.wait()
    heads_in_row(nk_raw, rows64.at[pl.ds(0, KV_HEADS)])
    new_keys = rows64[:KV_HEADS, :]
    heads_in_row(nv_raw, rows64.at[pl.ds(KV_HEADS, KV_HEADS)])
    new_values = rows64[KV_HEADS : 2 * KV_HEADS, :]
    for half in range(2):
        kv_half = slice(half * 4, half * 4 + 4)
        query = q_ref[half].astype(f32).reshape(4, 8, 128)
        own = jnp.sum(query * new_keys[kv_half][:, None, :], axis=2, keepdims=True) * SCALE
        own = own.reshape(HALF, 1)
        own_value = jnp.broadcast_to(new_values[kv_half][:, None, :], (4, 8, 128)).reshape(HALF, 128)
        all_merged(half).wait_recv()
        lses = []
        for i in range(n):
            stat = unpack(last[half, i, HALF:, :])[0]
            lses.append(
                jnp.concatenate(
                    [
                        jnp.sum(
                            jnp.where(lane == (side * 2 + p) * n + first[half], stat, 0.0),
                            axis=1,
                            keepdims=True,
                        )
                        for p in range(2)
                        for side in range(2)
                    ],
                    axis=0,
                )
            )
        top = own
        for lse in lses:
            top = jnp.maximum(top, lse)
        weight = jnp.exp(own - top)
        total = weight
        acc = weight * own_value
        for i in range(n):
            weight = jnp.exp(lses[i] - top)
            total = total + weight
            acc = acc + weight * last[half, i, :HALF, :].astype(f32)
        attn[half] = (acc / total).astype(bf16)
        for off in offsets(n):
            tell_first(half, peer(first[half], off)).start()
        told[half, first[half]] = attn[half]

    for half in range(2):
        all_told(half).wait_recv()
        rows32[half] = told[half].astype(f32).reshape(n * HALF, 128)
        for h in range(HALF // 2):
            tile = [rows32[half, pl.ds(2 * h + s, n, stride=HALF), :] for s in range(2)]
            told_all[half, second[half], h] = jnp.concatenate(tile, axis=0).astype(bf16)
        begin(TELL_SECOND, half)

    for half in range(2):
        forward(TELL_SECOND, half)
    loads[9].wait()
    loads[10].wait()
    depth = HALF // 2 * HEAD_DIM
    mixed = []
    for half in range(2):
        for leg in range(2, len(LEGS)):
            arrive(TELL_SECOND, half, leg).wait_recv()
        x = jnp.concatenate(
            [told_all[half, :, h].reshape(n * 2 * n, 128) for h in range(HALF // 2)], axis=1
        )
        w = jnp.concatenate(
            [
                w_buf[side, half * (HALF // 2) : (half + 1) * (HALF // 2)].reshape(depth, 128)
                for side in range(2)
            ],
            axis=1,
        )
        acc = jnp.dot(x, w, preferred_element_type=f32).reshape(n, 2, n, 256)
        mixed.append(acc[:, 0, :, :128] + acc[:, 1, :, 128:])
    turn[...] = mixed[1].reshape(requests, 128)
    other = jnp.concatenate([turn[pl.ds(i, n, stride=n), :] for i in range(n)], axis=0)
    layer = res_buf[0].astype(f32) + (mixed[0].reshape(requests, 128) + other)
    line[...] = layer.astype(bf16)

    hand = pltpu.make_async_remote_copy(
        src_ref=line,
        dst_ref=landed,
        send_sem=pass_sem.at[0],
        recv_sem=pass_sem.at[1],
        device_id={"segment": following},
        device_id_type=MESH,
    )
    hand.start()

    for half in range(2):
        for stage in (asked, parted, all_merged, all_told):
            stage(half).wait_send()
        for way in range(2):
            relay_in(half, way).wait_send()
            relay_out(half, way).wait_send()
        for ring in (ASK_SECOND, TELL_SECOND):
            for leg in range(len(LEGS)):
                leave(ring, half, leg).wait_send()
    hand.wait()
    out_ref[...] = landed[...]


def local(
    n_seg,
    n,
    queries,
    new_key,
    new_value,
    key_pool,
    value_pool,
    lengths,
    block_device,
    block_slot,
    residual,
    out_weight,
):
    f32, bf16 = jnp.float32, jnp.bfloat16
    slots = key_pool.shape[1]
    tokens = slots * BLK
    requests = n * n
    whole = pl.BlockSpec(memory_space=pltpu.VMEM)
    outside = pl.BlockSpec(memory_space=pltpu.HBM)
    blocks = block_device.shape[2]
    out = pl.pallas_call(
        functools.partial(kernel, n_seg, n),
        out_shape=jax.ShapeDtypeStruct((requests, 128), bf16),
        in_specs=[outside] * 10,
        out_specs=whole,
        scratch_shapes=[
            pltpu.VMEM((1, 1, HEADS * HEAD_DIM), bf16),
            pltpu.VMEM((1, 1, KV_HEADS * HEAD_DIM), bf16),
            pltpu.VMEM((1, 1, KV_HEADS * HEAD_DIM), bf16),
            pltpu.VMEM((1, requests), jnp.int32),
            pltpu.VMEM((1, blocks, requests), jnp.int32),
            pltpu.VMEM((1, blocks, requests), jnp.int32),
            pltpu.VMEM((1, requests, 128), bf16),
            pltpu.VMEM((HEADS, 128), f32),
            pltpu.VMEM((2, 2, PAIR, 128), bf16),
            pltpu.VMEM((slots, BLK, KV_HEADS * HEAD_DIM), bf16),
            pltpu.VMEM((slots, BLK, KV_HEADS * HEAD_DIM), bf16),
            pltpu.VMEM((2, HEADS // 2, HEAD_DIM, 128), bf16),
            pltpu.VMEM((4, 256, tokens), bf16),
            pltpu.VMEM((requests, PAIR // 2, tokens), f32),
            pltpu.VMEM((2, n, 2, n, PAIR, 128), bf16),
            pltpu.VMEM((2, n, n * HALF + PAIR, 128), bf16),
            pltpu.VMEM((2, n, n * HALF + PAIR, 128), bf16),
            pltpu.VMEM((2, n, HALF + PAIR, 128), bf16),
            pltpu.VMEM((2, n, HALF + PAIR, 128), bf16),
            pltpu.VMEM((2, HALF, 128), bf16),
            pltpu.VMEM((2, n, HALF, 128), bf16),
            pltpu.VMEM((2, n * HALF, 128), f32),
            pltpu.VMEM((2, n, HALF // 2, 2 * n, 128), bf16),
            pltpu.VMEM((requests, 128), f32),
            pltpu.VMEM((requests, 128), bf16),
            pltpu.VMEM((requests, 128), bf16),
            pltpu.SemaphoreType.DMA((4, 2)),
            pltpu.SemaphoreType.DMA((4, 2)),
            pltpu.SemaphoreType.DMA((2, 2 * len(LEGS))),
            pltpu.SemaphoreType.DMA((2, 2 * len(LEGS))),
            pltpu.VMEM((2, n * HALF + PAIR, 128), bf16),
            pltpu.SemaphoreType.DMA((2, 4)),
            pltpu.SemaphoreType.DMA((2, 4)),
            pltpu.SemaphoreType.DMA((11,)),
            pltpu.SemaphoreType.DMA((2,)),
        ],
        compiler_params=pltpu.CompilerParams(
            collective_id=0, has_side_effects=True, vmem_limit_bytes=60 * 1024 * 1024
        ),
        name="decode_layer",
    )(
        queries,
        new_key,
        new_value,
        lengths,
        jnp.swapaxes(block_device, 1, 2),
        jnp.swapaxes(block_slot, 1, 2),
        residual,
        key_pool[0],
        value_pool[0],
        out_weight[0].reshape(HEADS // 2, 2, HEAD_DIM, 128),
    )
    return out[None]


def solution(mesh):
    placed = (
        P("segment", "kv", None),
        P("segment", "kv", None),
        P("segment", "kv", None),
        P("segment", "kv", None, None),
        P("segment", "kv", None, None),
        P("segment", None),
        P("segment", None, None),
        P("segment", None, None),
        P("segment", None, "kv"),
        P("segment", None, "kv"),
    )
    n_seg = mesh.shape["segment"]
    n = next(i for i in range(1, 64) if i * i == mesh.shape["kv"])
    return jax.shard_map(
        functools.partial(local, n_seg, n),
        mesh=mesh,
        in_specs=placed,
        out_specs=P("segment", None, "kv"),
        check_vma=False,
    )
```

```python
import functools

import jax
import jax.numpy as jnp
from jax import lax
from jax.experimental import pallas as pl
from jax.experimental.pallas import tpu as pltpu
from jax.sharding import PartitionSpec as P

KV_HEADS = 8
HEAD_DIM = 128
HEADS = 64
HALF = HEADS // 2
PAIR = 16
BLK = 16
MESH = pl.DeviceIdType.MESH
EMPTY = -1e30
FLOOR = -1e29
SCALE = HEAD_DIM ** (-0.5)
LOG2_E = 1.4426950408889634

ASK_FIRST, PART, MERGED, TELL_FIRST = range(4)
ASK_SECOND, TELL_SECOND = range(2)

LEGS = (
    (0, 0, 3, -3),
    (0, 0, -3, 3),
    (0, 1, 3, -3),
    (0, 1, -3, 3),
    (0, None, 1, -1),
    (0, None, -1, 1),
    (-3, 0, -1, -2),
    (3, 0, 1, 2),
    (-3, 1, -1, -2),
    (3, 1, 1, 2),
    (-3, 0, 1, -4),
    (3, 1, -1, 4),
)
FAR, NEAR, ONWARD, ACROSS = (0, 1, 2, 3), (4, 5), (6, 7, 8, 9), (10, 11)


def offsets(n):
    near = []
    for step in range(1, n // 2 + 1):
        near.append(step)
        if step != n - step:
            near.append(n - step)
    return near


def heads_in_row(raw, rows):
    flat = raw[0].astype(jnp.float32)
    for h in range(rows.shape[0]):
        rows[h : h + 1, :] = flat[:, h * HEAD_DIM : (h + 1) * HEAD_DIM]


def kernel(
    n_seg,
    n,
    q_hbm,
    nk_hbm,
    nv_hbm,
    len_hbm,
    dev_hbm,
    slot_hbm,
    res_hbm,
    k_hbm,
    v_hbm,
    w_hbm,
    out_ref,
    q_raw,
    nk_raw,
    nv_raw,
    len_buf,
    dev_buf,
    slot_buf,
    res_buf,
    rows64,
    q_ref,
    k_buf,
    v_buf,
    w_buf,
    kt_buf,
    bias_buf,
    q_all,
    part,
    got,
    merged,
    last,
    attn,
    told,
    rows32,
    told_all,
    turn,
    line,
    landed,
    send_sem,
    recv_sem,
    leg_send,
    leg_recv,
    load_sem,
    pass_sem,
):
    f32, bf16 = jnp.float32, jnp.bfloat16
    seg = lax.axis_index("segment")
    me = lax.axis_index("kv")
    y, z = lax.div(me, n), lax.rem(me, n)
    first, second = (z, y), (y, z)
    slots = k_buf.shape[0]
    tokens = slots * BLK
    rows = n * PAIR

    def at_first(half, i):
        return y * n + i if half == 0 else i * n + z

    def at_second(half, i):
        return i * n + z if half == 0 else y * n + i

    def peer(base, off):
        return lax.rem(base + off, n)

    def copy(stage, half, src, dst, device):
        return pltpu.make_async_remote_copy(
            src_ref=src,
            dst_ref=dst,
            send_sem=send_sem.at[stage, half],
            recv_sem=recv_sem.at[stage, half],
            device_id={"kv": device},
            device_id_type=MESH,
        )

    def neighbours(half):
        return at_first(half, peer(first[half], 1)), at_second(half, peer(second[half], 1))

    following, before = lax.rem(seg + 1, n_seg), lax.rem(seg + n_seg - 1, n_seg)

    barrier = pltpu.get_barrier_semaphore()
    for off in offsets(n):
        for half in range(2):
            pl.semaphore_signal(
                barrier,
                inc=1,
                device_id={"kv": at_first(half, peer(first[half], off))},
                device_id_type=MESH,
            )
    for other in (following, before):
        pl.semaphore_signal(barrier, inc=1, device_id={"segment": other}, device_id_type=MESH)

    loads = [
        pltpu.make_async_copy(src, dst, load_sem.at[i])
        for i, (src, dst) in enumerate(
            (
                (q_hbm, q_raw),
                (len_hbm, len_buf),
                (dev_hbm, dev_buf),
                (slot_hbm, slot_buf),
                (k_hbm, k_buf),
                (v_hbm, v_buf),
                (nk_hbm, nk_raw),
                (nv_hbm, nv_raw),
                (res_hbm, res_buf),
                (w_hbm.at[:, 0], w_buf.at[0]),
                (w_hbm.at[:, 1], w_buf.at[1]),
            )
        )
    ]
    for load in loads:
        load.start()

    loads[0].wait()
    heads_in_row(q_raw, rows64)
    for half in range(2):
        for p in range(2):
            start = half * HALF + p * PAIR
            q_ref[half, p] = rows64[start : start + PAIR, :].astype(bf16)
            q_all[half, second[half], p, first[half]] = q_ref[half, p]

    pl.semaphore_wait(barrier, 2 * (n - 1) + 2)

    def ask_first(half, i):
        mine = first[half]
        return copy(
            ASK_FIRST, half, q_ref.at[half], q_all.at[half, second[half], :, mine], at_first(half, i)
        )

    def asked(half):
        every = q_all.at[half, second[half], :, pl.ds(0, n - 1)]
        return copy(ASK_FIRST, half, every, every, neighbours(half)[0])

    def piece_of(ring, half, block, piece):
        if piece is None:
            return (q_all if ring == ASK_SECOND else told_all).at[half, block]
        if ring == ASK_SECOND:
            return q_all.at[half, block, piece]
        rows_of = HALF // 4
        return told_all.at[half, block, pl.ds(piece * rows_of, rows_of)]

    def leg_copy(ring, half, leg, block):
        ref = piece_of(ring, half, peer(second[half], n + block), LEGS[leg][1])
        return pltpu.make_async_remote_copy(
            src_ref=ref,
            dst_ref=ref,
            send_sem=leg_send.at[ring, half * len(LEGS) + leg],
            recv_sem=leg_recv.at[ring, half * len(LEGS) + leg],
            device_id={"kv": at_second(half, peer(second[half], n + LEGS[leg][2]))},
            device_id_type=MESH,
        )

    def leave(ring, half, leg):
        return leg_copy(ring, half, leg, LEGS[leg][0])

    def arrive(ring, half, leg):
        return leg_copy(ring, half, leg, LEGS[leg][3])

    def begin(ring, half):
        for leg in FAR + NEAR:
            leave(ring, half, leg).start()

    def forward(ring):
        for piece in range(2):
            for half in range(2):
                for way in range(2):
                    leg = piece * 2 + way
                    arrive(ring, half, FAR[leg]).wait_recv()
                    leave(ring, half, ONWARD[leg]).start()
                    if piece == way:
                        leave(ring, half, ACROSS[way]).start()

    for off in offsets(n):
        for half in range(2):
            ask_first(half, peer(first[half], off)).start()

    requests = n * n
    for load in loads[1:4]:
        load.wait()
    blocks = dev_buf.shape[1]
    holder = jnp.where(dev_buf[0] == me, slot_buf[0], -1)
    numbers = lax.broadcasted_iota(jnp.int32, (blocks, requests), 0)
    live = jnp.clip(len_buf[...] - numbers * BLK, 0, BLK).astype(f32)
    slot_of = lax.broadcasted_iota(jnp.int32, (slots, requests), 0)
    count = jnp.zeros((slots, requests), f32)
    for b in range(blocks):
        count = count + jnp.where(slot_of == holder[b : b + 1, :], live[b : b + 1, :], 0.0)
    spread = (
        lax.div(lax.broadcasted_iota(jnp.int32, (slots, tokens), 1), BLK)
        == lax.broadcasted_iota(jnp.int32, (slots, tokens), 0)
    ).astype(bf16)
    limit = lax.dot_general(
        count.astype(bf16), spread, (((0,), (0,)), ((), ())), preferred_element_type=f32
    )
    place = lax.rem(lax.broadcasted_iota(jnp.int32, (requests, tokens), 1), BLK).astype(f32)
    mask = jnp.where(place < limit, 0.0, EMPTY)
    for r in range(requests):
        bias_buf[r] = jnp.broadcast_to(mask[r : r + 1, :], (PAIR // 2, tokens))

    for half in range(2):
        asked(half).wait_recv()
        begin(ASK_SECOND, half)
    loads[4].wait()
    for pair in range(4):
        kt_buf[pair] = k_buf[:, :, pair * 256 : (pair + 1) * 256].reshape(tokens, 256).T
    loads[5].wait()

    def tiles(count):
        inside = lax.rem(lax.broadcasted_iota(jnp.int32, (count * PAIR, 128), 0), PAIR)
        return inside < PAIR // 2

    lane = lax.broadcasted_iota(jnp.int32, (PAIR // 2, 128), 1)
    used = 4 * n

    def three(stat):
        high = stat.astype(bf16).astype(f32)
        rest = stat - high
        middle = rest.astype(bf16).astype(f32)
        low = rest - middle
        return jnp.where(
            lane < used,
            high,
            jnp.where(lane < 2 * used, pltpu.roll(middle, used, 1), pltpu.roll(low, 2 * used, 1)),
        )

    def pack(above, below):
        return jnp.concatenate([three(above), three(below)], axis=0).astype(bf16)

    def unpack(tile):
        sides = tile.astype(f32)
        sides = (sides + pltpu.roll(sides, 128 - used, 1)) + pltpu.roll(sides, 128 - 2 * used, 1)
        return sides[: PAIR // 2], sides[PAIR // 2 :]

    def attend(half, those):
        count = len(those) * n
        upper = tiles(count)
        keep_upper = upper.astype(f32).astype(bf16)
        keep_lower = (1.0 - upper.astype(f32)).astype(bf16)
        bias = jnp.concatenate(
            [
                bias_buf[pl.ds(b * n, n)]
                if half == 0
                else jnp.stack([bias_buf[f * n + b] for f in range(n)], axis=0)
                for b in those
            ],
            axis=0,
        )
        tops = [jnp.full((PAIR // 2, 128), FLOOR, f32) for _ in those]
        totals = [jnp.zeros((PAIR // 2, 128), f32) for _ in those]
        for p in range(2):
            pair = half * 2 + p
            x = jnp.concatenate([q_all[half, b, p].reshape(rows, 128) for b in those], axis=0)
            x = jnp.concatenate([x * keep_upper, x * keep_lower], axis=1)
            score = jnp.dot(x, kt_buf[pair], preferred_element_type=f32)
            score = score.reshape(count, 2, PAIR // 2, tokens) + bias[:, None]
            score = score.reshape(count * PAIR, tokens)
            top = jnp.maximum(jnp.max(score, axis=1, keepdims=True), FLOOR)
            prob = jnp.exp2((score - top) * (SCALE * LOG2_E))
            total = jnp.sum(prob, axis=1, keepdims=True)
            value = v_buf[:, :, pair * 256 : (pair + 1) * 256].reshape(tokens, 256)
            acc = jnp.dot(prob.astype(bf16), value, preferred_element_type=f32)
            acc = jnp.where(upper, acc[:, :128], acc[:, 128:])
            acc = acc.astype(bf16).reshape(count, PAIR, 128)
            top = top.reshape(count, 2, PAIR // 2, 1)
            total = total.reshape(count, 2, PAIR // 2, 1)
            for k, b in enumerate(those):
                for r in range(n):
                    part[half, b, r * HALF + p * PAIR : r * HALF + (p + 1) * PAIR, :] = acc[k * n + r]
                    for side in range(2):
                        here = lane == (side * 2 + p) * n + r
                        tops[k] = jnp.where(here, top[k * n + r, side], tops[k])
                        totals[k] = jnp.where(here, total[k * n + r, side], totals[k])
        for k, b in enumerate(those):
            part[half, b, n * HALF :, :] = pack(tops[k], totals[k])

    def send_part(half, i):
        return copy(PART, half, part.at[half, i], got.at[half, second[half]], at_second(half, i))

    def parted(half):
        every = got.at[half, pl.ds(0, n - 1)]
        return copy(PART, half, every, every, neighbours(half)[1])

    for half in range(2):
        attend(half, [second[half]])
        got[half, second[half]] = part[half, second[half]]

    forward(ASK_SECOND)

    def one_step(t, carry):
        @pl.when(t == 1)
        def _():
            for half in range(2):
                for leg in NEAR:
                    arrive(ASK_SECOND, half, leg).wait_recv()

        @pl.when(t == 2)
        def _():
            for half in range(2):
                for leg in ONWARD:
                    arrive(ASK_SECOND, half, leg).wait_recv()

        away = lax.rem(t + 2, 3) + 1
        those = [
            [peer(second[half], n - away), peer(second[half], away)] for half in range(2)
        ]
        for half in range(2):
            attend(half, those[half])
            for b in those[half]:
                send_part(half, b).start()
        return carry

    lax.fori_loop(0, 3, one_step, 0)
    for half in range(2):
        for leg in ACROSS:
            arrive(ASK_SECOND, half, leg).wait_recv()
        across = peer(second[half], n // 2)
        attend(half, [across])
        send_part(half, across).start()

    def send_merged(half, i):
        return copy(MERGED, half, merged.at[half, i], last.at[half, first[half]], at_first(half, i))

    def all_merged(half):
        every = last.at[half, pl.ds(0, n - 1)]
        return copy(MERGED, half, every, every, neighbours(half)[0])

    for half in range(2):
        parted(half).wait_recv()
        sides = [unpack(got[half, i, n * HALF :, :]) for i in range(n)]
        tops = jnp.stack([above for above, _ in sides], axis=0)
        totals = jnp.stack([below for _, below in sides], axis=0)
        top = jnp.max(tops, axis=0)
        weight = jnp.exp((tops - top[None]) * SCALE)
        total = jnp.sum(weight * totals, axis=0)
        some = jnp.maximum(total, 0.5)
        weight = weight / some[None]
        lse = jnp.where(total > 0.0, top * SCALE + jnp.log(some), EMPTY)
        tail = pack(lse, jnp.zeros_like(lse))
        for r in range(n):
            for p in range(2):
                scale = jnp.concatenate(
                    [
                        weight[:, :, (side * 2 + p) * n + r : (side * 2 + p) * n + r + 1]
                        for side in range(2)
                    ],
                    axis=1,
                )
                start = r * HALF + p * PAIR
                piece = got[half, :, start : start + PAIR, :].astype(f32)
                merged[half, r, p * PAIR : (p + 1) * PAIR, :] = jnp.sum(
                    piece * scale, axis=0
                ).astype(bf16)
            merged[half, r, HALF:, :] = tail
        for off in offsets(n):
            send_merged(half, peer(first[half], off)).start()
        last[half, first[half]] = merged[half, first[half]]

    def tell_first(half, i):
        return copy(TELL_FIRST, half, attn.at[half], told.at[half, first[half]], at_first(half, i))

    def all_told(half):
        every = told.at[half, pl.ds(0, n - 1)]
        return copy(TELL_FIRST, half, every, every, neighbours(half)[0])

    for load in loads[6:9]:
        load.wait()
    heads_in_row(nk_raw, rows64.at[pl.ds(0, KV_HEADS)])
    new_keys = rows64[:KV_HEADS, :]
    heads_in_row(nv_raw, rows64.at[pl.ds(KV_HEADS, KV_HEADS)])
    new_values = rows64[KV_HEADS : 2 * KV_HEADS, :]
    for half in range(2):
        kv_half = slice(half * 4, half * 4 + 4)
        query = q_ref[half].astype(f32).reshape(4, 8, 128)
        own = jnp.sum(query * new_keys[kv_half][:, None, :], axis=2, keepdims=True) * SCALE
        own = own.reshape(HALF, 1)
        own_value = jnp.broadcast_to(new_values[kv_half][:, None, :], (4, 8, 128)).reshape(HALF, 128)
        all_merged(half).wait_recv()
        lses = []
        for i in range(n):
            stat = unpack(last[half, i, HALF:, :])[0]
            lses.append(
                jnp.concatenate(
                    [
                        jnp.sum(
                            jnp.where(lane == (side * 2 + p) * n + first[half], stat, 0.0),
                            axis=1,
                            keepdims=True,
                        )
                        for p in range(2)
                        for side in range(2)
                    ],
                    axis=0,
                )
            )
        top = own
        for lse in lses:
            top = jnp.maximum(top, lse)
        weight = jnp.exp(own - top)
        total = weight
        acc = weight * own_value
        for i in range(n):
            weight = jnp.exp(lses[i] - top)
            total = total + weight
            acc = acc + weight * last[half, i, :HALF, :].astype(f32)
        attn[half] = (acc / total).astype(bf16)
        for off in offsets(n):
            tell_first(half, peer(first[half], off)).start()
        told[half, first[half]] = attn[half]

    for half in range(2):
        all_told(half).wait_recv()
        rows32[half] = told[half].astype(f32).reshape(n * HALF, 128)
        for h in range(HALF // 2):
            tile = [rows32[half, pl.ds(2 * h + s, n, stride=HALF), :] for s in range(2)]
            told_all[half, second[half], h] = jnp.concatenate(tile, axis=0).astype(bf16)
        begin(TELL_SECOND, half)

    forward(TELL_SECOND)
    loads[9].wait()
    loads[10].wait()
    depth = HALF // 2 * HEAD_DIM
    mixed = []
    for half in range(2):
        for leg in NEAR + ONWARD + ACROSS:
            arrive(TELL_SECOND, half, leg).wait_recv()
        x = jnp.concatenate(
            [told_all[half, :, h].reshape(n * 2 * n, 128) for h in range(HALF // 2)], axis=1
        )
        w = jnp.concatenate(
            [
                w_buf[side, half * (HALF // 2) : (half + 1) * (HALF // 2)].reshape(depth, 128)
                for side in range(2)
            ],
            axis=1,
        )
        acc = jnp.dot(x, w, preferred_element_type=f32).reshape(n, 2, n, 256)
        mixed.append(acc[:, 0, :, :128] + acc[:, 1, :, 128:])
    turn[...] = mixed[1].reshape(requests, 128)
    other = jnp.concatenate([turn[pl.ds(i, n, stride=n), :] for i in range(n)], axis=0)
    layer = res_buf[0].astype(f32) + (mixed[0].reshape(requests, 128) + other)
    line[...] = layer.astype(bf16)

    hand = pltpu.make_async_remote_copy(
        src_ref=line,
        dst_ref=landed,
        send_sem=pass_sem.at[0],
        recv_sem=pass_sem.at[1],
        device_id={"segment": following},
        device_id_type=MESH,
    )
    hand.start()

    for half in range(2):
        for stage in (asked, parted, all_merged, all_told):
            stage(half).wait_send()
        for ring in (ASK_SECOND, TELL_SECOND):
            for leg in range(len(LEGS)):
                leave(ring, half, leg).wait_send()
    hand.wait()
    out_ref[...] = landed[...]


def local(
    n_seg,
    n,
    queries,
    new_key,
    new_value,
    key_pool,
    value_pool,
    lengths,
    block_device,
    block_slot,
    residual,
    out_weight,
):
    f32, bf16 = jnp.float32, jnp.bfloat16
    slots = key_pool.shape[1]
    tokens = slots * BLK
    requests = n * n
    whole = pl.BlockSpec(memory_space=pltpu.VMEM)
    outside = pl.BlockSpec(memory_space=pltpu.HBM)
    blocks = block_device.shape[2]
    out = pl.pallas_call(
        functools.partial(kernel, n_seg, n),
        out_shape=jax.ShapeDtypeStruct((requests, 128), bf16),
        in_specs=[outside] * 10,
        out_specs=whole,
        scratch_shapes=[
            pltpu.VMEM((1, 1, HEADS * HEAD_DIM), bf16),
            pltpu.VMEM((1, 1, KV_HEADS * HEAD_DIM), bf16),
            pltpu.VMEM((1, 1, KV_HEADS * HEAD_DIM), bf16),
            pltpu.VMEM((1, requests), jnp.int32),
            pltpu.VMEM((1, blocks, requests), jnp.int32),
            pltpu.VMEM((1, blocks, requests), jnp.int32),
            pltpu.VMEM((1, requests, 128), bf16),
            pltpu.VMEM((HEADS, 128), f32),
            pltpu.VMEM((2, 2, PAIR, 128), bf16),
            pltpu.VMEM((slots, BLK, KV_HEADS * HEAD_DIM), bf16),
            pltpu.VMEM((slots, BLK, KV_HEADS * HEAD_DIM), bf16),
            pltpu.VMEM((2, HEADS // 2, HEAD_DIM, 128), bf16),
            pltpu.VMEM((4, 256, tokens), bf16),
            pltpu.VMEM((requests, PAIR // 2, tokens), f32),
            pltpu.VMEM((2, n, 2, n, PAIR, 128), bf16),
            pltpu.VMEM((2, n, n * HALF + PAIR, 128), bf16),
            pltpu.VMEM((2, n, n * HALF + PAIR, 128), bf16),
            pltpu.VMEM((2, n, HALF + PAIR, 128), bf16),
            pltpu.VMEM((2, n, HALF + PAIR, 128), bf16),
            pltpu.VMEM((2, HALF, 128), bf16),
            pltpu.VMEM((2, n, HALF, 128), bf16),
            pltpu.VMEM((2, n * HALF, 128), f32),
            pltpu.VMEM((2, n, HALF // 2, 2 * n, 128), bf16),
            pltpu.VMEM((requests, 128), f32),
            pltpu.VMEM((requests, 128), bf16),
            pltpu.VMEM((requests, 128), bf16),
            pltpu.SemaphoreType.DMA((4, 2)),
            pltpu.SemaphoreType.DMA((4, 2)),
            pltpu.SemaphoreType.DMA((2, 2 * len(LEGS))),
            pltpu.SemaphoreType.DMA((2, 2 * len(LEGS))),
            pltpu.SemaphoreType.DMA((11,)),
            pltpu.SemaphoreType.DMA((2,)),
        ],
        compiler_params=pltpu.CompilerParams(
            collective_id=0, has_side_effects=True, vmem_limit_bytes=60 * 1024 * 1024
        ),
        name="decode_layer",
    )(
        queries,
        new_key,
        new_value,
        lengths,
        jnp.swapaxes(block_device, 1, 2),
        jnp.swapaxes(block_slot, 1, 2),
        residual,
        key_pool[0],
        value_pool[0],
        out_weight[0].reshape(HEADS // 2, 2, HEAD_DIM, 128),
    )
    return out[None]


def solution(mesh):
    placed = (
        P("segment", "kv", None),
        P("segment", "kv", None),
        P("segment", "kv", None),
        P("segment", "kv", None, None),
        P("segment", "kv", None, None),
        P("segment", None),
        P("segment", None, None),
        P("segment", None, None),
        P("segment", None, "kv"),
        P("segment", None, "kv"),
    )
    n_seg = mesh.shape["segment"]
    n = next(i for i in range(1, 64) if i * i == mesh.shape["kv"])
    return jax.shard_map(
        functools.partial(local, n_seg, n),
        mesh=mesh,
        in_specs=placed,
        out_specs=P("segment", None, "kv"),
        check_vma=False,
    )
```

```python
import functools

import jax
import jax.numpy as jnp
from jax import lax
from jax.experimental import pallas as pl
from jax.experimental.pallas import tpu as pltpu
from jax.sharding import PartitionSpec as P

KV_HEADS = 8
HEAD_DIM = 128
HEADS = 64
HALF = HEADS // 2
PAIR = 16
BLK = 16
MESH = pl.DeviceIdType.MESH
EMPTY = -1e30
FLOOR = -1e29
SCALE = HEAD_DIM ** (-0.5)
LOG2_E = 1.4426950408889634

ASK_FIRST, PART, MERGED, TELL_FIRST = range(4)
ASK_SECOND, TELL_SECOND = range(2)

LEGS = (
    (0, None, 3, -3),
    (0, None, -3, 3),
    (0, None, 1, -1),
    (0, None, -1, 1),
    (-3, None, -1, -2),
    (3, None, 1, 2),
    (-3, 0, 1, -4),
    (3, 1, -1, 4),
)


def offsets(n):
    near = []
    for step in range(1, n // 2 + 1):
        near.append(step)
        if step != n - step:
            near.append(n - step)
    return near


def heads_in_row(raw, rows):
    flat = raw[0].astype(jnp.float32)
    for h in range(rows.shape[0]):
        rows[h : h + 1, :] = flat[:, h * HEAD_DIM : (h + 1) * HEAD_DIM]


def kernel(
    n_seg,
    n,
    q_hbm,
    nk_hbm,
    nv_hbm,
    len_hbm,
    dev_hbm,
    slot_hbm,
    res_hbm,
    k_hbm,
    v_hbm,
    w_hbm,
    out_ref,
    q_raw,
    nk_raw,
    nv_raw,
    len_buf,
    dev_buf,
    slot_buf,
    res_buf,
    rows64,
    q_ref,
    k_buf,
    v_buf,
    w_buf,
    kt_buf,
    bias_buf,
    q_all,
    part,
    got,
    merged,
    last,
    attn,
    told,
    rows32,
    told_all,
    turn,
    line,
    landed,
    send_sem,
    recv_sem,
    leg_send,
    leg_recv,
    load_sem,
    pass_sem,
):
    f32, bf16 = jnp.float32, jnp.bfloat16
    seg = lax.axis_index("segment")
    me = lax.axis_index("kv")
    y, z = lax.div(me, n), lax.rem(me, n)
    first, second = (z, y), (y, z)
    slots = k_buf.shape[0]
    tokens = slots * BLK
    rows = n * PAIR

    def at_first(half, i):
        return y * n + i if half == 0 else i * n + z

    def at_second(half, i):
        return i * n + z if half == 0 else y * n + i

    def peer(base, off):
        return lax.rem(base + off, n)

    def copy(stage, half, src, dst, device):
        return pltpu.make_async_remote_copy(
            src_ref=src,
            dst_ref=dst,
            send_sem=send_sem.at[stage, half],
            recv_sem=recv_sem.at[stage, half],
            device_id={"kv": device},
            device_id_type=MESH,
        )

    def neighbours(half):
        return at_first(half, peer(first[half], 1)), at_second(half, peer(second[half], 1))

    following, before = lax.rem(seg + 1, n_seg), lax.rem(seg + n_seg - 1, n_seg)

    barrier = pltpu.get_barrier_semaphore()
    for off in offsets(n):
        for half in range(2):
            pl.semaphore_signal(
                barrier,
                inc=1,
                device_id={"kv": at_first(half, peer(first[half], off))},
                device_id_type=MESH,
            )
    for other in (following, before):
        pl.semaphore_signal(barrier, inc=1, device_id={"segment": other}, device_id_type=MESH)

    loads = [
        pltpu.make_async_copy(src, dst, load_sem.at[i])
        for i, (src, dst) in enumerate(
            (
                (q_hbm, q_raw),
                (len_hbm, len_buf),
                (dev_hbm, dev_buf),
                (slot_hbm, slot_buf),
                (k_hbm, k_buf),
                (v_hbm, v_buf),
                (nk_hbm, nk_raw),
                (nv_hbm, nv_raw),
                (res_hbm, res_buf),
                (w_hbm.at[:, 0], w_buf.at[0]),
                (w_hbm.at[:, 1], w_buf.at[1]),
            )
        )
    ]
    for load in loads:
        load.start()

    loads[0].wait()
    heads_in_row(q_raw, rows64)
    for half in range(2):
        for p in range(2):
            start = half * HALF + p * PAIR
            q_ref[half, p] = rows64[start : start + PAIR, :].astype(bf16)
            q_all[half, second[half], p, first[half]] = q_ref[half, p]

    pl.semaphore_wait(barrier, 2 * (n - 1) + 2)

    def ask_first(half, i):
        mine = first[half]
        return copy(
            ASK_FIRST, half, q_ref.at[half], q_all.at[half, second[half], :, mine], at_first(half, i)
        )

    def asked(half):
        every = q_all.at[half, second[half], :, pl.ds(0, n - 1)]
        return copy(ASK_FIRST, half, every, every, neighbours(half)[0])

    def piece_of(ring, half, block, piece):
        if piece is None:
            return (q_all if ring == ASK_SECOND else told_all).at[half, block]
        if ring == ASK_SECOND:
            return q_all.at[half, block, piece]
        rows_of = HALF // 4
        return told_all.at[half, block, pl.ds(piece * rows_of, rows_of)]

    def leg_copy(ring, half, leg, block):
        ref = piece_of(ring, half, peer(second[half], n + block), LEGS[leg][1])
        return pltpu.make_async_remote_copy(
            src_ref=ref,
            dst_ref=ref,
            send_sem=leg_send.at[ring, half * len(LEGS) + leg],
            recv_sem=leg_recv.at[ring, half * len(LEGS) + leg],
            device_id={"kv": at_second(half, peer(second[half], n + LEGS[leg][2]))},
            device_id_type=MESH,
        )

    def leave(ring, half, leg):
        return leg_copy(ring, half, leg, LEGS[leg][0])

    def arrive(ring, half, leg):
        return leg_copy(ring, half, leg, LEGS[leg][3])

    def begin(ring, half):
        for leg in range(4):
            leave(ring, half, leg).start()

    def forward(ring, half):
        for way in range(2):
            arrive(ring, half, way).wait_recv()
            leave(ring, half, 4 + way).start()
        for way in range(2):
            leave(ring, half, 6 + way).start()

    for off in offsets(n):
        for half in range(2):
            ask_first(half, peer(first[half], off)).start()

    requests = n * n
    for load in loads[1:4]:
        load.wait()
    blocks = dev_buf.shape[1]
    holder = jnp.where(dev_buf[0] == me, slot_buf[0], -1)
    numbers = lax.broadcasted_iota(jnp.int32, (blocks, requests), 0)
    live = jnp.clip(len_buf[...] - numbers * BLK, 0, BLK).astype(f32)
    slot_of = lax.broadcasted_iota(jnp.int32, (slots, requests), 0)
    count = jnp.zeros((slots, requests), f32)
    for b in range(blocks):
        count = count + jnp.where(slot_of == holder[b : b + 1, :], live[b : b + 1, :], 0.0)
    spread = (
        lax.div(lax.broadcasted_iota(jnp.int32, (slots, tokens), 1), BLK)
        == lax.broadcasted_iota(jnp.int32, (slots, tokens), 0)
    ).astype(bf16)
    limit = lax.dot_general(
        count.astype(bf16), spread, (((0,), (0,)), ((), ())), preferred_element_type=f32
    )
    place = lax.rem(lax.broadcasted_iota(jnp.int32, (requests, tokens), 1), BLK).astype(f32)
    mask = jnp.where(place < limit, 0.0, EMPTY)
    for r in range(requests):
        bias_buf[r] = jnp.broadcast_to(mask[r : r + 1, :], (PAIR // 2, tokens))

    for half in range(2):
        asked(half).wait_recv()
        begin(ASK_SECOND, half)
    loads[4].wait()
    for pair in range(4):
        kt_buf[pair] = k_buf[:, :, pair * 256 : (pair + 1) * 256].reshape(tokens, 256).T
    loads[5].wait()

    def tiles(count):
        inside = lax.rem(lax.broadcasted_iota(jnp.int32, (count * PAIR, 128), 0), PAIR)
        return inside < PAIR // 2

    lane = lax.broadcasted_iota(jnp.int32, (PAIR // 2, 128), 1)
    used = 4 * n

    def three(stat):
        high = stat.astype(bf16).astype(f32)
        rest = stat - high
        middle = rest.astype(bf16).astype(f32)
        low = rest - middle
        return jnp.where(
            lane < used,
            high,
            jnp.where(lane < 2 * used, pltpu.roll(middle, used, 1), pltpu.roll(low, 2 * used, 1)),
        )

    def pack(above, below):
        return jnp.concatenate([three(above), three(below)], axis=0).astype(bf16)

    def unpack(tile):
        sides = tile.astype(f32)
        sides = (sides + pltpu.roll(sides, 128 - used, 1)) + pltpu.roll(sides, 128 - 2 * used, 1)
        return sides[: PAIR // 2], sides[PAIR // 2 :]

    def attend(half, those):
        count = len(those) * n
        upper = tiles(count)
        keep_upper = upper.astype(f32).astype(bf16)
        keep_lower = (1.0 - upper.astype(f32)).astype(bf16)
        bias = jnp.concatenate(
            [
                bias_buf[pl.ds(b * n, n)]
                if half == 0
                else jnp.stack([bias_buf[f * n + b] for f in range(n)], axis=0)
                for b in those
            ],
            axis=0,
        )
        tops = [jnp.full((PAIR // 2, 128), FLOOR, f32) for _ in those]
        totals = [jnp.zeros((PAIR // 2, 128), f32) for _ in those]
        for p in range(2):
            pair = half * 2 + p
            x = jnp.concatenate([q_all[half, b, p].reshape(rows, 128) for b in those], axis=0)
            x = jnp.concatenate([x * keep_upper, x * keep_lower], axis=1)
            score = jnp.dot(x, kt_buf[pair], preferred_element_type=f32)
            score = score.reshape(count, 2, PAIR // 2, tokens) + bias[:, None]
            score = score.reshape(count * PAIR, tokens)
            top = jnp.maximum(jnp.max(score, axis=1, keepdims=True), FLOOR)
            prob = jnp.exp2((score - top) * (SCALE * LOG2_E))
            total = jnp.sum(prob, axis=1, keepdims=True)
            value = v_buf[:, :, pair * 256 : (pair + 1) * 256].reshape(tokens, 256)
            acc = jnp.dot(prob.astype(bf16), value, preferred_element_type=f32)
            acc = jnp.where(upper, acc[:, :128], acc[:, 128:])
            acc = acc.astype(bf16).reshape(count, PAIR, 128)
            top = top.reshape(count, 2, PAIR // 2, 1)
            total = total.reshape(count, 2, PAIR // 2, 1)
            for k, b in enumerate(those):
                for r in range(n):
                    part[half, b, r * HALF + p * PAIR : r * HALF + (p + 1) * PAIR, :] = acc[k * n + r]
                    for side in range(2):
                        here = lane == (side * 2 + p) * n + r
                        tops[k] = jnp.where(here, top[k * n + r, side], tops[k])
                        totals[k] = jnp.where(here, total[k * n + r, side], totals[k])
        for k, b in enumerate(those):
            part[half, b, n * HALF :, :] = pack(tops[k], totals[k])

    def send_part(half, i):
        return copy(PART, half, part.at[half, i], got.at[half, second[half]], at_second(half, i))

    def parted(half):
        every = got.at[half, pl.ds(0, n - 1)]
        return copy(PART, half, every, every, neighbours(half)[1])

    for half in range(2):
        attend(half, [second[half]])
        got[half, second[half]] = part[half, second[half]]

    for half in range(2):
        forward(ASK_SECOND, half)

    for legs, away in (((2, 3), (3, 5, 1, 7)), ((4, 5, 6, 7), (2, 6, 4))):
        for half in range(2):
            for leg in legs:
                arrive(ASK_SECOND, half, leg).wait_recv()
        for half in range(2):
            those = [peer(second[half], off) for off in away]
            attend(half, those)
            for b in those:
                send_part(half, b).start()

    def send_merged(half, i):
        return copy(MERGED, half, merged.at[half, i], last.at[half, first[half]], at_first(half, i))

    def all_merged(half):
        every = last.at[half, pl.ds(0, n - 1)]
        return copy(MERGED, half, every, every, neighbours(half)[0])

    for half in range(2):
        parted(half).wait_recv()
        sides = [unpack(got[half, i, n * HALF :, :]) for i in range(n)]
        tops = jnp.stack([above for above, _ in sides], axis=0)
        totals = jnp.stack([below for _, below in sides], axis=0)
        top = jnp.max(tops, axis=0)
        weight = jnp.exp((tops - top[None]) * SCALE)
        total = jnp.sum(weight * totals, axis=0)
        some = jnp.maximum(total, 0.5)
        weight = weight / some[None]
        lse = jnp.where(total > 0.0, top * SCALE + jnp.log(some), EMPTY)
        tail = pack(lse, jnp.zeros_like(lse))
        for r in range(n):
            for p in range(2):
                scale = jnp.concatenate(
                    [
                        weight[:, :, (side * 2 + p) * n + r : (side * 2 + p) * n + r + 1]
                        for side in range(2)
                    ],
                    axis=1,
                )
                start = r * HALF + p * PAIR
                piece = got[half, :, start : start + PAIR, :].astype(f32)
                merged[half, r, p * PAIR : (p + 1) * PAIR, :] = jnp.sum(
                    piece * scale, axis=0
                ).astype(bf16)
            merged[half, r, HALF:, :] = tail
        for off in offsets(n):
            send_merged(half, peer(first[half], off)).start()
        last[half, first[half]] = merged[half, first[half]]

    def tell_first(half, i):
        return copy(TELL_FIRST, half, attn.at[half], told.at[half, first[half]], at_first(half, i))

    def all_told(half):
        every = told.at[half, pl.ds(0, n - 1)]
        return copy(TELL_FIRST, half, every, every, neighbours(half)[0])

    for load in loads[6:9]:
        load.wait()
    heads_in_row(nk_raw, rows64.at[pl.ds(0, KV_HEADS)])
    new_keys = rows64[:KV_HEADS, :]
    heads_in_row(nv_raw, rows64.at[pl.ds(KV_HEADS, KV_HEADS)])
    new_values = rows64[KV_HEADS : 2 * KV_HEADS, :]
    for half in range(2):
        kv_half = slice(half * 4, half * 4 + 4)
        query = q_ref[half].astype(f32).reshape(4, 8, 128)
        own = jnp.sum(query * new_keys[kv_half][:, None, :], axis=2, keepdims=True) * SCALE
        own = own.reshape(HALF, 1)
        own_value = jnp.broadcast_to(new_values[kv_half][:, None, :], (4, 8, 128)).reshape(HALF, 128)
        all_merged(half).wait_recv()
        lses = []
        for i in range(n):
            stat = unpack(last[half, i, HALF:, :])[0]
            lses.append(
                jnp.concatenate(
                    [
                        jnp.sum(
                            jnp.where(lane == (side * 2 + p) * n + first[half], stat, 0.0),
                            axis=1,
                            keepdims=True,
                        )
                        for p in range(2)
                        for side in range(2)
                    ],
                    axis=0,
                )
            )
        top = own
        for lse in lses:
            top = jnp.maximum(top, lse)
        weight = jnp.exp(own - top)
        total = weight
        acc = weight * own_value
        for i in range(n):
            weight = jnp.exp(lses[i] - top)
            total = total + weight
            acc = acc + weight * last[half, i, :HALF, :].astype(f32)
        attn[half] = (acc / total).astype(bf16)
        for off in offsets(n):
            tell_first(half, peer(first[half], off)).start()
        told[half, first[half]] = attn[half]

    for half in range(2):
        all_told(half).wait_recv()
        rows32[half] = told[half].astype(f32).reshape(n * HALF, 128)
        for h in range(HALF // 2):
            tile = [rows32[half, pl.ds(2 * h + s, n, stride=HALF), :] for s in range(2)]
            told_all[half, second[half], h] = jnp.concatenate(tile, axis=0).astype(bf16)
        begin(TELL_SECOND, half)

    for half in range(2):
        forward(TELL_SECOND, half)
    loads[9].wait()
    loads[10].wait()
    depth = HALF // 2 * HEAD_DIM
    mixed = []
    for half in range(2):
        for leg in range(2, len(LEGS)):
            arrive(TELL_SECOND, half, leg).wait_recv()
        x = jnp.concatenate(
            [told_all[half, :, h].reshape(n * 2 * n, 128) for h in range(HALF // 2)], axis=1
        )
        w = jnp.concatenate(
            [
                w_buf[side, half * (HALF // 2) : (half + 1) * (HALF // 2)].reshape(depth, 128)
                for side in range(2)
            ],
            axis=1,
        )
        acc = jnp.dot(x, w, preferred_element_type=f32).reshape(n, 2, n, 256)
        mixed.append(acc[:, 0, :, :128] + acc[:, 1, :, 128:])
    turn[...] = mixed[1].reshape(requests, 128)
    other = jnp.concatenate([turn[pl.ds(i, n, stride=n), :] for i in range(n)], axis=0)
    layer = res_buf[0].astype(f32) + (mixed[0].reshape(requests, 128) + other)
    line[...] = layer.astype(bf16)

    hand = pltpu.make_async_remote_copy(
        src_ref=line,
        dst_ref=landed,
        send_sem=pass_sem.at[0],
        recv_sem=pass_sem.at[1],
        device_id={"segment": following},
        device_id_type=MESH,
    )
    hand.start()

    for half in range(2):
        for stage in (asked, parted, all_merged, all_told):
            stage(half).wait_send()
        for ring in (ASK_SECOND, TELL_SECOND):
            for leg in range(len(LEGS)):
                leave(ring, half, leg).wait_send()
    hand.wait()
    out_ref[...] = landed[...]


def local(
    n_seg,
    n,
    queries,
    new_key,
    new_value,
    key_pool,
    value_pool,
    lengths,
    block_device,
    block_slot,
    residual,
    out_weight,
):
    f32, bf16 = jnp.float32, jnp.bfloat16
    slots = key_pool.shape[1]
    tokens = slots * BLK
    requests = n * n
    whole = pl.BlockSpec(memory_space=pltpu.VMEM)
    outside = pl.BlockSpec(memory_space=pltpu.HBM)
    blocks = block_device.shape[2]
    out = pl.pallas_call(
        functools.partial(kernel, n_seg, n),
        out_shape=jax.ShapeDtypeStruct((requests, 128), bf16),
        in_specs=[outside] * 10,
        out_specs=whole,
        scratch_shapes=[
            pltpu.VMEM((1, 1, HEADS * HEAD_DIM), bf16),
            pltpu.VMEM((1, 1, KV_HEADS * HEAD_DIM), bf16),
            pltpu.VMEM((1, 1, KV_HEADS * HEAD_DIM), bf16),
            pltpu.VMEM((1, requests), jnp.int32),
            pltpu.VMEM((1, blocks, requests), jnp.int32),
            pltpu.VMEM((1, blocks, requests), jnp.int32),
            pltpu.VMEM((1, requests, 128), bf16),
            pltpu.VMEM((HEADS, 128), f32),
            pltpu.VMEM((2, 2, PAIR, 128), bf16),
            pltpu.VMEM((slots, BLK, KV_HEADS * HEAD_DIM), bf16),
            pltpu.VMEM((slots, BLK, KV_HEADS * HEAD_DIM), bf16),
            pltpu.VMEM((2, HEADS // 2, HEAD_DIM, 128), bf16),
            pltpu.VMEM((4, 256, tokens), bf16),
            pltpu.VMEM((requests, PAIR // 2, tokens), f32),
            pltpu.VMEM((2, n, 2, n, PAIR, 128), bf16),
            pltpu.VMEM((2, n, n * HALF + PAIR, 128), bf16),
            pltpu.VMEM((2, n, n * HALF + PAIR, 128), bf16),
            pltpu.VMEM((2, n, HALF + PAIR, 128), bf16),
            pltpu.VMEM((2, n, HALF + PAIR, 128), bf16),
            pltpu.VMEM((2, HALF, 128), bf16),
            pltpu.VMEM((2, n, HALF, 128), bf16),
            pltpu.VMEM((2, n * HALF, 128), f32),
            pltpu.VMEM((2, n, HALF // 2, 2 * n, 128), bf16),
            pltpu.VMEM((requests, 128), f32),
            pltpu.VMEM((requests, 128), bf16),
            pltpu.VMEM((requests, 128), bf16),
            pltpu.SemaphoreType.DMA((4, 2)),
            pltpu.SemaphoreType.DMA((4, 2)),
            pltpu.SemaphoreType.DMA((2, 2 * len(LEGS))),
            pltpu.SemaphoreType.DMA((2, 2 * len(LEGS))),
            pltpu.SemaphoreType.DMA((11,)),
            pltpu.SemaphoreType.DMA((2,)),
        ],
        compiler_params=pltpu.CompilerParams(
            collective_id=0, has_side_effects=True, vmem_limit_bytes=60 * 1024 * 1024
        ),
        name="decode_layer",
    )(
        queries,
        new_key,
        new_value,
        lengths,
        jnp.swapaxes(block_device, 1, 2),
        jnp.swapaxes(block_slot, 1, 2),
        residual,
        key_pool[0],
        value_pool[0],
        out_weight[0].reshape(HEADS // 2, 2, HEAD_DIM, 128),
    )
    return out[None]


def solution(mesh):
    placed = (
        P("segment", "kv", None),
        P("segment", "kv", None),
        P("segment", "kv", None),
        P("segment", "kv", None, None),
        P("segment", "kv", None, None),
        P("segment", None),
        P("segment", None, None),
        P("segment", None, None),
        P("segment", None, "kv"),
        P("segment", None, "kv"),
    )
    n_seg = mesh.shape["segment"]
    n = next(i for i in range(1, 64) if i * i == mesh.shape["kv"])
    return jax.shard_map(
        functools.partial(local, n_seg, n),
        mesh=mesh,
        in_specs=placed,
        out_specs=P("segment", None, "kv"),
        check_vma=False,
    )
```

```python
import functools

import jax
import jax.numpy as jnp
from jax import lax
from jax.experimental import pallas as pl
from jax.experimental.pallas import tpu as pltpu
from jax.sharding import PartitionSpec as P

KV_HEADS = 8
HEAD_DIM = 128
HEADS = 64
HALF = HEADS // 2
PAIR = 16
BLK = 16
MESH = pl.DeviceIdType.MESH
EMPTY = -1e30
FLOOR = -1e29
SCALE = HEAD_DIM ** (-0.5)
LOG2_E = 1.4426950408889634

ASK_FIRST, PART, MERGED, TELL_FIRST = range(4)
ASK_SECOND, TELL_SECOND = range(2)

LEGS = (
    (0, None, 3, -3),
    (0, None, -3, 3),
    (0, None, 1, -1),
    (0, None, -1, 1),
    (-3, None, -1, -2),
    (3, None, 1, 2),
    (-3, 0, 1, -4),
    (3, 1, -1, 4),
)


def offsets(n):
    near = []
    for step in range(1, n // 2 + 1):
        near.append(step)
        if step != n - step:
            near.append(n - step)
    return near


def heads_in_row(raw, rows):
    flat = raw[0].astype(jnp.float32)
    for h in range(rows.shape[0]):
        rows[h : h + 1, :] = flat[:, h * HEAD_DIM : (h + 1) * HEAD_DIM]


def kernel(
    n_seg,
    n,
    q_hbm,
    nk_hbm,
    nv_hbm,
    len_hbm,
    dev_hbm,
    slot_hbm,
    res_hbm,
    k_hbm,
    v_hbm,
    w_hbm,
    out_ref,
    q_raw,
    nk_raw,
    nv_raw,
    len_buf,
    dev_buf,
    slot_buf,
    res_buf,
    rows64,
    q_ref,
    k_buf,
    v_buf,
    w_buf,
    kt_buf,
    bias_buf,
    q_all,
    part,
    got,
    merged,
    last,
    attn,
    told,
    rows32,
    told_all,
    turn,
    line,
    landed,
    send_sem,
    recv_sem,
    leg_send,
    leg_recv,
    load_sem,
    pass_sem,
):
    f32, bf16 = jnp.float32, jnp.bfloat16
    seg = lax.axis_index("segment")
    me = lax.axis_index("kv")
    y, z = lax.div(me, n), lax.rem(me, n)
    first, second = (z, y), (y, z)
    slots = k_buf.shape[0]
    tokens = slots * BLK
    rows = n * PAIR

    def at_first(half, i):
        return y * n + i if half == 0 else i * n + z

    def at_second(half, i):
        return i * n + z if half == 0 else y * n + i

    def peer(base, off):
        return lax.rem(base + off, n)

    def copy(stage, half, src, dst, device):
        return pltpu.make_async_remote_copy(
            src_ref=src,
            dst_ref=dst,
            send_sem=send_sem.at[stage, half],
            recv_sem=recv_sem.at[stage, half],
            device_id={"kv": device},
            device_id_type=MESH,
        )

    def neighbours(half):
        return at_first(half, peer(first[half], 1)), at_second(half, peer(second[half], 1))

    following, before = lax.rem(seg + 1, n_seg), lax.rem(seg + n_seg - 1, n_seg)

    barrier = pltpu.get_barrier_semaphore()
    for off in offsets(n):
        for half in range(2):
            pl.semaphore_signal(
                barrier,
                inc=1,
                device_id={"kv": at_first(half, peer(first[half], off))},
                device_id_type=MESH,
            )
    for other in (following, before):
        pl.semaphore_signal(barrier, inc=1, device_id={"segment": other}, device_id_type=MESH)

    loads = [
        pltpu.make_async_copy(src, dst, load_sem.at[i])
        for i, (src, dst) in enumerate(
            (
                (q_hbm, q_raw),
                (len_hbm, len_buf),
                (dev_hbm, dev_buf),
                (slot_hbm, slot_buf),
                (k_hbm, k_buf),
                (v_hbm, v_buf),
                (nk_hbm, nk_raw),
                (nv_hbm, nv_raw),
                (res_hbm, res_buf),
                (w_hbm.at[:, 0], w_buf.at[0]),
                (w_hbm.at[:, 1], w_buf.at[1]),
            )
        )
    ]
    for load in loads:
        load.start()

    loads[0].wait()
    heads_in_row(q_raw, rows64)
    for half in range(2):
        for p in range(2):
            start = half * HALF + p * PAIR
            q_ref[half, p] = rows64[start : start + PAIR, :].astype(bf16)
            q_all[half, second[half], p, first[half]] = q_ref[half, p]

    pl.semaphore_wait(barrier, 2 * (n - 1) + 2)

    def ask_first(half, i):
        mine = first[half]
        return copy(
            ASK_FIRST, half, q_ref.at[half], q_all.at[half, second[half], :, mine], at_first(half, i)
        )

    def asked(half):
        every = q_all.at[half, second[half], :, pl.ds(0, n - 1)]
        return copy(ASK_FIRST, half, every, every, neighbours(half)[0])

    def piece_of(ring, half, block, piece):
        if piece is None:
            return (q_all if ring == ASK_SECOND else told_all).at[half, block]
        if ring == ASK_SECOND:
            return q_all.at[half, block, piece]
        rows_of = HALF // 4
        return told_all.at[half, block, pl.ds(piece * rows_of, rows_of)]

    def leg_copy(ring, half, leg, block):
        ref = piece_of(ring, half, peer(second[half], n + block), LEGS[leg][1])
        return pltpu.make_async_remote_copy(
            src_ref=ref,
            dst_ref=ref,
            send_sem=leg_send.at[ring, half * len(LEGS) + leg],
            recv_sem=leg_recv.at[ring, half * len(LEGS) + leg],
            device_id={"kv": at_second(half, peer(second[half], n + LEGS[leg][2]))},
            device_id_type=MESH,
        )

    def leave(ring, half, leg):
        return leg_copy(ring, half, leg, LEGS[leg][0])

    def arrive(ring, half, leg):
        return leg_copy(ring, half, leg, LEGS[leg][3])

    def begin(ring, half):
        for leg in range(4):
            leave(ring, half, leg).start()

    def forward(ring, half):
        for way in range(2):
            arrive(ring, half, way).wait_recv()
            leave(ring, half, 4 + way).start()
        for way in range(2):
            leave(ring, half, 6 + way).start()

    for off in offsets(n):
        for half in range(2):
            ask_first(half, peer(first[half], off)).start()

    requests = n * n
    for load in loads[1:4]:
        load.wait()
    blocks = dev_buf.shape[1]
    holder = jnp.where(dev_buf[0] == me, slot_buf[0], -1)
    numbers = lax.broadcasted_iota(jnp.int32, (blocks, requests), 0)
    live = jnp.clip(len_buf[...] - numbers * BLK, 0, BLK).astype(f32)
    slot_of = lax.broadcasted_iota(jnp.int32, (slots, requests), 0)
    count = jnp.zeros((slots, requests), f32)
    for b in range(blocks):
        count = count + jnp.where(slot_of == holder[b : b + 1, :], live[b : b + 1, :], 0.0)
    spread = (
        lax.div(lax.broadcasted_iota(jnp.int32, (slots, tokens), 1), BLK)
        == lax.broadcasted_iota(jnp.int32, (slots, tokens), 0)
    ).astype(bf16)
    limit = lax.dot_general(
        count.astype(bf16), spread, (((0,), (0,)), ((), ())), preferred_element_type=f32
    )
    place = lax.rem(lax.broadcasted_iota(jnp.int32, (requests, tokens), 1), BLK).astype(f32)
    mask = jnp.where(place < limit, 0.0, EMPTY)
    for r in range(requests):
        bias_buf[r] = jnp.broadcast_to(mask[r : r + 1, :], (PAIR // 2, tokens))

    for half in range(2):
        asked(half).wait_recv()
        begin(ASK_SECOND, half)
    loads[4].wait()
    for pair in range(4):
        kt_buf[pair] = k_buf[:, :, pair * 256 : (pair + 1) * 256].reshape(tokens, 256).T
    loads[5].wait()

    def tiles(count):
        inside = lax.rem(lax.broadcasted_iota(jnp.int32, (count * PAIR, 128), 0), PAIR)
        return inside < PAIR // 2

    lane = lax.broadcasted_iota(jnp.int32, (PAIR // 2, 128), 1)
    used = 4 * n

    def three(stat):
        high = stat.astype(bf16).astype(f32)
        rest = stat - high
        middle = rest.astype(bf16).astype(f32)
        low = rest - middle
        return jnp.where(
            lane < used,
            high,
            jnp.where(lane < 2 * used, pltpu.roll(middle, used, 1), pltpu.roll(low, 2 * used, 1)),
        )

    def pack(above, below):
        return jnp.concatenate([three(above), three(below)], axis=0).astype(bf16)

    def unpack(tile):
        sides = tile.astype(f32)
        sides = (sides + pltpu.roll(sides, 128 - used, 1)) + pltpu.roll(sides, 128 - 2 * used, 1)
        return sides[: PAIR // 2], sides[PAIR // 2 :]

    def attend(half, those):
        count = len(those) * n
        upper = tiles(count)
        keep_upper = upper.astype(f32).astype(bf16)
        keep_lower = (1.0 - upper.astype(f32)).astype(bf16)
        bias = jnp.concatenate(
            [
                bias_buf[pl.ds(b * n, n)]
                if half == 0
                else jnp.stack([bias_buf[f * n + b] for f in range(n)], axis=0)
                for b in those
            ],
            axis=0,
        )
        tops = [jnp.full((PAIR // 2, 128), FLOOR, f32) for _ in those]
        totals = [jnp.zeros((PAIR // 2, 128), f32) for _ in those]
        for p in range(2):
            pair = half * 2 + p
            x = jnp.concatenate([q_all[half, b, p].reshape(rows, 128) for b in those], axis=0)
            x = jnp.concatenate([x * keep_upper, x * keep_lower], axis=1)
            score = jnp.dot(x, kt_buf[pair], preferred_element_type=f32)
            score = score.reshape(count, 2, PAIR // 2, tokens) + bias[:, None]
            score = score.reshape(count * PAIR, tokens)
            top = jnp.maximum(jnp.max(score, axis=1, keepdims=True), FLOOR)
            prob = jnp.exp2((score - top) * (SCALE * LOG2_E))
            total = jnp.sum(prob, axis=1, keepdims=True)
            value = v_buf[:, :, pair * 256 : (pair + 1) * 256].reshape(tokens, 256)
            acc = jnp.dot(prob.astype(bf16), value, preferred_element_type=f32)
            acc = jnp.where(upper, acc[:, :128], acc[:, 128:])
            acc = acc.astype(bf16).reshape(count, PAIR, 128)
            top = top.reshape(count, 2, PAIR // 2, 1)
            total = total.reshape(count, 2, PAIR // 2, 1)
            for k, b in enumerate(those):
                for r in range(n):
                    part[half, b, r * HALF + p * PAIR : r * HALF + (p + 1) * PAIR, :] = acc[k * n + r]
                    for side in range(2):
                        here = lane == (side * 2 + p) * n + r
                        tops[k] = jnp.where(here, top[k * n + r, side], tops[k])
                        totals[k] = jnp.where(here, total[k * n + r, side], totals[k])
        for k, b in enumerate(those):
            part[half, b, n * HALF :, :] = pack(tops[k], totals[k])

    def send_part(half, i):
        return copy(PART, half, part.at[half, i], got.at[half, second[half]], at_second(half, i))

    def parted(half):
        every = got.at[half, pl.ds(0, n - 1)]
        return copy(PART, half, every, every, neighbours(half)[1])

    for half in range(2):
        forward(ASK_SECOND, half)

    def one_step(t, carry):
        @pl.when(t == 1)
        def _():
            for half in range(2):
                for leg in (2, 3):
                    arrive(ASK_SECOND, half, leg).wait_recv()

        @pl.when(t == 2)
        def _():
            for half in range(2):
                for leg in (4, 5):
                    arrive(ASK_SECOND, half, leg).wait_recv()

        away = lax.rem(t + 2, 3) + 1
        those = [
            [peer(second[half], n - away), peer(second[half], away)] for half in range(2)
        ]
        for half in range(2):
            attend(half, those[half])
            for b in those[half]:
                send_part(half, b).start()
        return carry

    lax.fori_loop(0, 3, one_step, 0)
    for half in range(2):
        for leg in (6, 7):
            arrive(ASK_SECOND, half, leg).wait_recv()
        across = peer(second[half], n // 2)
        attend(half, [across])
        send_part(half, across).start()

    for half in range(2):
        attend(half, [second[half]])
        got[half, second[half]] = part[half, second[half]]

    def send_merged(half, i):
        return copy(MERGED, half, merged.at[half, i], last.at[half, first[half]], at_first(half, i))

    def all_merged(half):
        every = last.at[half, pl.ds(0, n - 1)]
        return copy(MERGED, half, every, every, neighbours(half)[0])

    for half in range(2):
        parted(half).wait_recv()
        sides = [unpack(got[half, i, n * HALF :, :]) for i in range(n)]
        tops = jnp.stack([above for above, _ in sides], axis=0)
        totals = jnp.stack([below for _, below in sides], axis=0)
        top = jnp.max(tops, axis=0)
        weight = jnp.exp((tops - top[None]) * SCALE)
        total = jnp.sum(weight * totals, axis=0)
        some = jnp.maximum(total, 0.5)
        weight = weight / some[None]
        lse = jnp.where(total > 0.0, top * SCALE + jnp.log(some), EMPTY)
        tail = pack(lse, jnp.zeros_like(lse))
        for r in range(n):
            for p in range(2):
                scale = jnp.concatenate(
                    [
                        weight[:, :, (side * 2 + p) * n + r : (side * 2 + p) * n + r + 1]
                        for side in range(2)
                    ],
                    axis=1,
                )
                start = r * HALF + p * PAIR
                piece = got[half, :, start : start + PAIR, :].astype(f32)
                merged[half, r, p * PAIR : (p + 1) * PAIR, :] = jnp.sum(
                    piece * scale, axis=0
                ).astype(bf16)
            merged[half, r, HALF:, :] = tail
        for off in offsets(n):
            send_merged(half, peer(first[half], off)).start()
        last[half, first[half]] = merged[half, first[half]]

    def tell_first(half, i):
        return copy(TELL_FIRST, half, attn.at[half], told.at[half, first[half]], at_first(half, i))

    def all_told(half):
        every = told.at[half, pl.ds(0, n - 1)]
        return copy(TELL_FIRST, half, every, every, neighbours(half)[0])

    for load in loads[6:9]:
        load.wait()
    heads_in_row(nk_raw, rows64.at[pl.ds(0, KV_HEADS)])
    new_keys = rows64[:KV_HEADS, :]
    heads_in_row(nv_raw, rows64.at[pl.ds(KV_HEADS, KV_HEADS)])
    new_values = rows64[KV_HEADS : 2 * KV_HEADS, :]
    for half in range(2):
        kv_half = slice(half * 4, half * 4 + 4)
        query = q_ref[half].astype(f32).reshape(4, 8, 128)
        own = jnp.sum(query * new_keys[kv_half][:, None, :], axis=2, keepdims=True) * SCALE
        own = own.reshape(HALF, 1)
        own_value = jnp.broadcast_to(new_values[kv_half][:, None, :], (4, 8, 128)).reshape(HALF, 128)
        all_merged(half).wait_recv()
        lses = []
        for i in range(n):
            stat = unpack(last[half, i, HALF:, :])[0]
            lses.append(
                jnp.concatenate(
                    [
                        jnp.sum(
                            jnp.where(lane == (side * 2 + p) * n + first[half], stat, 0.0),
                            axis=1,
                            keepdims=True,
                        )
                        for p in range(2)
                        for side in range(2)
                    ],
                    axis=0,
                )
            )
        top = own
        for lse in lses:
            top = jnp.maximum(top, lse)
        weight = jnp.exp(own - top)
        total = weight
        acc = weight * own_value
        for i in range(n):
            weight = jnp.exp(lses[i] - top)
            total = total + weight
            acc = acc + weight * last[half, i, :HALF, :].astype(f32)
        attn[half] = (acc / total).astype(bf16)
        for off in offsets(n):
            tell_first(half, peer(first[half], off)).start()
        told[half, first[half]] = attn[half]

    for half in range(2):
        all_told(half).wait_recv()
        rows32[half] = told[half].astype(f32).reshape(n * HALF, 128)
        for h in range(HALF // 2):
            tile = [rows32[half, pl.ds(2 * h + s, n, stride=HALF), :] for s in range(2)]
            told_all[half, second[half], h] = jnp.concatenate(tile, axis=0).astype(bf16)
        begin(TELL_SECOND, half)

    for half in range(2):
        forward(TELL_SECOND, half)
    loads[9].wait()
    loads[10].wait()
    depth = HALF // 2 * HEAD_DIM
    mixed = []
    for half in range(2):
        for leg in range(2, len(LEGS)):
            arrive(TELL_SECOND, half, leg).wait_recv()
        x = jnp.concatenate(
            [told_all[half, :, h].reshape(n * 2 * n, 128) for h in range(HALF // 2)], axis=1
        )
        w = jnp.concatenate(
            [
                w_buf[side, half * (HALF // 2) : (half + 1) * (HALF // 2)].reshape(depth, 128)
                for side in range(2)
            ],
            axis=1,
        )
        acc = jnp.dot(x, w, preferred_element_type=f32).reshape(n, 2, n, 256)
        mixed.append(acc[:, 0, :, :128] + acc[:, 1, :, 128:])
    turn[...] = mixed[1].reshape(requests, 128)
    other = jnp.concatenate([turn[pl.ds(i, n, stride=n), :] for i in range(n)], axis=0)
    layer = res_buf[0].astype(f32) + (mixed[0].reshape(requests, 128) + other)
    line[...] = layer.astype(bf16)

    hand = pltpu.make_async_remote_copy(
        src_ref=line,
        dst_ref=landed,
        send_sem=pass_sem.at[0],
        recv_sem=pass_sem.at[1],
        device_id={"segment": following},
        device_id_type=MESH,
    )
    hand.start()

    for half in range(2):
        for stage in (asked, parted, all_merged, all_told):
            stage(half).wait_send()
        for ring in (ASK_SECOND, TELL_SECOND):
            for leg in range(len(LEGS)):
                leave(ring, half, leg).wait_send()
    hand.wait()
    out_ref[...] = landed[...]


def local(
    n_seg,
    n,
    queries,
    new_key,
    new_value,
    key_pool,
    value_pool,
    lengths,
    block_device,
    block_slot,
    residual,
    out_weight,
):
    f32, bf16 = jnp.float32, jnp.bfloat16
    slots = key_pool.shape[1]
    tokens = slots * BLK
    requests = n * n
    whole = pl.BlockSpec(memory_space=pltpu.VMEM)
    outside = pl.BlockSpec(memory_space=pltpu.HBM)
    blocks = block_device.shape[2]
    out = pl.pallas_call(
        functools.partial(kernel, n_seg, n),
        out_shape=jax.ShapeDtypeStruct((requests, 128), bf16),
        in_specs=[outside] * 10,
        out_specs=whole,
        scratch_shapes=[
            pltpu.VMEM((1, 1, HEADS * HEAD_DIM), bf16),
            pltpu.VMEM((1, 1, KV_HEADS * HEAD_DIM), bf16),
            pltpu.VMEM((1, 1, KV_HEADS * HEAD_DIM), bf16),
            pltpu.VMEM((1, requests), jnp.int32),
            pltpu.VMEM((1, blocks, requests), jnp.int32),
            pltpu.VMEM((1, blocks, requests), jnp.int32),
            pltpu.VMEM((1, requests, 128), bf16),
            pltpu.VMEM((HEADS, 128), f32),
            pltpu.VMEM((2, 2, PAIR, 128), bf16),
            pltpu.VMEM((slots, BLK, KV_HEADS * HEAD_DIM), bf16),
            pltpu.VMEM((slots, BLK, KV_HEADS * HEAD_DIM), bf16),
            pltpu.VMEM((2, HEADS // 2, HEAD_DIM, 128), bf16),
            pltpu.VMEM((4, 256, tokens), bf16),
            pltpu.VMEM((requests, PAIR // 2, tokens), f32),
            pltpu.VMEM((2, n, 2, n, PAIR, 128), bf16),
            pltpu.VMEM((2, n, n * HALF + PAIR, 128), bf16),
            pltpu.VMEM((2, n, n * HALF + PAIR, 128), bf16),
            pltpu.VMEM((2, n, HALF + PAIR, 128), bf16),
            pltpu.VMEM((2, n, HALF + PAIR, 128), bf16),
            pltpu.VMEM((2, HALF, 128), bf16),
            pltpu.VMEM((2, n, HALF, 128), bf16),
            pltpu.VMEM((2, n * HALF, 128), f32),
            pltpu.VMEM((2, n, HALF // 2, 2 * n, 128), bf16),
            pltpu.VMEM((requests, 128), f32),
            pltpu.VMEM((requests, 128), bf16),
            pltpu.VMEM((requests, 128), bf16),
            pltpu.SemaphoreType.DMA((4, 2)),
            pltpu.SemaphoreType.DMA((4, 2)),
            pltpu.SemaphoreType.DMA((2, 2 * len(LEGS))),
            pltpu.SemaphoreType.DMA((2, 2 * len(LEGS))),
            pltpu.SemaphoreType.DMA((11,)),
            pltpu.SemaphoreType.DMA((2,)),
        ],
        compiler_params=pltpu.CompilerParams(
            collective_id=0, has_side_effects=True, vmem_limit_bytes=60 * 1024 * 1024
        ),
        name="decode_layer",
    )(
        queries,
        new_key,
        new_value,
        lengths,
        jnp.swapaxes(block_device, 1, 2),
        jnp.swapaxes(block_slot, 1, 2),
        residual,
        key_pool[0],
        value_pool[0],
        out_weight[0].reshape(HEADS // 2, 2, HEAD_DIM, 128),
    )
    return out[None]


def solution(mesh):
    placed = (
        P("segment", "kv", None),
        P("segment", "kv", None),
        P("segment", "kv", None),
        P("segment", "kv", None, None),
        P("segment", "kv", None, None),
        P("segment", None),
        P("segment", None, None),
        P("segment", None, None),
        P("segment", None, "kv"),
        P("segment", None, "kv"),
    )
    n_seg = mesh.shape["segment"]
    n = next(i for i in range(1, 64) if i * i == mesh.shape["kv"])
    return jax.shard_map(
        functools.partial(local, n_seg, n),
        mesh=mesh,
        in_specs=placed,
        out_specs=P("segment", None, "kv"),
        check_vma=False,
    )
```

```python
import functools

import jax
import jax.numpy as jnp
from jax import lax
from jax.experimental import pallas as pl
from jax.experimental.pallas import tpu as pltpu
from jax.sharding import PartitionSpec as P

KV_HEADS = 8
HEAD_DIM = 128
HEADS = 64
HALF = HEADS // 2
PAIR = 16
BLK = 16
MESH = pl.DeviceIdType.MESH
EMPTY = -1e30
FLOOR = -1e29
SCALE = HEAD_DIM ** (-0.5)
LOG2_E = 1.4426950408889634

ASK_FIRST, PART, MERGED, TELL_FIRST = range(4)
ASK_SECOND, TELL_SECOND = range(2)

LEGS = (
    (0, None, 3, -3),
    (0, None, -3, 3),
    (0, None, 1, -1),
    (0, None, -1, 1),
    (-3, None, -1, -2),
    (3, None, 1, 2),
    (-3, 0, 1, -4),
    (3, 1, -1, 4),
)


def offsets(n):
    near = []
    for step in range(1, n // 2 + 1):
        near.append(step)
        if step != n - step:
            near.append(n - step)
    return near


def heads_in_row(raw, rows):
    flat = raw[0].astype(jnp.float32)
    for h in range(rows.shape[0]):
        rows[h : h + 1, :] = flat[:, h * HEAD_DIM : (h + 1) * HEAD_DIM]


def kernel(
    n_seg,
    n,
    q_hbm,
    nk_hbm,
    nv_hbm,
    len_hbm,
    dev_hbm,
    slot_hbm,
    res_hbm,
    k_hbm,
    v_hbm,
    w_hbm,
    out_ref,
    q_raw,
    nk_raw,
    nv_raw,
    len_buf,
    dev_buf,
    slot_buf,
    res_buf,
    rows64,
    q_ref,
    k_buf,
    v_buf,
    w_buf,
    kt_buf,
    bias_buf,
    q_all,
    part,
    got,
    merged,
    last,
    attn,
    told,
    rows32,
    told_all,
    turn,
    line,
    landed,
    send_sem,
    recv_sem,
    leg_send,
    leg_recv,
    load_sem,
    pass_sem,
):
    f32, bf16 = jnp.float32, jnp.bfloat16
    seg = lax.axis_index("segment")
    me = lax.axis_index("kv")
    y, z = lax.div(me, n), lax.rem(me, n)
    first, second = (z, y), (y, z)
    slots = k_buf.shape[0]
    tokens = slots * BLK
    rows = n * PAIR

    def at_first(half, i):
        return y * n + i if half == 0 else i * n + z

    def at_second(half, i):
        return i * n + z if half == 0 else y * n + i

    def peer(base, off):
        return lax.rem(base + off, n)

    def copy(stage, half, src, dst, device):
        return pltpu.make_async_remote_copy(
            src_ref=src,
            dst_ref=dst,
            send_sem=send_sem.at[stage, half],
            recv_sem=recv_sem.at[stage, half],
            device_id={"kv": device},
            device_id_type=MESH,
        )

    def neighbours(half):
        return at_first(half, peer(first[half], 1)), at_second(half, peer(second[half], 1))

    following, before = lax.rem(seg + 1, n_seg), lax.rem(seg + n_seg - 1, n_seg)

    barrier = pltpu.get_barrier_semaphore()
    for off in offsets(n):
        for half in range(2):
            pl.semaphore_signal(
                barrier,
                inc=1,
                device_id={"kv": at_first(half, peer(first[half], off))},
                device_id_type=MESH,
            )
    for other in (following, before):
        pl.semaphore_signal(barrier, inc=1, device_id={"segment": other}, device_id_type=MESH)

    loads = [
        pltpu.make_async_copy(src, dst, load_sem.at[i])
        for i, (src, dst) in enumerate(
            (
                (q_hbm, q_raw),
                (len_hbm, len_buf),
                (dev_hbm, dev_buf),
                (slot_hbm, slot_buf),
                (k_hbm, k_buf),
                (v_hbm, v_buf),
                (nk_hbm, nk_raw),
                (nv_hbm, nv_raw),
                (res_hbm, res_buf),
                (w_hbm.at[:, 0], w_buf.at[0]),
                (w_hbm.at[:, 1], w_buf.at[1]),
            )
        )
    ]
    for load in loads:
        load.start()

    loads[0].wait()
    heads_in_row(q_raw, rows64)
    for half in range(2):
        for p in range(2):
            start = half * HALF + p * PAIR
            q_ref[half, p] = rows64[start : start + PAIR, :].astype(bf16)
            q_all[half, second[half], p, first[half]] = q_ref[half, p]

    pl.semaphore_wait(barrier, 2 * (n - 1) + 2)

    def ask_first(half, i):
        mine = first[half]
        return copy(
            ASK_FIRST, half, q_ref.at[half], q_all.at[half, second[half], :, mine], at_first(half, i)
        )

    def asked(half):
        every = q_all.at[half, second[half], :, pl.ds(0, n - 1)]
        return copy(ASK_FIRST, half, every, every, neighbours(half)[0])

    def piece_of(ring, half, block, piece):
        if piece is None:
            return (q_all if ring == ASK_SECOND else told_all).at[half, block]
        if ring == ASK_SECOND:
            return q_all.at[half, block, piece]
        rows_of = HALF // 4
        return told_all.at[half, block, pl.ds(piece * rows_of, rows_of)]

    def leg_copy(ring, half, leg, block):
        ref = piece_of(ring, half, peer(second[half], n + block), LEGS[leg][1])
        return pltpu.make_async_remote_copy(
            src_ref=ref,
            dst_ref=ref,
            send_sem=leg_send.at[ring, half * len(LEGS) + leg],
            recv_sem=leg_recv.at[ring, half * len(LEGS) + leg],
            device_id={"kv": at_second(half, peer(second[half], n + LEGS[leg][2]))},
            device_id_type=MESH,
        )

    def leave(ring, half, leg):
        return leg_copy(ring, half, leg, LEGS[leg][0])

    def arrive(ring, half, leg):
        return leg_copy(ring, half, leg, LEGS[leg][3])

    def begin(ring, half):
        for leg in range(4):
            leave(ring, half, leg).start()

    def forward(ring, half):
        for way in range(2):
            arrive(ring, half, way).wait_recv()
            leave(ring, half, 4 + way).start()
        for way in range(2):
            leave(ring, half, 6 + way).start()

    for off in offsets(n):
        for half in range(2):
            ask_first(half, peer(first[half], off)).start()

    requests = n * n
    for load in loads[1:4]:
        load.wait()
    blocks = dev_buf.shape[1]
    holder = jnp.where(dev_buf[0] == me, slot_buf[0], -1)
    numbers = lax.broadcasted_iota(jnp.int32, (blocks, requests), 0)
    live = jnp.clip(len_buf[...] - numbers * BLK, 0, BLK).astype(f32)
    slot_of = lax.broadcasted_iota(jnp.int32, (slots, requests), 0)
    count = jnp.zeros((slots, requests), f32)
    for b in range(blocks):
        count = count + jnp.where(slot_of == holder[b : b + 1, :], live[b : b + 1, :], 0.0)
    spread = (
        lax.div(lax.broadcasted_iota(jnp.int32, (slots, tokens), 1), BLK)
        == lax.broadcasted_iota(jnp.int32, (slots, tokens), 0)
    ).astype(bf16)
    limit = lax.dot_general(
        count.astype(bf16), spread, (((0,), (0,)), ((), ())), preferred_element_type=f32
    )
    place = lax.rem(lax.broadcasted_iota(jnp.int32, (requests, tokens), 1), BLK).astype(f32)
    mask = jnp.where(place < limit, 0.0, EMPTY)
    for r in range(requests):
        bias_buf[r] = jnp.broadcast_to(mask[r : r + 1, :], (PAIR // 2, tokens))

    for half in range(2):
        asked(half).wait_recv()
        begin(ASK_SECOND, half)
    loads[4].wait()
    for pair in range(4):
        kt_buf[pair] = k_buf[:, :, pair * 256 : (pair + 1) * 256].reshape(tokens, 256).T
    loads[5].wait()

    def tiles(count):
        inside = lax.rem(lax.broadcasted_iota(jnp.int32, (count * PAIR, 128), 0), PAIR)
        return inside < PAIR // 2

    lane = lax.broadcasted_iota(jnp.int32, (PAIR // 2, 128), 1)
    used = 4 * n

    def three(stat):
        high = stat.astype(bf16).astype(f32)
        rest = stat - high
        middle = rest.astype(bf16).astype(f32)
        low = rest - middle
        return jnp.where(
            lane < used,
            high,
            jnp.where(lane < 2 * used, pltpu.roll(middle, used, 1), pltpu.roll(low, 2 * used, 1)),
        )

    def pack(above, below):
        return jnp.concatenate([three(above), three(below)], axis=0).astype(bf16)

    def unpack(tile):
        sides = tile.astype(f32)
        sides = (sides + pltpu.roll(sides, 128 - used, 1)) + pltpu.roll(sides, 128 - 2 * used, 1)
        return sides[: PAIR // 2], sides[PAIR // 2 :]

    def attend(half, those):
        count = len(those) * n
        upper = tiles(count)
        keep_upper = upper.astype(f32).astype(bf16)
        keep_lower = (1.0 - upper.astype(f32)).astype(bf16)
        bias = jnp.concatenate(
            [
                bias_buf[pl.ds(b * n, n)]
                if half == 0
                else jnp.stack([bias_buf[f * n + b] for f in range(n)], axis=0)
                for b in those
            ],
            axis=0,
        )
        tops = [jnp.full((PAIR // 2, 128), FLOOR, f32) for _ in those]
        totals = [jnp.zeros((PAIR // 2, 128), f32) for _ in those]
        for p in range(2):
            pair = half * 2 + p
            x = jnp.concatenate([q_all[half, b, p].reshape(rows, 128) for b in those], axis=0)
            x = jnp.concatenate([x * keep_upper, x * keep_lower], axis=1)
            score = jnp.dot(x, kt_buf[pair], preferred_element_type=f32)
            score = score.reshape(count, 2, PAIR // 2, tokens) + bias[:, None]
            score = score.reshape(count * PAIR, tokens)
            top = jnp.maximum(jnp.max(score, axis=1, keepdims=True), FLOOR)
            prob = jnp.exp2((score - top) * (SCALE * LOG2_E))
            total = jnp.sum(prob, axis=1, keepdims=True)
            value = v_buf[:, :, pair * 256 : (pair + 1) * 256].reshape(tokens, 256)
            acc = jnp.dot(prob.astype(bf16), value, preferred_element_type=f32)
            acc = jnp.where(upper, acc[:, :128], acc[:, 128:])
            acc = acc.astype(bf16).reshape(count, PAIR, 128)
            top = top.reshape(count, 2, PAIR // 2, 1)
            total = total.reshape(count, 2, PAIR // 2, 1)
            for k, b in enumerate(those):
                for r in range(n):
                    part[half, b, r * HALF + p * PAIR : r * HALF + (p + 1) * PAIR, :] = acc[k * n + r]
                    for side in range(2):
                        here = lane == (side * 2 + p) * n + r
                        tops[k] = jnp.where(here, top[k * n + r, side], tops[k])
                        totals[k] = jnp.where(here, total[k * n + r, side], totals[k])
        for k, b in enumerate(those):
            part[half, b, n * HALF :, :] = pack(tops[k], totals[k])

    def send_part(half, i):
        return copy(PART, half, part.at[half, i], got.at[half, second[half]], at_second(half, i))

    def parted(half):
        every = got.at[half, pl.ds(0, n - 1)]
        return copy(PART, half, every, every, neighbours(half)[1])

    for half in range(2):
        forward(ASK_SECOND, half)

    def one_step(t, carry):
        @pl.when(t == 1)
        def _():
            for half in range(2):
                for leg in (2, 3):
                    arrive(ASK_SECOND, half, leg).wait_recv()

        @pl.when(t == 2)
        def _():
            for half in range(2):
                for leg in (4, 5):
                    arrive(ASK_SECOND, half, leg).wait_recv()

        away = lax.rem(t + 2, 3) + 1
        those = [
            [peer(second[half], n - away), peer(second[half], away)] for half in range(2)
        ]
        for half in range(2):
            for b in those[half]:
                attend(half, [b])
                send_part(half, b).start()
        return carry

    lax.fori_loop(0, 3, one_step, 0)
    for half in range(2):
        for leg in (6, 7):
            arrive(ASK_SECOND, half, leg).wait_recv()
        across = peer(second[half], n // 2)
        attend(half, [across])
        send_part(half, across).start()

    for half in range(2):
        attend(half, [second[half]])
        got[half, second[half]] = part[half, second[half]]

    def send_merged(half, i):
        return copy(MERGED, half, merged.at[half, i], last.at[half, first[half]], at_first(half, i))

    def all_merged(half):
        every = last.at[half, pl.ds(0, n - 1)]
        return copy(MERGED, half, every, every, neighbours(half)[0])

    for half in range(2):
        parted(half).wait_recv()
        sides = [unpack(got[half, i, n * HALF :, :]) for i in range(n)]
        tops = jnp.stack([above for above, _ in sides], axis=0)
        totals = jnp.stack([below for _, below in sides], axis=0)
        top = jnp.max(tops, axis=0)
        weight = jnp.exp((tops - top[None]) * SCALE)
        total = jnp.sum(weight * totals, axis=0)
        some = jnp.maximum(total, 0.5)
        weight = weight / some[None]
        lse = jnp.where(total > 0.0, top * SCALE + jnp.log(some), EMPTY)
        tail = pack(lse, jnp.zeros_like(lse))
        for r in range(n):
            for p in range(2):
                scale = jnp.concatenate(
                    [
                        weight[:, :, (side * 2 + p) * n + r : (side * 2 + p) * n + r + 1]
                        for side in range(2)
                    ],
                    axis=1,
                )
                start = r * HALF + p * PAIR
                piece = got[half, :, start : start + PAIR, :].astype(f32)
                merged[half, r, p * PAIR : (p + 1) * PAIR, :] = jnp.sum(
                    piece * scale, axis=0
                ).astype(bf16)
            merged[half, r, HALF:, :] = tail
        for off in offsets(n):
            send_merged(half, peer(first[half], off)).start()
        last[half, first[half]] = merged[half, first[half]]

    def tell_first(half, i):
        return copy(TELL_FIRST, half, attn.at[half], told.at[half, first[half]], at_first(half, i))

    def all_told(half):
        every = told.at[half, pl.ds(0, n - 1)]
        return copy(TELL_FIRST, half, every, every, neighbours(half)[0])

    for load in loads[6:9]:
        load.wait()
    heads_in_row(nk_raw, rows64.at[pl.ds(0, KV_HEADS)])
    new_keys = rows64[:KV_HEADS, :]
    heads_in_row(nv_raw, rows64.at[pl.ds(KV_HEADS, KV_HEADS)])
    new_values = rows64[KV_HEADS : 2 * KV_HEADS, :]
    for half in range(2):
        kv_half = slice(half * 4, half * 4 + 4)
        query = q_ref[half].astype(f32).reshape(4, 8, 128)
        own = jnp.sum(query * new_keys[kv_half][:, None, :], axis=2, keepdims=True) * SCALE
        own = own.reshape(HALF, 1)
        own_value = jnp.broadcast_to(new_values[kv_half][:, None, :], (4, 8, 128)).reshape(HALF, 128)
        all_merged(half).wait_recv()
        lses = []
        for i in range(n):
            stat = unpack(last[half, i, HALF:, :])[0]
            lses.append(
                jnp.concatenate(
                    [
                        jnp.sum(
                            jnp.where(lane == (side * 2 + p) * n + first[half], stat, 0.0),
                            axis=1,
                            keepdims=True,
                        )
                        for p in range(2)
                        for side in range(2)
                    ],
                    axis=0,
                )
            )
        top = own
        for lse in lses:
            top = jnp.maximum(top, lse)
        weight = jnp.exp(own - top)
        total = weight
        acc = weight * own_value
        for i in range(n):
            weight = jnp.exp(lses[i] - top)
            total = total + weight
            acc = acc + weight * last[half, i, :HALF, :].astype(f32)
        attn[half] = (acc / total).astype(bf16)
        for off in offsets(n):
            tell_first(half, peer(first[half], off)).start()
        told[half, first[half]] = attn[half]

    for half in range(2):
        all_told(half).wait_recv()
        rows32[half] = told[half].astype(f32).reshape(n * HALF, 128)
        for h in range(HALF // 2):
            tile = [rows32[half, pl.ds(2 * h + s, n, stride=HALF), :] for s in range(2)]
            told_all[half, second[half], h] = jnp.concatenate(tile, axis=0).astype(bf16)
        begin(TELL_SECOND, half)

    for half in range(2):
        forward(TELL_SECOND, half)
    loads[9].wait()
    loads[10].wait()
    depth = HALF // 2 * HEAD_DIM
    mixed = []
    for half in range(2):
        for leg in range(2, len(LEGS)):
            arrive(TELL_SECOND, half, leg).wait_recv()
        x = jnp.concatenate(
            [told_all[half, :, h].reshape(n * 2 * n, 128) for h in range(HALF // 2)], axis=1
        )
        w = jnp.concatenate(
            [
                w_buf[side, half * (HALF // 2) : (half + 1) * (HALF // 2)].reshape(depth, 128)
                for side in range(2)
            ],
            axis=1,
        )
        acc = jnp.dot(x, w, preferred_element_type=f32).reshape(n, 2, n, 256)
        mixed.append(acc[:, 0, :, :128] + acc[:, 1, :, 128:])
    turn[...] = mixed[1].reshape(requests, 128)
    other = jnp.concatenate([turn[pl.ds(i, n, stride=n), :] for i in range(n)], axis=0)
    layer = res_buf[0].astype(f32) + (mixed[0].reshape(requests, 128) + other)
    line[...] = layer.astype(bf16)

    hand = pltpu.make_async_remote_copy(
        src_ref=line,
        dst_ref=landed,
        send_sem=pass_sem.at[0],
        recv_sem=pass_sem.at[1],
        device_id={"segment": following},
        device_id_type=MESH,
    )
    hand.start()

    for half in range(2):
        for stage in (asked, parted, all_merged, all_told):
            stage(half).wait_send()
        for ring in (ASK_SECOND, TELL_SECOND):
            for leg in range(len(LEGS)):
                leave(ring, half, leg).wait_send()
    hand.wait()
    out_ref[...] = landed[...]


def local(
    n_seg,
    n,
    queries,
    new_key,
    new_value,
    key_pool,
    value_pool,
    lengths,
    block_device,
    block_slot,
    residual,
    out_weight,
):
    f32, bf16 = jnp.float32, jnp.bfloat16
    slots = key_pool.shape[1]
    tokens = slots * BLK
    requests = n * n
    whole = pl.BlockSpec(memory_space=pltpu.VMEM)
    outside = pl.BlockSpec(memory_space=pltpu.HBM)
    blocks = block_device.shape[2]
    out = pl.pallas_call(
        functools.partial(kernel, n_seg, n),
        out_shape=jax.ShapeDtypeStruct((requests, 128), bf16),
        in_specs=[outside] * 10,
        out_specs=whole,
        scratch_shapes=[
            pltpu.VMEM((1, 1, HEADS * HEAD_DIM), bf16),
            pltpu.VMEM((1, 1, KV_HEADS * HEAD_DIM), bf16),
            pltpu.VMEM((1, 1, KV_HEADS * HEAD_DIM), bf16),
            pltpu.VMEM((1, requests), jnp.int32),
            pltpu.VMEM((1, blocks, requests), jnp.int32),
            pltpu.VMEM((1, blocks, requests), jnp.int32),
            pltpu.VMEM((1, requests, 128), bf16),
            pltpu.VMEM((HEADS, 128), f32),
            pltpu.VMEM((2, 2, PAIR, 128), bf16),
            pltpu.VMEM((slots, BLK, KV_HEADS * HEAD_DIM), bf16),
            pltpu.VMEM((slots, BLK, KV_HEADS * HEAD_DIM), bf16),
            pltpu.VMEM((2, HEADS // 2, HEAD_DIM, 128), bf16),
            pltpu.VMEM((4, 256, tokens), bf16),
            pltpu.VMEM((requests, PAIR // 2, tokens), f32),
            pltpu.VMEM((2, n, 2, n, PAIR, 128), bf16),
            pltpu.VMEM((2, n, n * HALF + PAIR, 128), bf16),
            pltpu.VMEM((2, n, n * HALF + PAIR, 128), bf16),
            pltpu.VMEM((2, n, HALF + PAIR, 128), bf16),
            pltpu.VMEM((2, n, HALF + PAIR, 128), bf16),
            pltpu.VMEM((2, HALF, 128), bf16),
            pltpu.VMEM((2, n, HALF, 128), bf16),
            pltpu.VMEM((2, n * HALF, 128), f32),
            pltpu.VMEM((2, n, HALF // 2, 2 * n, 128), bf16),
            pltpu.VMEM((requests, 128), f32),
            pltpu.VMEM((requests, 128), bf16),
            pltpu.VMEM((requests, 128), bf16),
            pltpu.SemaphoreType.DMA((4, 2)),
            pltpu.SemaphoreType.DMA((4, 2)),
            pltpu.SemaphoreType.DMA((2, 2 * len(LEGS))),
            pltpu.SemaphoreType.DMA((2, 2 * len(LEGS))),
            pltpu.SemaphoreType.DMA((11,)),
            pltpu.SemaphoreType.DMA((2,)),
        ],
        compiler_params=pltpu.CompilerParams(
            collective_id=0, has_side_effects=True, vmem_limit_bytes=60 * 1024 * 1024
        ),
        name="decode_layer",
    )(
        queries,
        new_key,
        new_value,
        lengths,
        jnp.swapaxes(block_device, 1, 2),
        jnp.swapaxes(block_slot, 1, 2),
        residual,
        key_pool[0],
        value_pool[0],
        out_weight[0].reshape(HEADS // 2, 2, HEAD_DIM, 128),
    )
    return out[None]


def solution(mesh):
    placed = (
        P("segment", "kv", None),
        P("segment", "kv", None),
        P("segment", "kv", None),
        P("segment", "kv", None, None),
        P("segment", "kv", None, None),
        P("segment", None),
        P("segment", None, None),
        P("segment", None, None),
        P("segment", None, "kv"),
        P("segment", None, "kv"),
    )
    n_seg = mesh.shape["segment"]
    n = next(i for i in range(1, 64) if i * i == mesh.shape["kv"])
    return jax.shard_map(
        functools.partial(local, n_seg, n),
        mesh=mesh,
        in_specs=placed,
        out_specs=P("segment", None, "kv"),
        check_vma=False,
    )
```

```python
import functools

import jax
import jax.numpy as jnp
from jax import lax
from jax.experimental import pallas as pl
from jax.experimental.pallas import tpu as pltpu
from jax.sharding import PartitionSpec as P

KV_HEADS = 8
HEAD_DIM = 128
HEADS = 64
HALF = HEADS // 2
PAIR = 16
BLK = 16
MESH = pl.DeviceIdType.MESH
EMPTY = -1e30
FLOOR = -1e29
SCALE = HEAD_DIM ** (-0.5)
LOG2_E = 1.4426950408889634

ASK_FIRST, PART, MERGED, TELL_FIRST = range(4)
ASK_SECOND, TELL_SECOND = range(2)

LEGS = (
    (0, None, 3, -3),
    (0, None, -3, 3),
    (0, None, 1, -1),
    (0, None, -1, 1),
    (-3, None, -1, -2),
    (3, None, 1, 2),
    (-3, 0, 1, -4),
    (3, 1, -1, 4),
)


def offsets(n):
    near = []
    for step in range(1, n // 2 + 1):
        near.append(step)
        if step != n - step:
            near.append(n - step)
    return near


def heads_in_row(raw, rows):
    flat = raw[0].astype(jnp.float32)
    for h in range(rows.shape[0]):
        rows[h : h + 1, :] = flat[:, h * HEAD_DIM : (h + 1) * HEAD_DIM]


def kernel(
    n_seg,
    n,
    q_hbm,
    nk_hbm,
    nv_hbm,
    len_hbm,
    dev_hbm,
    slot_hbm,
    res_hbm,
    k_hbm,
    v_hbm,
    w_hbm,
    out_ref,
    q_raw,
    nk_raw,
    nv_raw,
    len_buf,
    dev_buf,
    slot_buf,
    res_buf,
    rows64,
    q_ref,
    k_buf,
    v_buf,
    w_buf,
    kt_buf,
    bias_buf,
    q_all,
    part,
    got,
    merged,
    last,
    attn,
    told,
    rows32,
    told_all,
    turn,
    line,
    landed,
    send_sem,
    recv_sem,
    leg_send,
    leg_recv,
    load_sem,
    pass_sem,
):
    f32, bf16 = jnp.float32, jnp.bfloat16
    seg = lax.axis_index("segment")
    me = lax.axis_index("kv")
    y, z = lax.div(me, n), lax.rem(me, n)
    first, second = (z, y), (y, z)
    slots = k_buf.shape[0]
    tokens = slots * BLK
    rows = n * PAIR

    def at_first(half, i):
        return y * n + i if half == 0 else i * n + z

    def at_second(half, i):
        return i * n + z if half == 0 else y * n + i

    def peer(base, off):
        return lax.rem(base + off, n)

    def copy(stage, half, src, dst, device):
        return pltpu.make_async_remote_copy(
            src_ref=src,
            dst_ref=dst,
            send_sem=send_sem.at[stage, half],
            recv_sem=recv_sem.at[stage, half],
            device_id={"kv": device},
            device_id_type=MESH,
        )

    def neighbours(half):
        return at_first(half, peer(first[half], 1)), at_second(half, peer(second[half], 1))

    following, before = lax.rem(seg + 1, n_seg), lax.rem(seg + n_seg - 1, n_seg)

    barrier = pltpu.get_barrier_semaphore()
    for off in offsets(n):
        for half in range(2):
            pl.semaphore_signal(
                barrier,
                inc=1,
                device_id={"kv": at_first(half, peer(first[half], off))},
                device_id_type=MESH,
            )
    for other in (following, before):
        pl.semaphore_signal(barrier, inc=1, device_id={"segment": other}, device_id_type=MESH)

    loads = [
        pltpu.make_async_copy(src, dst, load_sem.at[i])
        for i, (src, dst) in enumerate(
            (
                (q_hbm, q_raw),
                (len_hbm, len_buf),
                (dev_hbm, dev_buf),
                (slot_hbm, slot_buf),
                (k_hbm, k_buf),
                (v_hbm, v_buf),
                (nk_hbm, nk_raw),
                (nv_hbm, nv_raw),
                (res_hbm, res_buf),
                (w_hbm.at[:, 0], w_buf.at[0]),
                (w_hbm.at[:, 1], w_buf.at[1]),
            )
        )
    ]
    for load in loads:
        load.start()

    loads[0].wait()
    heads_in_row(q_raw, rows64)
    for half in range(2):
        for p in range(2):
            start = half * HALF + p * PAIR
            q_ref[half, p] = rows64[start : start + PAIR, :].astype(bf16)
            q_all[half, second[half], p, first[half]] = q_ref[half, p]

    pl.semaphore_wait(barrier, 2 * (n - 1) + 2)

    def ask_first(half, i):
        mine = first[half]
        return copy(
            ASK_FIRST, half, q_ref.at[half], q_all.at[half, second[half], :, mine], at_first(half, i)
        )

    def asked(half):
        every = q_all.at[half, second[half], :, pl.ds(0, n - 1)]
        return copy(ASK_FIRST, half, every, every, neighbours(half)[0])

    def piece_of(ring, half, block, piece):
        if piece is None:
            return (q_all if ring == ASK_SECOND else told_all).at[half, block]
        if ring == ASK_SECOND:
            return q_all.at[half, block, piece]
        rows_of = HALF // 4
        return told_all.at[half, block, pl.ds(piece * rows_of, rows_of)]

    def leg_copy(ring, half, leg, block):
        ref = piece_of(ring, half, peer(second[half], n + block), LEGS[leg][1])
        return pltpu.make_async_remote_copy(
            src_ref=ref,
            dst_ref=ref,
            send_sem=leg_send.at[ring, half * len(LEGS) + leg],
            recv_sem=leg_recv.at[ring, half * len(LEGS) + leg],
            device_id={"kv": at_second(half, peer(second[half], n + LEGS[leg][2]))},
            device_id_type=MESH,
        )

    def leave(ring, half, leg):
        return leg_copy(ring, half, leg, LEGS[leg][0])

    def arrive(ring, half, leg):
        return leg_copy(ring, half, leg, LEGS[leg][3])

    def begin(ring, half):
        for leg in range(4):
            leave(ring, half, leg).start()

    def forward(ring, half):
        for way in range(2):
            arrive(ring, half, way).wait_recv()
            leave(ring, half, 4 + way).start()
        for way in range(2):
            leave(ring, half, 6 + way).start()

    for off in offsets(n):
        for half in range(2):
            ask_first(half, peer(first[half], off)).start()

    requests = n * n
    for load in loads[1:4]:
        load.wait()
    blocks = dev_buf.shape[1]
    holder = jnp.where(dev_buf[0] == me, slot_buf[0], -1)
    numbers = lax.broadcasted_iota(jnp.int32, (blocks, requests), 0)
    live = jnp.clip(len_buf[...] - numbers * BLK, 0, BLK).astype(f32)
    slot_of = lax.broadcasted_iota(jnp.int32, (slots, requests), 0)
    count = jnp.zeros((slots, requests), f32)
    for b in range(blocks):
        count = count + jnp.where(slot_of == holder[b : b + 1, :], live[b : b + 1, :], 0.0)
    spread = (
        lax.div(lax.broadcasted_iota(jnp.int32, (slots, tokens), 1), BLK)
        == lax.broadcasted_iota(jnp.int32, (slots, tokens), 0)
    ).astype(bf16)
    limit = lax.dot_general(
        count.astype(bf16), spread, (((0,), (0,)), ((), ())), preferred_element_type=f32
    )
    place = lax.rem(lax.broadcasted_iota(jnp.int32, (requests, tokens), 1), BLK).astype(f32)
    mask = jnp.where(place < limit, 0.0, EMPTY)
    for r in range(requests):
        bias_buf[r] = jnp.broadcast_to(mask[r : r + 1, :], (PAIR // 2, tokens))

    for half in range(2):
        asked(half).wait_recv()
        begin(ASK_SECOND, half)
    loads[4].wait()
    for pair in range(4):
        kt_buf[pair] = k_buf[:, :, pair * 256 : (pair + 1) * 256].reshape(tokens, 256).T
    loads[5].wait()

    def tiles(count):
        inside = lax.rem(lax.broadcasted_iota(jnp.int32, (count * PAIR, 128), 0), PAIR)
        return inside < PAIR // 2

    lane = lax.broadcasted_iota(jnp.int32, (PAIR // 2, 128), 1)
    used = 4 * n

    def three(stat):
        high = stat.astype(bf16).astype(f32)
        rest = stat - high
        middle = rest.astype(bf16).astype(f32)
        low = rest - middle
        return jnp.where(
            lane < used,
            high,
            jnp.where(lane < 2 * used, pltpu.roll(middle, used, 1), pltpu.roll(low, 2 * used, 1)),
        )

    def pack(above, below):
        return jnp.concatenate([three(above), three(below)], axis=0).astype(bf16)

    def unpack(tile):
        sides = tile.astype(f32)
        sides = (sides + pltpu.roll(sides, 128 - used, 1)) + pltpu.roll(sides, 128 - 2 * used, 1)
        return sides[: PAIR // 2], sides[PAIR // 2 :]

    def attend(half, those):
        count = len(those) * n
        upper = tiles(count)
        keep_upper = upper.astype(f32).astype(bf16)
        keep_lower = (1.0 - upper.astype(f32)).astype(bf16)
        bias = jnp.concatenate(
            [
                bias_buf[pl.ds(b * n, n)]
                if half == 0
                else jnp.stack([bias_buf[f * n + b] for f in range(n)], axis=0)
                for b in those
            ],
            axis=0,
        )
        tops = [jnp.full((PAIR // 2, 128), FLOOR, f32) for _ in those]
        totals = [jnp.zeros((PAIR // 2, 128), f32) for _ in those]
        for p in range(2):
            pair = half * 2 + p
            x = jnp.concatenate([q_all[half, b, p].reshape(rows, 128) for b in those], axis=0)
            x = jnp.concatenate([x * keep_upper, x * keep_lower], axis=1)
            score = jnp.dot(x, kt_buf[pair], preferred_element_type=f32)
            score = score.reshape(count, 2, PAIR // 2, tokens) + bias[:, None]
            score = score.reshape(count * PAIR, tokens)
            top = jnp.maximum(jnp.max(score, axis=1, keepdims=True), FLOOR)
            prob = jnp.exp2((score - top) * (SCALE * LOG2_E))
            total = jnp.sum(prob, axis=1, keepdims=True)
            value = v_buf[:, :, pair * 256 : (pair + 1) * 256].reshape(tokens, 256)
            acc = jnp.dot(prob.astype(bf16), value, preferred_element_type=f32)
            acc = jnp.where(upper, acc[:, :128], acc[:, 128:])
            acc = acc.astype(bf16).reshape(count, PAIR, 128)
            top = top.reshape(count, 2, PAIR // 2, 1)
            total = total.reshape(count, 2, PAIR // 2, 1)
            for k, b in enumerate(those):
                for r in range(n):
                    part[half, b, r * HALF + p * PAIR : r * HALF + (p + 1) * PAIR, :] = acc[k * n + r]
                    for side in range(2):
                        here = lane == (side * 2 + p) * n + r
                        tops[k] = jnp.where(here, top[k * n + r, side], tops[k])
                        totals[k] = jnp.where(here, total[k * n + r, side], totals[k])
        for k, b in enumerate(those):
            part[half, b, n * HALF :, :] = pack(tops[k], totals[k])

    def send_part(half, i):
        return copy(PART, half, part.at[half, i], got.at[half, second[half]], at_second(half, i))

    def parted(half):
        every = got.at[half, pl.ds(0, n - 1)]
        return copy(PART, half, every, every, neighbours(half)[1])

    for half in range(2):
        forward(ASK_SECOND, half)

    def one_step(t, carry):
        @pl.when(t == 1)
        def _():
            for half in range(2):
                for leg in (2, 3):
                    arrive(ASK_SECOND, half, leg).wait_recv()

        @pl.when(t == 2)
        def _():
            for half in range(2):
                for leg in (4, 5):
                    arrive(ASK_SECOND, half, leg).wait_recv()

        away = lax.rem(t + 2, 3) + 1
        those = [
            [peer(second[half], n - away), peer(second[half], away)] for half in range(2)
        ]
        for half in range(2):
            for b in those[half]:
                attend(half, [b])
                send_part(half, b).start()
        return carry

    lax.fori_loop(0, 2, one_step, 0)
    for half in range(2):
        for leg in (6, 7):
            arrive(ASK_SECOND, half, leg).wait_recv()
        across = peer(second[half], n // 2)
        attend(half, [across])
        send_part(half, across).start()
    lax.fori_loop(2, 3, one_step, 0)

    for half in range(2):
        attend(half, [second[half]])
        got[half, second[half]] = part[half, second[half]]

    def send_merged(half, i):
        return copy(MERGED, half, merged.at[half, i], last.at[half, first[half]], at_first(half, i))

    def all_merged(half):
        every = last.at[half, pl.ds(0, n - 1)]
        return copy(MERGED, half, every, every, neighbours(half)[0])

    for half in range(2):
        parted(half).wait_recv()
        sides = [unpack(got[half, i, n * HALF :, :]) for i in range(n)]
        tops = jnp.stack([above for above, _ in sides], axis=0)
        totals = jnp.stack([below for _, below in sides], axis=0)
        top = jnp.max(tops, axis=0)
        weight = jnp.exp((tops - top[None]) * SCALE)
        total = jnp.sum(weight * totals, axis=0)
        some = jnp.maximum(total, 0.5)
        weight = weight / some[None]
        lse = jnp.where(total > 0.0, top * SCALE + jnp.log(some), EMPTY)
        tail = pack(lse, jnp.zeros_like(lse))
        for r in range(n):
            for p in range(2):
                scale = jnp.concatenate(
                    [
                        weight[:, :, (side * 2 + p) * n + r : (side * 2 + p) * n + r + 1]
                        for side in range(2)
                    ],
                    axis=1,
                )
                start = r * HALF + p * PAIR
                piece = got[half, :, start : start + PAIR, :].astype(f32)
                merged[half, r, p * PAIR : (p + 1) * PAIR, :] = jnp.sum(
                    piece * scale, axis=0
                ).astype(bf16)
            merged[half, r, HALF:, :] = tail
        for off in offsets(n):
            send_merged(half, peer(first[half], off)).start()
        last[half, first[half]] = merged[half, first[half]]

    def tell_first(half, i):
        return copy(TELL_FIRST, half, attn.at[half], told.at[half, first[half]], at_first(half, i))

    def all_told(half):
        every = told.at[half, pl.ds(0, n - 1)]
        return copy(TELL_FIRST, half, every, every, neighbours(half)[0])

    for load in loads[6:9]:
        load.wait()
    heads_in_row(nk_raw, rows64.at[pl.ds(0, KV_HEADS)])
    new_keys = rows64[:KV_HEADS, :]
    heads_in_row(nv_raw, rows64.at[pl.ds(KV_HEADS, KV_HEADS)])
    new_values = rows64[KV_HEADS : 2 * KV_HEADS, :]
    for half in range(2):
        kv_half = slice(half * 4, half * 4 + 4)
        query = q_ref[half].astype(f32).reshape(4, 8, 128)
        own = jnp.sum(query * new_keys[kv_half][:, None, :], axis=2, keepdims=True) * SCALE
        own = own.reshape(HALF, 1)
        own_value = jnp.broadcast_to(new_values[kv_half][:, None, :], (4, 8, 128)).reshape(HALF, 128)
        all_merged(half).wait_recv()
        lses = []
        for i in range(n):
            stat = unpack(last[half, i, HALF:, :])[0]
            lses.append(
                jnp.concatenate(
                    [
                        jnp.sum(
                            jnp.where(lane == (side * 2 + p) * n + first[half], stat, 0.0),
                            axis=1,
                            keepdims=True,
                        )
                        for p in range(2)
                        for side in range(2)
                    ],
                    axis=0,
                )
            )
        top = own
        for lse in lses:
            top = jnp.maximum(top, lse)
        weight = jnp.exp(own - top)
        total = weight
        acc = weight * own_value
        for i in range(n):
            weight = jnp.exp(lses[i] - top)
            total = total + weight
            acc = acc + weight * last[half, i, :HALF, :].astype(f32)
        attn[half] = (acc / total).astype(bf16)
        for off in offsets(n):
            tell_first(half, peer(first[half], off)).start()
        told[half, first[half]] = attn[half]

    for half in range(2):
        all_told(half).wait_recv()
        rows32[half] = told[half].astype(f32).reshape(n * HALF, 128)
        for h in range(HALF // 2):
            tile = [rows32[half, pl.ds(2 * h + s, n, stride=HALF), :] for s in range(2)]
            told_all[half, second[half], h] = jnp.concatenate(tile, axis=0).astype(bf16)
        begin(TELL_SECOND, half)

    for half in range(2):
        forward(TELL_SECOND, half)
    loads[9].wait()
    loads[10].wait()
    depth = HALF // 2 * HEAD_DIM
    mixed = []
    for half in range(2):
        for leg in range(2, len(LEGS)):
            arrive(TELL_SECOND, half, leg).wait_recv()
        x = jnp.concatenate(
            [told_all[half, :, h].reshape(n * 2 * n, 128) for h in range(HALF // 2)], axis=1
        )
        w = jnp.concatenate(
            [
                w_buf[side, half * (HALF // 2) : (half + 1) * (HALF // 2)].reshape(depth, 128)
                for side in range(2)
            ],
            axis=1,
        )
        acc = jnp.dot(x, w, preferred_element_type=f32).reshape(n, 2, n, 256)
        mixed.append(acc[:, 0, :, :128] + acc[:, 1, :, 128:])
    turn[...] = mixed[1].reshape(requests, 128)
    other = jnp.concatenate([turn[pl.ds(i, n, stride=n), :] for i in range(n)], axis=0)
    layer = res_buf[0].astype(f32) + (mixed[0].reshape(requests, 128) + other)
    line[...] = layer.astype(bf16)

    hand = pltpu.make_async_remote_copy(
        src_ref=line,
        dst_ref=landed,
        send_sem=pass_sem.at[0],
        recv_sem=pass_sem.at[1],
        device_id={"segment": following},
        device_id_type=MESH,
    )
    hand.start()

    for half in range(2):
        for stage in (asked, parted, all_merged, all_told):
            stage(half).wait_send()
        for ring in (ASK_SECOND, TELL_SECOND):
            for leg in range(len(LEGS)):
                leave(ring, half, leg).wait_send()
    hand.wait()
    out_ref[...] = landed[...]


def local(
    n_seg,
    n,
    queries,
    new_key,
    new_value,
    key_pool,
    value_pool,
    lengths,
    block_device,
    block_slot,
    residual,
    out_weight,
):
    f32, bf16 = jnp.float32, jnp.bfloat16
    slots = key_pool.shape[1]
    tokens = slots * BLK
    requests = n * n
    whole = pl.BlockSpec(memory_space=pltpu.VMEM)
    outside = pl.BlockSpec(memory_space=pltpu.HBM)
    blocks = block_device.shape[2]
    out = pl.pallas_call(
        functools.partial(kernel, n_seg, n),
        out_shape=jax.ShapeDtypeStruct((requests, 128), bf16),
        in_specs=[outside] * 10,
        out_specs=whole,
        scratch_shapes=[
            pltpu.VMEM((1, 1, HEADS * HEAD_DIM), bf16),
            pltpu.VMEM((1, 1, KV_HEADS * HEAD_DIM), bf16),
            pltpu.VMEM((1, 1, KV_HEADS * HEAD_DIM), bf16),
            pltpu.VMEM((1, requests), jnp.int32),
            pltpu.VMEM((1, blocks, requests), jnp.int32),
            pltpu.VMEM((1, blocks, requests), jnp.int32),
            pltpu.VMEM((1, requests, 128), bf16),
            pltpu.VMEM((HEADS, 128), f32),
            pltpu.VMEM((2, 2, PAIR, 128), bf16),
            pltpu.VMEM((slots, BLK, KV_HEADS * HEAD_DIM), bf16),
            pltpu.VMEM((slots, BLK, KV_HEADS * HEAD_DIM), bf16),
            pltpu.VMEM((2, HEADS // 2, HEAD_DIM, 128), bf16),
            pltpu.VMEM((4, 256, tokens), bf16),
            pltpu.VMEM((requests, PAIR // 2, tokens), f32),
            pltpu.VMEM((2, n, 2, n, PAIR, 128), bf16),
            pltpu.VMEM((2, n, n * HALF + PAIR, 128), bf16),
            pltpu.VMEM((2, n, n * HALF + PAIR, 128), bf16),
            pltpu.VMEM((2, n, HALF + PAIR, 128), bf16),
            pltpu.VMEM((2, n, HALF + PAIR, 128), bf16),
            pltpu.VMEM((2, HALF, 128), bf16),
            pltpu.VMEM((2, n, HALF, 128), bf16),
            pltpu.VMEM((2, n * HALF, 128), f32),
            pltpu.VMEM((2, n, HALF // 2, 2 * n, 128), bf16),
            pltpu.VMEM((requests, 128), f32),
            pltpu.VMEM((requests, 128), bf16),
            pltpu.VMEM((requests, 128), bf16),
            pltpu.SemaphoreType.DMA((4, 2)),
            pltpu.SemaphoreType.DMA((4, 2)),
            pltpu.SemaphoreType.DMA((2, 2 * len(LEGS))),
            pltpu.SemaphoreType.DMA((2, 2 * len(LEGS))),
            pltpu.SemaphoreType.DMA((11,)),
            pltpu.SemaphoreType.DMA((2,)),
        ],
        compiler_params=pltpu.CompilerParams(
            collective_id=0, has_side_effects=True, vmem_limit_bytes=60 * 1024 * 1024
        ),
        name="decode_layer",
    )(
        queries,
        new_key,
        new_value,
        lengths,
        jnp.swapaxes(block_device, 1, 2),
        jnp.swapaxes(block_slot, 1, 2),
        residual,
        key_pool[0],
        value_pool[0],
        out_weight[0].reshape(HEADS // 2, 2, HEAD_DIM, 128),
    )
    return out[None]


def solution(mesh):
    placed = (
        P("segment", "kv", None),
        P("segment", "kv", None),
        P("segment", "kv", None),
        P("segment", "kv", None, None),
        P("segment", "kv", None, None),
        P("segment", None),
        P("segment", None, None),
        P("segment", None, None),
        P("segment", None, "kv"),
        P("segment", None, "kv"),
    )
    n_seg = mesh.shape["segment"]
    n = next(i for i in range(1, 64) if i * i == mesh.shape["kv"])
    return jax.shard_map(
        functools.partial(local, n_seg, n),
        mesh=mesh,
        in_specs=placed,
        out_specs=P("segment", None, "kv"),
        check_vma=False,
    )
```
